32 devices in a mesh: seq: 4 (over x, core), fsdp: 8 (over z, y).
Axes of the slice: x: 2, y: 2, z: 4, core: 2. Of those that a mesh axis runs over, the one named last changes fastest.
Arguments:
- tokens: bfloat16 [8, 1024, 1024], P('fsdp', 'seq'), may hold values from -6 to 6
- attn_gain: bfloat16 [1024], P('fsdp'), may hold values from 0.5 to 1.5
- query_heads: bfloat16 [1024, 96], P('fsdp'), may hold values from -0.1875 to 0.1875
- query_shared: bfloat16 [1024, 384], P('fsdp'), may hold values from -0.375 to 0.375
- key_heads: bfloat16 [1024, 32], P('fsdp'), may hold values from -0.375 to 0.375
- key_shared: bfloat16 [1024, 128], P('fsdp'), may hold values from -0.375 to 0.375
- value_heads: bfloat16 [1024, 32], P('fsdp'), may hold values from -0.1875 to 0.1875
- value_shared: bfloat16 [1024, 128], P('fsdp'), may hold values from -0.1875 to 0.1875
- out_proj: bfloat16 [1024, 1024], P('fsdp'), may hold values from -1.5 to 1.5
- ffn_gain: bfloat16 [1024], P('fsdp'), may hold values from 0.5 to 1.5
- gate_proj: bfloat16 [1024, 2816], P('fsdp'), may hold values from -0.1875 to 0.1875
- up_proj: bfloat16 [1024, 2816], P('fsdp'), may hold values from -0.1875 to 0.1875
- down_proj: bfloat16 [2816, 1024], P('fsdp'), may hold values from -0.109375 to 0.109375
- cotangent: bfloat16 [8, 1024, 1024], P('fsdp', 'seq'), may hold values from -6 to 6
Outputs:
- output: bfloat16 [8, 1024, 1024], P('fsdp', 'seq')
- input_grad: bfloat16 [8, 1024, 1024], P('fsdp', 'seq')
- attn_gain_grad: float32 [1024], P('fsdp')
- query_heads_grad: float32 [1024, 96], P('fsdp')
- query_shared_grad: float32 [1024, 384], P('fsdp')
- key_heads_grad: float32 [1024, 32], P('fsdp')
- key_shared_grad: float32 [1024, 128], P('fsdp')
- value_heads_grad: float32 [1024, 32], P('fsdp')
- value_shared_grad: float32 [1024, 128], P('fsdp')
- out_proj_grad: float32 [1024, 1024], P('fsdp')
- ffn_gain_grad: float32 [1024], P('fsdp')
- gate_proj_grad: float32 [1024, 2816], P('fsdp')
- up_proj_grad: float32 [1024, 2816], P('fsdp')
- down_proj_grad: float32 [2816, 1024], P('fsdp')
The draws below stay inside these ranges and needn't reach their ends.
All inputs are finite; a program needn't handle non-finite values.
Results may differ from the reference program's by a relative error of at most 0.02.
The reference program's roundings to bfloat16 on the way count: a program that leaves them out, or rounds other values in their place, can miss the bound.
Values may be sent and summed in bfloat16 or wider, within the bound.
A program may use at most 192 MiB of HBM per device.

```python
import jax
import jax.numpy as jnp
from jax import lax

D = 1024
H = 16
DH = 64
RQ = 6
RK = 2
FF = 2816
SEQ_LEN = 1024
SEQS = 8


def block_scale(stream_key, dims, shards, smallest, largest):
    gain, own = 1.0, jax.random.fold_in(stream_key, 6)
    for dim, shards_of in shards:
        heights = jnp.exp(jax.random.uniform(jax.random.fold_in(own, dim), (shards_of,), jnp.float32, smallest / len(shards), largest / len(shards)))
        gain = gain * jnp.repeat(heights, dims[dim] // shards_of).reshape([-1 if axis == dim else 1 for axis in range(len(dims))])
    return gain


def gaussian(stream_key, dims, width, limit, split=(), kind=jnp.bfloat16):
    values = jax.random.normal(stream_key, dims, jnp.float32) * width
    if len(split) > 0:
        values = block_scale(stream_key, dims, split, -0.22, 0.18) * values
    return jnp.clip(values, min=-limit, max=limit).astype(kind)


def setup_inputs(seed: int = 0) -> dict:
    keys = jax.random.split(jax.random.key(seed), 15)
    return {
        "tokens": gaussian(keys[0], (SEQS, SEQ_LEN, D), 1.0, 6.0, ((0, 8), (1, 4))),
        "attn_gain": jnp.clip(1.0 + 0.1 * jax.random.normal(keys[1], (D,), jnp.float32), 0.5, 1.5).astype(jnp.bfloat16),
        "query_heads": gaussian(keys[2], (D, H * RQ), D ** -0.5, 0.1875, ((0, 8),)),
        "query_shared": gaussian(keys[3], (D, RQ * DH), (D // 4) ** -0.5, 0.375, ((0, 8),)),
        "key_heads": gaussian(keys[4], (D, H * RK), (D // 4) ** -0.5, 0.375, ((0, 8),)),
        "key_shared": gaussian(keys[5], (D, RK * DH), (D // 4) ** -0.5, 0.375, ((0, 8),)),
        "value_heads": gaussian(keys[6], (D, H * RK), D ** -0.5, 0.1875, ((0, 8),)),
        "value_shared": gaussian(keys[7], (D, RK * DH), D ** -0.5, 0.1875, ((0, 8),)),
        "out_proj": gaussian(keys[8], (D, H * DH), (max(D // 64, 1)) ** -0.5, 1.5, ((0, 8),)),
        "ffn_gain": jnp.clip(1.0 + 0.1 * jax.random.normal(keys[9], (D,), jnp.float32), 0.5, 1.5).astype(jnp.bfloat16),
        "gate_proj": gaussian(keys[10], (D, FF), D ** -0.5, 0.1875, ((0, 8),)),
        "up_proj": gaussian(keys[11], (D, FF), D ** -0.5, 0.1875, ((0, 8),)),
        "down_proj": gaussian(keys[12], (FF, D), FF ** -0.5, 0.109375, ((0, 8),)),
        "cotangent": gaussian(keys[13], (SEQS, SEQ_LEN, D), 1.0, 6.0, ((0, 8), (1, 4))),
    }


norm_eps = 1e-06
rope_base = 10000.0
masked_score = -1e+30
highest = lax.Precision.HIGHEST

@jax.custom_vjp
def low(v):
    return lax.optimization_barrier(v.astype(jnp.bfloat16)).astype(jnp.float32)

@jax.custom_vjp
def low_back(v):
    return v

def low_keep(v):
    return (low(v), None)

def low_pass(kept, grad):
    return (grad,)

def back_keep(v):
    return (v, None)

def back_low(kept, grad):
    return (low(grad),)
low.defvjp(low_keep, low_pass)
low_back.defvjp(back_keep, back_low)

def matmul_hi(left_mat, right_mat):
    return jnp.dot(left_mat, right_mat, precision=highest)

def rope_tables(length):
    positions = jnp.arange(length, dtype=jnp.float32)
    frequency = rope_base ** (-2.0 * jnp.arange(DH // 2, dtype=jnp.float32) / DH)
    angles = positions[:, None] * frequency[None, :]
    return (jnp.cos(angles), jnp.sin(angles))

def rotate(factor, cosine_table, sine_table):
    half_size = factor.shape[-1] // 2
    first_half = factor[..., :half_size]
    second_half = factor[..., half_size:]
    cosine_row = cosine_table[:, None, :]
    sine_row = sine_table[:, None, :]
    return jnp.concatenate([first_half * cosine_row - second_half * sine_row, first_half * sine_row + second_half * cosine_row], axis=-1)

def rms_norm(values, gain_vec):
    inv_rms = lax.rsqrt(lax.optimization_barrier(jnp.mean(values * values, axis=-1, keepdims=True)) + norm_eps)
    return values * inv_rms * gain_vec

def layer(inputs, attn_gain, query_heads, query_shared, key_heads, key_shared, value_heads, value_shared, out_proj, ffn_gain, gate_proj, up_proj, down_proj):
    length = inputs.shape[0]
    cosine_table, sine_table = rope_tables(length)
    normed = low(rms_norm(inputs, attn_gain))
    heads_q = low(low_back(matmul_hi(normed, query_heads))).reshape(length, H, RQ)
    heads_k = low(low_back(matmul_hi(normed, key_heads))).reshape(length, H, RK)
    heads_v = low(low_back(matmul_hi(normed, value_heads))).reshape(length, H, RK)
    shared_q = low(rotate(low_back(matmul_hi(normed, query_shared)).reshape(length, RQ, DH), cosine_table, sine_table))
    shared_k = low(rotate(low_back(matmul_hi(normed, key_shared)).reshape(length, RK, DH), cosine_table, sine_table))
    shared_v = low(low_back(matmul_hi(normed, value_shared)).reshape(length, RK, DH))
    queries = low(jnp.einsum('thr,trd->htd', heads_q, shared_q, precision=highest) / RQ)
    keys_all = low(jnp.einsum('thr,trd->htd', heads_k, shared_k, precision=highest) / RK)
    values_all = low(jnp.einsum('thr,trd->htd', heads_v, shared_v, precision=highest) / RK)
    scaling = DH ** (-0.5)
    block_rows = min(512, length)
    blocks = length // block_rows

    def attend(block_id):
        first_row = block_id * block_rows
        query_block = lax.dynamic_slice_in_dim(queries, first_row, block_rows, 1)
        scores = low_back(jnp.einsum('hqd,hkd->hqk', query_block, keys_all, precision=highest) * scaling)
        row_ids = first_row + jnp.arange(block_rows, dtype=jnp.int32)
        col_ids = jnp.arange(length, dtype=jnp.int32)
        scores = jnp.where((col_ids[None, :] <= row_ids[:, None])[None], scores, masked_score)
        row_max = lax.optimization_barrier(jnp.max(scores, axis=-1, keepdims=True))
        exponent = jnp.exp(scores - row_max)
        softmax_rows = exponent / lax.optimization_barrier(jnp.sum(exponent, axis=-1, keepdims=True))
        return jnp.einsum('hqk,hkd->qhd', low(softmax_rows), values_all, precision=highest)
    attended = lax.map(jax.checkpoint(attend), jnp.arange(blocks, dtype=jnp.int32)).reshape(length, H * DH)
    attended = low(low_back(attended))
    middle = inputs + low_back(jnp.dot(attended, out_proj.T, precision=highest))
    normed_two = low(rms_norm(middle, ffn_gain))
    gate_pre = low_back(matmul_hi(normed_two, gate_proj))
    up_pre = low_back(matmul_hi(normed_two, up_proj))
    mixed_act = low(jax.nn.silu(gate_pre) * up_pre)
    return middle + low_back(matmul_hi(mixed_act, down_proj))

def reference(tokens, attn_gain, query_heads, query_shared, key_heads, key_shared, value_heads, value_shared, out_proj, ffn_gain, gate_proj, up_proj, down_proj, cotangent):
    params = tuple((weight.astype(jnp.float32) for weight in (attn_gain, query_heads, query_shared, key_heads, key_shared, value_heads, value_shared, out_proj, ffn_gain, gate_proj, up_proj, down_proj)))

    def step(totals, pair):
        sequence, grad_seq = pair
        result, pullback = jax.vjp(layer, sequence.astype(jnp.float32), *params)
        grads = pullback(grad_seq.astype(jnp.float32))
        totals = tuple((before + extra for before, extra in zip(totals, grads[1:])))
        return (totals, (result.astype(jnp.bfloat16), grads[0].astype(jnp.bfloat16)))
    zero_grads = tuple((jnp.zeros(weight.shape, jnp.float32) for weight in params))
    totals, outputs = lax.scan(step, zero_grads, (tokens, cotangent))
    return (outputs[0], outputs[1], totals[0], totals[1], totals[2], totals[3], totals[4], totals[5], totals[6], totals[7], totals[8], totals[9], totals[10], totals[11])
```

```python
import functools

import jax
import jax.numpy as jnp
import numpy as np
from jax import lax
from jax.experimental import pallas as pl
from jax.experimental.pallas import tpu as pltpu
from jax.sharding import PartitionSpec as P

H = 16
DH = 64
RQ = 6
RK = 2
NS = 4
LH = H // NS
EPS = 1e-06
BASE = 10000.0
MASKED = -1e30
NSH = 320
NH = 40
WF = 384
F32 = jnp.float32
BF16 = jnp.bfloat16
VMEM_LIMIT = 56 << 20


def dot_nn(a, b):
    return lax.dot_general(a, b, (((1,), (0,)), ((), ())), preferred_element_type=F32)


def dot_nt(a, b):
    return lax.dot_general(a, b, (((1,), (1,)), ((), ())), preferred_element_type=F32)


class Net:
    def __init__(self, n, send_sems, recv_sems):
        self.n = n
        self.ni = 2 if n <= 8 else 4
        self.no = n // self.ni
        self.s = lax.axis_index("seq")
        self.f = lax.axis_index("fsdp")
        self.o = self.f // self.ni
        self.i = self.f % self.ni
        self.core = self.s % 2
        self.sib = self.s + 1 - 2 * self.core
        self.across = (self.s + 2) % 4
        self.diag = (self.sib + 2) % 4
        self.send_sems = send_sems
        self.recv_sems = recv_sems
        self.sends = 0
        self.recvs = 0
        self.open = []

    def at(self, o, i):
        return o * self.ni + i

    def outer(self, k):
        return (self.o + k) % self.no

    def inner(self, m):
        return (self.i + m) % self.ni

    def take(self, count):
        first = self.recvs
        self.recvs += count
        return first

    def barrier(self):
        sem = pltpu.get_barrier_semaphore()
        peers = [{"seq": self.sib}, {"seq": self.across}]
        peers += [{"fsdp": self.at(self.outer(k), self.i)} for k in range(1, self.no)]
        peers += [{"fsdp": self.at(self.o, self.inner(m))} for m in range(1, self.ni)]
        for peer in peers:
            pl.semaphore_signal(sem, inc=1, device_id=peer, device_id_type=pl.DeviceIdType.MESH)
        pl.semaphore_wait(sem, len(peers))

    def send(self, src, dst, slot, device, when=None):
        copy = pltpu.make_async_remote_copy(
            src_ref=src,
            dst_ref=dst,
            send_sem=self.send_sems.at[self.sends],
            recv_sem=self.recv_sems.at[slot],
            device_id=device,
            device_id_type=pl.DeviceIdType.MESH,
        )
        self.sends += 1
        if when is None:
            copy.start()
        else:
            pl.when(when)(copy.start)
        self.open.append((copy, when))

    def local(self, src, dst):
        copy = pltpu.make_async_copy(src, dst, self.send_sems.at[self.sends])
        self.sends += 1
        copy.start()
        return copy

    def arrived(self, dst, slot):
        pltpu.make_async_remote_copy(
            src_ref=dst,
            dst_ref=dst,
            send_sem=self.send_sems.at[0],
            recv_sem=self.recv_sems.at[slot],
            device_id={"seq": self.sib},
            device_id_type=pl.DeviceIdType.MESH,
        ).wait_recv()

    def drain(self):
        for copy, when in self.open:
            if when is None:
                copy.wait_send()
            else:
                pl.when(when)(copy.wait_send)
        self.open = []


class Gather:
    def __init__(self, net, src, dst):
        self.net, self.src, self.dst = net, src, dst
        self.slot = net.take(net.n)

    def start(self):
        net = self.net
        own = self.dst.at[net.f]
        for m in range(1, net.ni):
            net.send(self.src, own, self.slot + net.f, {"fsdp": net.at(net.o, net.inner(m))})
        for k in range(1, net.no):
            net.send(self.src, own, self.slot + net.f, {"fsdp": net.at(net.outer(k), net.i)})
        self.own = net.local(self.src, own)

    def block(self, index):
        self.net.arrived(self.dst.at[index], self.slot + index)

    def forward(self, k, then=None):
        net = self.net
        index = net.at((net.o - k + net.no) % net.no, net.i)
        self.block(index)
        for m in range(1, net.ni):
            net.send(self.dst.at[index], self.dst.at[index], self.slot + index, {"fsdp": net.at(net.o, net.inner(m))})
        if then is not None:
            then(index)

    def finish(self, then=None):
        net = self.net
        for k in range(net.no):
            for m in range(1, net.ni):
                index = net.at((net.o - k + net.no) % net.no, net.inner(m))
                self.block(index)
                if then is not None:
                    then(index)
        self.own.wait()


class Spread:
    def __init__(self, net, src, dst, group):
        self.net, self.src, self.dst = net, src, dst
        self.wide = net.no // NS
        self.first = group * self.wide
        self.slot = net.take(net.n // NS)
        self.mine = jnp.logical_and(net.o >= self.first, net.o < self.first + self.wide)

    def place(self, o, i):
        return (o - self.first) * self.net.ni + i

    def start(self):
        net = self.net
        index = jnp.where(self.mine, self.place(net.o, net.i), 0)
        own = self.dst.at[index]
        for m in range(1, net.ni):
            net.send(self.src, own, self.slot + index, {"fsdp": net.at(net.o, net.inner(m))}, self.mine)
        for k in range(1, net.no):
            net.send(self.src, own, self.slot + index, {"fsdp": net.at(net.outer(k), net.i)}, self.mine)
        self.own = pltpu.make_async_copy(self.src, own, net.send_sems.at[net.sends])
        net.sends += 1
        pl.when(self.mine)(self.own.start)

    def forward(self):
        net = self.net
        for g in range(self.wide):
            other = net.o != self.first + g
            index = g * net.ni + net.i

            @pl.when(other)
            def _():
                net.arrived(self.dst.at[index], self.slot + index)

            for m in range(1, net.ni):
                net.send(
                    self.dst.at[index],
                    self.dst.at[index],
                    self.slot + index,
                    {"fsdp": net.at(net.o, net.inner(m))},
                    other,
                )

    def finish(self):
        net = self.net
        for g in range(self.wide):
            for m in range(1, net.ni):
                index = g * net.ni + net.inner(m)
                net.arrived(self.dst.at[index], self.slot + index)
        pl.when(self.mine)(self.own.wait)


class Share:
    def __init__(self, net, dst):
        self.net, self.dst = net, dst
        self.slot = net.take(NS)

    def start(self, src):
        net = self.net
        own = self.dst(net.s)
        net.send(src, own, self.slot + net.s, {"seq": net.across})
        net.send(src, own, self.slot + net.s, {"seq": net.sib})

    def forward(self):
        net = self.net
        far = self.dst(net.across)
        net.arrived(far, self.slot + net.across)
        net.send(far, far, self.slot + net.across, {"seq": net.sib})

    def near(self):
        net = self.net
        net.arrived(self.dst(net.sib), self.slot + net.sib)

    def last(self):
        net = self.net
        net.arrived(self.dst(net.diag), self.slot + net.diag)


def first_kernel(
    n,
    tok_in,
    wf_in,
    wo_in,
    wg_in,
    wu_in,
    wd_in,
    cot_in,
    cos_ref,
    sin_ref,
    tok,
    cot,
    wo,
    wg,
    wu,
    wd,
    att,
    normed,
    wft,
    gains,
    shared,
    heads,
    qt,
    kt,
    vt,
    kn,
    vn,
    lse,
    att_t,
    wf,
    send_sems,
    recv_sems,
):
    net = Net(n, send_sems, recv_sems)
    tokens = tok_in.shape[0]
    length = tokens * NS
    rows = wf_in.shape[0]
    net.barrier()

    g_wf = Gather(net, wf_in, wf.at[net.core])
    s_tok = Share(net, lambda r: tok.at[r])
    slot_sib = net.take(n)

    def to_sibling(index):
        here = wf.at[net.core, index]
        net.send(here, here, slot_sib + index, {"seq": net.sib})

    g_wf.start()
    net.send(wf_in, wf.at[net.core, net.f], slot_sib + net.f, {"seq": net.sib})
    s_tok.start(tok_in)
    own_tok = net.local(tok_in, tok.at[net.s])
    for k in range(1, net.no):
        g_wf.forward(k, to_sibling)
    g_wf.finish(to_sibling)

    g_wo = Gather(net, wo_in, wo.at[net.s])
    g_wg = Gather(net, wg_in, wg)
    g_wu = Gather(net, wu_in, wu)
    group = (NS - net.s) % NS
    g_wd = Spread(net, wd_in, wd, group)
    g_wo.start()
    g_wg.start()
    g_wu.start()
    g_wd.start()
    s_tok.forward()
    s_cot = Share(net, lambda r: cot.at[r])
    s_cot.start(cot_in)
    own_cot = net.local(cot_in, cot.at[net.s])
    for index in range(n):
        net.arrived(wf.at[1 - net.core, index], slot_sib + index)

    for half in range(2):
        whole = wf[half].reshape(n * rows, WF).astype(F32).T
        wft[half] = whole.astype(BF16)
        if half == 0:
            gains[...] = whole[NSH + NH : NSH + NH + 8, :]
    own_tok.wait()
    s_tok.near()
    s_tok.last()

    s_att = [Share(net, lambda r, j=j: att.at[r, pl.ds(tokens * j, tokens)]) for j in range(NS)]
    for j in range(NS):
        here = slice(tokens * j, tokens * (j + 1))
        values = tok[j].astype(F32)
        inv = lax.rsqrt(jnp.mean(values * values, axis=-1, keepdims=True) + EPS)
        block = (values * inv * gains[0:1, :]).astype(BF16)
        normed[here, :] = block
        parts = [dot_nt(wft[half], block) for half in range(2)]
        own = dot_nt(wft[net.core, NSH:, :], block)
        cosine, sine = cos_ref[:, here], sin_ref[:, here]

        def turned(piece):
            first, second = piece[: DH // 2], piece[DH // 2 :]
            return jnp.concatenate([first * cosine - second * sine, first * sine + second * cosine], axis=0)

        def piece(half, index):
            return parts[half][DH * index : DH * (index + 1)]

        def rounded(v):
            return v.astype(BF16).astype(F32)

        sq = [rounded(turned(piece(0, r))) for r in range(5)] + [rounded(turned(piece(1, 0)))]
        sk = [rounded(turned(piece(1, 1 + r))) for r in range(RK)]
        sv = [rounded(piece(1, 3 + r)) for r in range(RK)]
        for index, part in enumerate(sq + sk + sv):
            shared[index // 5, DH * (index % 5) : DH * (index % 5 + 1), here] = part.astype(BF16)
        own = rounded(own[:NH])
        heads[:, here] = own
        for h in range(LH):
            q = sum(own[h * RQ + r : h * RQ + r + 1] * sq[r] for r in range(RQ)) * (1.0 / RQ)
            first = LH * RQ
            k = sum(own[first + h * RK + r : first + h * RK + r + 1] * sk[r] for r in range(RK)) * (1.0 / RK)
            first = LH * (RQ + RK)
            v = sum(own[first + h * RK + r : first + h * RK + r + 1] * sv[r] for r in range(RK)) * (1.0 / RK)
            qt[h, :, here] = (q.astype(BF16).astype(F32) * DH**-0.5).astype(BF16)
            kt[h, :, here] = k.astype(BF16)
            vt[h, :, here] = v.astype(BF16)
            kn[h, here, :] = rounded(k).T.astype(BF16)
            vn[h, here, :] = rounded(v).T.astype(BF16)

        upto = tokens * j

        def one_head(h, _):
            q = qt[h, :, here]
            keep = lax.broadcasted_iota(jnp.int32, (tokens, tokens), 0) <= lax.broadcasted_iota(
                jnp.int32, (tokens, tokens), 1
            )
            diagonal = jnp.where(keep, dot_nn(kn[h, here, :], q), MASKED)
            top = jnp.max(diagonal, axis=0, keepdims=True)
            if j > 0:
                below = dot_nn(kn[h, 0:upto, :], q)
                top = jnp.maximum(top, jnp.max(below, axis=0, keepdims=True))
            diagonal = jnp.exp(diagonal - top)
            total = jnp.sum(diagonal, axis=0, keepdims=True)
            if j > 0:
                below = jnp.exp(below - top)
                total = total + jnp.sum(below, axis=0, keepdims=True)
            inverse = 1.0 / total
            result = dot_nn(vt[h, :, here], (diagonal * inverse).astype(BF16))
            if j > 0:
                result = result + dot_nn(vt[h, :, 0:upto], (below * inverse).astype(BF16))
            lse[h, :, here] = top + jnp.log(total)
            att_t[h, :, here] = result.astype(BF16)
            return 0

        lax.fori_loop(0, LH, one_head, 0)
        turn = att_t[:, :, here].reshape(LH * DH, tokens).astype(F32).T
        att[net.s, here, :] = turn.astype(BF16)
        s_att[j].start(att.at[net.s, pl.ds(tokens * j, tokens)])
        if j == 0:
            for k in range(1, net.no):
                g_wo.forward(k)
        if j == 1:
            g_wo.finish()
            s_wo = Share(net, lambda r: wo.at[r])
            s_wo.start(wo.at[net.s])
            for k in range(1, net.no):
                g_wg.forward(k)
        if j == 2:
            s_cot.forward()
            for k in range(1, net.no):
                g_wu.forward(k)
    for share in s_att:
        share.forward()
    s_wo.forward()
    g_wd.forward()
    for share in s_att:
        share.near()
        share.last()
    for share in (s_cot, s_wo):
        share.near()
        share.last()
    own_cot.wait()
    g_wg.finish()
    g_wu.finish()
    g_wd.finish()
    net.drain()


def sems(n):
    return [pltpu.SemaphoreType.DMA((40 * n,)), pltpu.SemaphoreType.DMA((8 * n + 40,))]


def any_space(count):
    return [pl.BlockSpec(memory_space=pl.ANY)] * count


def vmem_space(count):
    return [pl.BlockSpec(memory_space=pltpu.VMEM)] * count


def run_first(n, tok, wf, wo, wg, wu, wd, cot, cosine, sine):
    tokens, width = tok.shape
    rows, cols = wg.shape
    length = tokens * NS
    shapes = [
        ((NS, tokens, width), BF16),
        ((NS, tokens, width), BF16),
        ((NS, n, rows, LH * DH), BF16),
        ((n, rows, cols), BF16),
        ((n, rows, cols), BF16),
        ((n // NS,) + wd.shape, BF16),
        ((NS, length, LH * DH), BF16),
        ((length, width), BF16),
        ((2, WF, width), BF16),
        ((8, width), F32),
        ((2, NSH, length), BF16),
        ((NH, length), F32),
        ((LH, DH, length), BF16),
        ((LH, DH, length), BF16),
        ((LH, DH, length), BF16),
        ((LH, length, DH), BF16),
        ((LH, length, DH), BF16),
        ((LH, 1, length), F32),
        ((LH, DH, length), BF16),
    ]
    return pl.pallas_call(
        functools.partial(first_kernel, n),
        out_shape=[jax.ShapeDtypeStruct(*shape) for shape in shapes],
        in_specs=any_space(7) + vmem_space(2),
        out_specs=vmem_space(len(shapes)),
        scratch_shapes=[pltpu.VMEM((2, n, rows, WF), BF16)] + sems(n),
        compiler_params=pltpu.CompilerParams(collective_id=1, has_side_effects=True, vmem_limit_bytes=VMEM_LIMIT),
    )(tok, wf, wo, wg, wu, wd, cot, cosine, sine)


def tables(length):
    positions = np.arange(length, dtype=np.float32)
    frequency = (BASE ** (-2.0 * np.arange(DH // 2, dtype=np.float32) / DH)).astype(np.float32)
    angles = frequency[:, None] * positions[None, :]
    return np.cos(angles).astype(np.float32), np.sin(angles).astype(np.float32)


def prepare(attn_gain, qh, qs, kh, ks, vh, vs, out_proj, ffn_gain, gate, up):
    s = lax.axis_index("seq")
    rows = qs.shape[0]
    cols = gate.shape[1] // NS
    first = ((NS - s) % NS) * cols
    wg = lax.dynamic_slice(gate, (0, first), (rows, cols))
    wu = lax.dynamic_slice(up, (0, first), (rows, cols))
    wo = lax.dynamic_slice(out_proj, (0, s * LH * DH), (rows, LH * DH))
    half = jnp.where(s % 2 == 0, qs[:, :NSH], jnp.concatenate([qs[:, NSH:], ks, vs], axis=1))
    own = [
        lax.dynamic_slice(w, (0, s * LH * r), (rows, LH * r)) for w, r in ((qh, RQ), (kh, RK), (vh, RK))
    ]
    rest = jnp.zeros((rows, WF - NSH - NH - 2), BF16)
    wf = jnp.concatenate([half, *own, attn_gain[:, None], ffn_gain[:, None], rest], axis=1)
    return wf, wo, wg, wu


class Fold:
    def __init__(self, net, out, into):
        self.net, self.out, self.into = net, out, into
        self.slot = net.take(3)

    def to_diag(self, value):
        net = self.net
        self.out[0] = value.astype(BF16)
        net.send(self.out.at[0], self.into.at[0], self.slot, {"seq": net.sib})

    def to_across(self, value):
        net = self.net
        net.arrived(self.into.at[0], self.slot)
        self.out[1] = (value + self.into[0].astype(F32)).astype(BF16)
        net.send(self.out.at[1], self.into.at[2], self.slot + 2, {"seq": net.across})

    def to_sibling(self, value):
        net = self.net
        self.out[2] = value.astype(BF16)
        net.send(self.out.at[2], self.into.at[1], self.slot + 1, {"seq": net.sib})

    def total(self, value):
        net = self.net
        net.arrived(self.into.at[1], self.slot + 1)
        net.arrived(self.into.at[2], self.slot + 2)
        return value + self.into[1].astype(F32) + self.into[2].astype(F32)


def second_kernel(
    n,
    tok,
    cot,
    wo,
    wg_in,
    wu_in,
    wd,
    att,
    gains,
    result,
    branch,
    grad_mid,
    gain_grad,
    wg_grad,
    wu_grad,
    wd_grad,
    n2_t,
    gg_all,
    gu_all,
    mixed_t,
    mid_own,
    inv_own,
    dn_own,
    out_own,
    dn_out,
    dn_in,
    res_out,
    res_in,
    across_keep,
    send_sems,
    recv_sems,
):
    net = Net(n, send_sems, recv_sems)
    tokens, width = tok.shape[1:]
    cols = wg_in.shape[2]
    net.barrier()
    gain = gains[1:2, :]
    f_dn = Fold(net, dn_out, dn_in)
    f_res = Fold(net, res_out, res_in)
    order = (net.diag, net.across, net.sib, net.s)

    for step, b in enumerate(order):
        here = slice(tokens * step, tokens * (step + 1))
        rows = pl.ds(pl.multiple_of(b * tokens, tokens), tokens)
        middle = tok[b].astype(F32)
        for r in range(NS):
            middle = middle + dot_nt(att[r, rows, :], wo[r].reshape(width, LH * DH))
        inv = lax.rsqrt(jnp.mean(middle * middle, axis=-1, keepdims=True) + EPS)
        normal = middle * inv
        normed = (normal * gain).astype(BF16)
        n2_t[:, here] = (normal * gain).astype(BF16).astype(F32).T.astype(BF16)
        if step == 3:
            mid_own[...] = middle
            inv_own[...] = jnp.broadcast_to(inv, inv_own.shape)
        wg = wg_in[...].reshape(width, cols)
        wu = wu_in[...].reshape(width, cols)
        gate = dot_nn(normed, wg)
        up = dot_nn(normed, wu)
        sg = jax.nn.sigmoid(gate)
        act = gate * sg
        mixed = (act * up).astype(BF16)
        mixed_t[:, here] = mixed.astype(F32).T.astype(BF16)
        grad_mixed = dot_nt(cot[b], wd[...])
        gg = (grad_mixed * up * sg * (1.0 + gate * (1.0 - sg))).astype(BF16)
        gu = (grad_mixed * act).astype(BF16)
        gg_all[here, :] = gg
        gu_all[here, :] = gu
        dn = dot_nt(gg, wg) + dot_nt(gu, wu)
        if step == 0:
            f_dn.to_diag(dn)
        elif step == 1:
            f_dn.to_across(dn)
        elif step == 2:
            f_dn.to_sibling(dn)
        else:
            dn_own[...] = dn
        part = dot_nn(mixed, wd[...])
        if step == 0:
            f_res.to_diag(part)
        elif step == 1:
            across_keep[...] = part
        elif step == 2:
            f_res.to_sibling(part)
        else:
            out_own[...] = part

    wd_rows = wd_grad.shape[1]
    down = sum(dot_nn(mixed_t[:, tokens * k : tokens * (k + 1)], cot[b]) for k, b in enumerate(order))
    for index in range(wd_grad.shape[0]):
        wd_grad[index] = down[wd_rows * index : wd_rows * (index + 1)].astype(BF16)

    total = f_dn.total(dn_own[...])
    inv = inv_own[:, 0:1]
    normal = mid_own[...] * inv
    scaled = total * gain
    mid_grad = cot[net.s].astype(F32) + inv * (scaled - normal * jnp.mean(scaled * normal, axis=-1, keepdims=True))
    grad_mid[...] = mid_grad
    gain_grad[...] = jnp.broadcast_to(jnp.sum(total * normal, axis=0, keepdims=True), gain_grad.shape)
    branch[net.s] = mid_grad.astype(BF16)
    s_branch = Share(net, lambda r: branch.at[r])
    s_branch.start(branch.at[net.s])
    f_res.to_across(across_keep[...])

    rows = wg_grad.shape[1]
    wg_grad[...] = dot_nn(n2_t[...], gg_all[...]).astype(BF16).reshape(wg_grad.shape)
    wu_grad[...] = dot_nn(n2_t[...], gu_all[...]).astype(BF16).reshape(wu_grad.shape)

    s_branch.forward()
    result[...] = (mid_own[...] + f_res.total(out_own[...])).astype(BF16)
    s_branch.near()
    s_branch.last()
    net.drain()


def run_second(n, tok, cot, wo, wg, wu, wd, att, gains):
    tokens, width = tok.shape[1:]
    length = tokens * NS
    rows, cols = wg.shape[1:]
    quarter = wd.shape[0]
    shapes = [
        ((tokens, width), BF16),
        ((NS, tokens, width), BF16),
        ((tokens, width), F32),
        ((8, width), F32),
        ((n, rows, cols), BF16),
        ((n, rows, cols), BF16),
        ((n // NS, quarter * NS // n, width), BF16),
    ]
    scratch = [
        ((width, length), BF16),
        ((length, cols), BF16),
        ((length, cols), BF16),
        ((cols, length), BF16),
        ((tokens, width), F32),
        ((tokens, 128), F32),
        ((tokens, width), F32),
        ((tokens, width), F32),
        ((3, tokens, width), BF16),
        ((3, tokens, width), BF16),
        ((3, tokens, width), BF16),
        ((3, tokens, width), BF16),
        ((tokens, width), F32),
    ]
    return pl.pallas_call(
        functools.partial(second_kernel, n),
        out_shape=[jax.ShapeDtypeStruct(*shape) for shape in shapes],
        in_specs=vmem_space(8),
        out_specs=vmem_space(len(shapes)),
        scratch_shapes=[pltpu.VMEM(*s) for s in scratch] + sems(n),
        compiler_params=pltpu.CompilerParams(collective_id=2, has_side_effects=True, vmem_limit_bytes=VMEM_LIMIT),
    )(tok, cot, wo, wg, wu, wd, att, gains)


class Reduce:
    def __init__(self, net, src, near, stage, far):
        self.net, self.src, self.near, self.stage, self.far = net, src, near, stage, far
        self.slot_near = net.take((net.ni - 1) * net.no)
        self.slot_far = net.take(net.no - 1)

    def start(self):
        net = self.net
        for k in [*range(1, net.no), 0]:
            o = net.outer(k)
            for m in range(1, net.ni):
                net.send(
                    self.src.at[net.at(o, net.inner(m))],
                    self.near.at[m - 1, o],
                    self.slot_near + (m - 1) * net.no + o,
                    {"fsdp": net.at(net.o, net.inner(m))},
                )

    def column(self, o):
        net = self.net
        value = self.src[net.at(o, net.i)].astype(F32)
        for m in range(1, net.ni):
            net.arrived(self.near.at[m - 1, o], self.slot_near + (m - 1) * net.no + o)
            value = value + self.near[m - 1, o].astype(F32)
        return value

    def forward(self, k):
        net = self.net
        o = net.outer(k)
        self.stage[k - 1] = self.column(o).astype(BF16)
        net.send(self.stage.at[k - 1], self.far.at[k - 1], self.slot_far + k - 1, {"fsdp": net.at(o, net.i)})

    def finish(self):
        net = self.net
        value = self.column(net.o)
        for k in range(1, net.no):
            net.arrived(self.far.at[k - 1], self.slot_far + k - 1)
            value = value + self.far[k - 1].astype(F32)
        return value


class Collect:
    def __init__(self, net, src, near, stage, far, group, into):
        self.net, self.src, self.near, self.stage, self.far, self.into = net, src, near, stage, far, into
        self.wide = net.no // NS
        self.first = group * self.wide
        self.mine = jnp.logical_and(net.o >= self.first, net.o < self.first + self.wide)
        self.slot_near = net.take((net.ni - 1) * self.wide)
        self.slot_far = net.take(net.no - 1)
        self.slot_into = net.take(1)
        self.owner = (NS - net.o // self.wide) % NS

    def start(self):
        net = self.net
        for g in range(self.wide):
            for m in range(1, net.ni):
                net.send(
                    self.src.at[g * net.ni + net.inner(m)],
                    self.near.at[m - 1, g],
                    self.slot_near + (m - 1) * self.wide + g,
                    {"fsdp": net.at(net.o, net.inner(m))},
                )

    def forward(self):
        net = self.net
        for g in range(self.wide):
            value = self.src[g * net.ni + net.i].astype(F32)
            for m in range(1, net.ni):
                net.arrived(self.near.at[m - 1, g], self.slot_near + (m - 1) * self.wide + g)
                value = value + self.near[m - 1, g].astype(F32)
            self.stage[g] = value.astype(BF16)
            o = self.first + g
            step = (o - net.o + net.no) % net.no
            away = step > 0
            place = jnp.where(away, step - 1, 0)
            net.send(self.stage.at[g], self.far.at[place], self.slot_far + place, {"fsdp": net.at(o, net.i)}, away)

    def finish(self):
        net = self.net

        @pl.when(self.mine)
        def _():
            value = self.stage[net.o - self.first].astype(F32)
            for k in range(1, net.no):
                net.arrived(self.far.at[k - 1], self.slot_far + k - 1)
                value = value + self.far[k - 1].astype(F32)
            self.into[...] = value.astype(BF16)

        net.send(self.into, self.into, self.slot_into, {"seq": net.across}, self.mine)
        net.send(self.into, self.into, self.slot_into, {"seq": net.sib}, self.mine)

    def forward_into(self):
        net = self.net
        other = net.s != self.owner
        pl.when(other)(lambda: net.arrived(self.into, self.slot_into))
        net.send(self.into, self.into, self.slot_into, {"seq": net.sib}, net.across == self.owner)


def third_kernel(
    n,
    tok,
    branch,
    grad_mid,
    gain_grad,
    wg_grad,
    wu_grad,
    wd_grad,
    wo,
    normed,
    wft,
    gains,
    shared,
    heads,
    qt,
    kt,
    kn,
    vn,
    lse,
    att_t,
    cos_ref,
    sin_ref,
    input_grad,
    wg_out,
    wu_out,
    wd_out,
    wo_out,
    wf_out,
    grad_att,
    grad_q,
    grad_k,
    grad_v,
    factors,
    wo_grad,
    wf_grad,
    wf_near,
    gate_near,
    gate_stage,
    gate_far,
    up_near,
    up_stage,
    up_far,
    down_near,
    down_stage,
    down_far,
    o_near,
    o_stage,
    o_far,
    f_near,
    f_stage,
    f_far,
    gn_out,
    gn_in,
    gn_keep,
    send_sems,
    recv_sems,
):
    net = Net(n, send_sems, recv_sems)
    tokens, width = tok.shape[1:]
    length = NS * tokens
    rows = wg_grad.shape[1]
    net.barrier()

    group = (NS - net.s) % NS
    r_up = Reduce(net, wu_grad, up_near, up_stage, up_far)
    r_gate = Reduce(net, wg_grad, gate_near, gate_stage, gate_far)
    r_down = Collect(net, wd_grad, down_near, down_stage, down_far, group, wd_out)
    r_down.start()
    r_gate.start()
    r_up.start()

    wo_t = wo[net.s].reshape(width, LH * DH).astype(F32).T.astype(BF16)
    for b in range(NS):
        here = slice(tokens * b, tokens * (b + 1))
        grad_att[:, :, here] = dot_nt(wo_t, branch[b]).astype(BF16).reshape(LH, DH, tokens)
    out_t = sum(
        dot_nn(att_t[:, :, tokens * b : tokens * (b + 1)].reshape(LH * DH, tokens), branch[b]) for b in range(NS)
    )
    wo_grad[...] = out_t.T.astype(BF16).reshape(wo_grad.shape)
    r_o = Reduce(net, wo_grad, o_near, o_stage, o_far)

    grad_k[...] = jnp.zeros_like(grad_k)
    grad_v[...] = jnp.zeros_like(grad_v)
    factors[...] = jnp.zeros_like(factors)
    f_gn = Fold(net, gn_out, gn_in)

    for j in range(NS - 1, -1, -1):
        here = slice(tokens * j, tokens * (j + 1))
        upto = tokens * j

        def one_head(h, _):
            q = qt[h, :, here]
            da = grad_att[h, :, here]
            stat = lse[h, :, here]
            keep = lax.broadcasted_iota(jnp.int32, (tokens, tokens), 0) <= lax.broadcasted_iota(
                jnp.int32, (tokens, tokens), 1
            )
            probs = jnp.exp(jnp.where(keep, dot_nn(kn[h, here, :], q), MASKED) - stat)
            grad_probs = dot_nn(vn[h, here, :], da)
            delta = jnp.sum(probs * grad_probs, axis=0, keepdims=True)
            if j > 0:
                probs_low = jnp.exp(dot_nn(kn[h, 0:upto, :], q) - stat)
                grad_low = dot_nn(vn[h, 0:upto, :], da)
                delta = delta + jnp.sum(probs_low * grad_low, axis=0, keepdims=True)
            ds = (probs * (grad_probs - delta)).astype(BF16)
            gq = dot_nn(kt[h, :, here], ds)
            grad_k[h, :, here] += dot_nt(q, ds)
            grad_v[h, :, here] += dot_nt(da, probs.astype(BF16))
            if j > 0:
                ds_low = (probs_low * (grad_low - delta)).astype(BF16)
                gq = gq + dot_nn(kt[h, :, 0:upto], ds_low)
                grad_k[h, :, 0:upto] += dot_nt(q, ds_low)
                grad_v[h, :, 0:upto] += dot_nt(da, probs_low.astype(BF16))
            grad_q[h] = gq * DH**-0.5
            return 0

        lax.fori_loop(0, LH, one_head, 0)

        cosine, sine = cos_ref[:, here], sin_ref[:, here]

        def turned_back(piece):
            first, second = piece[: DH // 2], piece[DH // 2 :]
            return jnp.concatenate([first * cosine + second * sine, second * cosine - first * sine], axis=0)

        own = heads[:, here]
        rows_of = []
        pieces = []
        base = 0
        for grads, rank, turn in (
            ([grad_q[h] for h in range(LH)], RQ, True),
            ([grad_k[h, :, here] for h in range(LH)], RK, True),
            ([grad_v[h, :, here] for h in range(LH)], RK, False),
        ):
            for r in range(rank):
                index = len(pieces)
                part = shared[index // 5, DH * (index % 5) : DH * (index % 5 + 1), here].astype(F32)
                rot = sum(own[base + h * rank + r : base + h * rank + r + 1] * grads[h] for h in range(LH)) * (1.0 / rank)
                pieces.append(turned_back(rot) if turn else rot)
                for h in range(LH):
                    rows_of.append(
                        (base + h * rank + r, jnp.sum(part * grads[h], axis=0, keepdims=True) * (1.0 / rank))
                    )
            base += LH * rank
        for index, value in enumerate(pieces):
            factors[index // 5, DH * (index % 5) : DH * (index % 5 + 1), here] = value.astype(BF16)
        own_rows = jnp.concatenate([value for _, value in sorted(rows_of, key=lambda pair: pair[0])], axis=0)
        own_rows = jnp.concatenate([own_rows, jnp.zeros((WF - NSH - NH, tokens), F32)], axis=0)
        factors[net.core, NSH:, here] = own_rows.astype(BF16)

        if j == 3:
            r_down.forward()
        if j == 2:
            for k in range(1, net.no):
                r_gate.forward(k)
        if j == 1:
            for k in range(1, net.no):
                r_up.forward(k)
    r_o.start()

    attn_gain = jnp.zeros((1, width), F32)

    def normed_grad(b):
        columns = pl.ds(pl.multiple_of(b * tokens, tokens), tokens)
        value = sum(dot_nn(factors[half, :, columns].astype(F32).T.astype(BF16), wft[half]) for half in range(2))
        x = tok[b].astype(F32)
        scale = lax.rsqrt(jnp.mean(x * x, axis=-1, keepdims=True) + EPS)
        return value, x * scale, scale

    value, normal, _ = normed_grad(net.diag)
    attn_gain += jnp.sum(value * normal, axis=0, keepdims=True)
    f_gn.to_diag(value)
    value, normal, _ = normed_grad(net.across)
    attn_gain += jnp.sum(value * normal, axis=0, keepdims=True)
    f_gn.to_across(value)
    value, normal, _ = normed_grad(net.sib)
    attn_gain += jnp.sum(value * normal, axis=0, keepdims=True)
    f_gn.to_sibling(value)
    value, normal, scale = normed_grad(net.s)
    attn_gain += jnp.sum(value * normal, axis=0, keepdims=True)
    gn_keep[...] = value

    other = dot_nn(factors[1 - net.core], normed[...])
    wf_grad[1] = other.T.astype(BF16).reshape(wf_grad.shape[1:])
    slot_sib = net.take(1)
    net.send(wf_grad.at[1], wf_near, slot_sib, {"seq": net.sib})
    mine = dot_nn(factors[net.core], normed[...])
    mine = jnp.concatenate(
        [mine[: NSH + NH], attn_gain, gain_grad[0:1], mine[NSH + NH + 2 :]],
        axis=0,
    )
    mine = mine.T
    net.arrived(wf_near, slot_sib)
    wf_grad[0] = (mine.reshape(wf_grad.shape[1:]) + wf_near[...].astype(F32)).astype(BF16)
    r_f = Reduce(net, wf_grad.at[0], f_near, f_stage, f_far)
    r_f.start()

    for k in range(1, net.no):
        r_o.forward(k)
    for k in range(1, net.no):
        r_f.forward(k)
    total = f_gn.total(gn_keep[...])
    scaled = total * gains[0:1, :]
    input_grad[...] = (
        grad_mid[...] + scale * (scaled - normal * jnp.mean(scaled * normal, axis=-1, keepdims=True))
    ).astype(BF16)

    shares = []
    r_down.finish()
    for reduce, out in ((r_gate, wg_out), (r_up, wu_out), (r_o, wo_out), (r_f, wf_out)):
        out[net.s] = reduce.finish().astype(BF16)
        share = Share(net, lambda r, out=out: out.at[r])
        share.start(out.at[net.s])
        shares.append(share)
    r_down.forward_into()
    for share in shares:
        share.forward()
    for share in shares:
        share.near()
        share.last()
    net.drain()


def run_third(n, tok, branch, grad_mid, gain_grad, wg_grad, wu_grad, wd_grad, wo, normed, wft, gains, shared, heads, qt, kt, kn, vn, lse, att_t, cosine, sine):
    tokens, width = tok.shape[1:]
    length = tokens * NS
    rows, cols = wg_grad.shape[1:]
    down = wd_grad.shape[1:]
    hd = LH * DH
    ni = 2 if n <= 8 else 4
    no = n // ni
    wide = no // NS
    shapes = [
        ((tokens, width), BF16),
        ((NS, rows, cols), BF16),
        ((NS, rows, cols), BF16),
        (down, BF16),
        ((NS, rows, hd), BF16),
        ((NS, rows, WF), BF16),
    ]
    scratch = [
        ((LH, DH, length), BF16),
        ((LH, DH, tokens), F32),
        ((LH, DH, length), F32),
        ((LH, DH, length), F32),
        ((2, WF, length), BF16),
        ((n, rows, hd), BF16),
        ((2, n, rows, WF), BF16),
        ((n, rows, WF), BF16),
    ]
    for last in (cols, cols):
        scratch += [((ni - 1, no, rows, last), BF16), ((no - 1, rows, last), BF16), ((no - 1, rows, last), BF16)]
    scratch += [((ni - 1, wide) + down, BF16), ((wide,) + down, BF16), ((no - 1,) + down, BF16)]
    for last in (hd, WF):
        scratch += [((ni - 1, no, rows, last), BF16), ((no - 1, rows, last), BF16), ((no - 1, rows, last), BF16)]
    scratch += [((3, tokens, width), BF16), ((3, tokens, width), BF16), ((tokens, width), F32)]
    return pl.pallas_call(
        functools.partial(third_kernel, n),
        out_shape=[jax.ShapeDtypeStruct(*shape) for shape in shapes],
        in_specs=vmem_space(21),
        out_specs=vmem_space(len(shapes)),
        scratch_shapes=[pltpu.VMEM(*s) for s in scratch] + sems(n),
        compiler_params=pltpu.CompilerParams(collective_id=3, has_side_effects=True, vmem_limit_bytes=VMEM_LIMIT),
    )(tok, branch, grad_mid, gain_grad, wg_grad, wu_grad, wd_grad, wo, normed, wft, gains, shared, heads, qt, kt, kn, vn, lse, att_t, cosine, sine)


def shards(tokens, attn_gain, qh, qs, kh, ks, vh, vs, out_proj, ffn_gain, gate, up, down, cotangent):
    n = lax.axis_size("fsdp")
    wf, wo, wg, wu = prepare(attn_gain, qh, qs, kh, ks, vh, vs, out_proj, ffn_gain, gate, up)
    cosine, sine = tables(tokens.shape[1] * NS)
    (tok, cot, wo, wg, wu, wd, att, normed, wft, gains, shared, heads, qt, kt, vt, kn, vn, lse, att_t) = run_first(
        n, tokens[0], wf, wo, wg, wu, down, cotangent[0], cosine, sine
    )
    wd = wd.reshape(-1, wd.shape[-1])
    result, branch, grad_mid, gain_grad, wg_grad, wu_grad, wd_grad = run_second(
        n, tok, cot, wo, wg, wu, wd, att, gains
    )
    input_grad, wg_out, wu_out, wd_out, wo_out, wf_out = run_third(
        n, tok, branch, grad_mid, gain_grad, wg_grad, wu_grad, wd_grad, wo, normed, wft, gains, shared, heads, qt, kt, kn, vn, lse, att_t, cosine, sine
    )
    rank_of = [(NS - b) % NS for b in range(NS)]
    gate_grad = jnp.concatenate([wg_out[r] for r in rank_of], axis=1).astype(F32)
    up_grad = jnp.concatenate([wu_out[r] for r in rank_of], axis=1).astype(F32)
    out_grad = jnp.concatenate([wo_out[r] for r in range(NS)], axis=1).astype(F32)
    f = wf_out.astype(F32)
    first = f[0, :, :NSH] + f[2, :, :NSH]
    last = f[1, :, :NSH] + f[3, :, :NSH]
    qs_grad = jnp.concatenate([first, last[:, :DH]], axis=1)
    ks_grad = last[:, DH : DH + RK * DH]
    vs_grad = last[:, DH + RK * DH :]
    at = NSH
    heads_grad = []
    for rank in (RQ, RK, RK):
        heads_grad.append(jnp.concatenate([f[r, :, at : at + LH * rank] for r in range(NS)], axis=1))
        at += LH * rank
    attn_gain_grad = jnp.sum(f[:, :, at], axis=0)
    ffn_gain_grad = jnp.sum(f[:, :, at + 1], axis=0)
    return (
        result[None],
        input_grad[None],
        attn_gain_grad,
        heads_grad[0],
        qs_grad,
        heads_grad[1],
        ks_grad,
        heads_grad[2],
        vs_grad,
        out_grad,
        ffn_gain_grad,
        gate_grad,
        up_grad,
        wd_out.astype(F32),
    )


def solution(mesh):
    tokens = P("fsdp", "seq", None)
    matrix = P("fsdp", None)
    vector = P("fsdp")
    kinds = (vector,) + (matrix,) * 7 + (vector,) + (matrix,) * 3
    return jax.shard_map(
        shards,
        mesh=mesh,
        in_specs=(tokens,) + kinds + (tokens,),
        out_specs=(tokens, tokens) + kinds,
        check_vma=False,
    )
```

```python
import functools

import jax
import jax.numpy as jnp
import numpy as np
from jax import lax
from jax.experimental import pallas as pl
from jax.experimental.pallas import tpu as pltpu
from jax.sharding import PartitionSpec as P

H = 16
DH = 64
RQ = 6
RK = 2
NS = 4
LH = H // NS
EPS = 1e-06
BASE = 10000.0
MASKED = -1e30
NSH = 320
NH = 40
WF = 384
F32 = jnp.float32
BF16 = jnp.bfloat16
VMEM_LIMIT = 62 << 20


def dot_nn(a, b):
    return lax.dot_general(a, b, (((1,), (0,)), ((), ())), preferred_element_type=F32)


def dot_nt(a, b):
    return lax.dot_general(a, b, (((1,), (1,)), ((), ())), preferred_element_type=F32)


class Net:
    def __init__(self, n, send_sems, recv_sems):
        self.n = n
        self.ni = 2 if n <= 8 else 4
        self.no = n // self.ni
        self.s = lax.axis_index("seq")
        self.f = lax.axis_index("fsdp")
        self.o = self.f // self.ni
        self.i = self.f % self.ni
        self.core = self.s % 2
        self.sib = self.s + 1 - 2 * self.core
        self.across = (self.s + 2) % 4
        self.diag = (self.sib + 2) % 4
        self.send_sems = send_sems
        self.recv_sems = recv_sems
        self.sends = 0
        self.recvs = 0
        self.open = []

    def at(self, o, i):
        return o * self.ni + i

    def outer(self, k):
        return (self.o + k) % self.no

    def inner(self, m):
        return (self.i + m) % self.ni

    def take(self, count):
        first = self.recvs
        self.recvs += count
        return first

    def barrier(self):
        sem = pltpu.get_barrier_semaphore()
        peers = [{"seq": self.sib}, {"seq": self.across}]
        peers += [{"fsdp": self.at(self.outer(k), self.i)} for k in range(1, self.no)]
        peers += [{"fsdp": self.at(self.o, self.inner(m))} for m in range(1, self.ni)]
        for peer in peers:
            pl.semaphore_signal(sem, inc=1, device_id=peer, device_id_type=pl.DeviceIdType.MESH)
        pl.semaphore_wait(sem, len(peers))

    def send(self, src, dst, slot, device, when=None):
        copy = pltpu.make_async_remote_copy(
            src_ref=src,
            dst_ref=dst,
            send_sem=self.send_sems.at[self.sends],
            recv_sem=self.recv_sems.at[slot],
            device_id=device,
            device_id_type=pl.DeviceIdType.MESH,
        )
        self.sends += 1
        if when is None:
            copy.start()
        else:
            pl.when(when)(copy.start)
        self.open.append((copy, when))

    def local(self, src, dst):
        copy = pltpu.make_async_copy(src, dst, self.send_sems.at[self.sends])
        self.sends += 1
        copy.start()
        return copy

    def arrived(self, dst, slot):
        pltpu.make_async_remote_copy(
            src_ref=dst,
            dst_ref=dst,
            send_sem=self.send_sems.at[0],
            recv_sem=self.recv_sems.at[slot],
            device_id={"seq": self.sib},
            device_id_type=pl.DeviceIdType.MESH,
        ).wait_recv()

    def taken(self):
        copies, self.open = self.open, []
        return copies

    def settle(self, copies):
        for copy, when in copies:
            if when is None:
                copy.wait_send()
            else:
                pl.when(when)(copy.wait_send)


class Gather:
    def __init__(self, net, src, dst):
        self.net, self.src, self.dst = net, src, dst
        self.slot = net.take(net.n)

    def start(self):
        net = self.net
        own = self.dst.at[net.f]
        for m in range(1, net.ni):
            net.send(self.src, own, self.slot + net.f, {"fsdp": net.at(net.o, net.inner(m))})
        for k in range(1, net.no):
            net.send(self.src, own, self.slot + net.f, {"fsdp": net.at(net.outer(k), net.i)})
        self.own = net.local(self.src, own)

    def block(self, index):
        self.net.arrived(self.dst.at[index], self.slot + index)

    def forward(self, k, then=None):
        net = self.net
        index = net.at((net.o - k + net.no) % net.no, net.i)
        self.block(index)
        for m in range(1, net.ni):
            net.send(self.dst.at[index], self.dst.at[index], self.slot + index, {"fsdp": net.at(net.o, net.inner(m))})
        if then is not None:
            then(index)

    def finish(self, then=None):
        net = self.net
        for k in range(net.no):
            for m in range(1, net.ni):
                index = net.at((net.o - k + net.no) % net.no, net.inner(m))
                self.block(index)
                if then is not None:
                    then(index)
        self.own.wait()


class Spread:
    def __init__(self, net, src, dst, group):
        self.net, self.src, self.dst = net, src, dst
        self.wide = net.no // NS
        self.first = group * self.wide
        self.slot = net.take(net.n // NS)
        self.mine = jnp.logical_and(net.o >= self.first, net.o < self.first + self.wide)

    def place(self, o, i):
        return (o - self.first) * self.net.ni + i

    def start(self):
        net = self.net
        index = jnp.where(self.mine, self.place(net.o, net.i), 0)
        own = self.dst.at[index]
        for m in range(1, net.ni):
            net.send(self.src, own, self.slot + index, {"fsdp": net.at(net.o, net.inner(m))}, self.mine)
        for k in range(1, net.no):
            net.send(self.src, own, self.slot + index, {"fsdp": net.at(net.outer(k), net.i)}, self.mine)
        self.own = pltpu.make_async_copy(self.src, own, net.send_sems.at[net.sends])
        net.sends += 1
        pl.when(self.mine)(self.own.start)

    def forward(self):
        net = self.net
        for g in range(self.wide):
            other = net.o != self.first + g
            index = g * net.ni + net.i

            @pl.when(other)
            def _():
                net.arrived(self.dst.at[index], self.slot + index)

            for m in range(1, net.ni):
                net.send(
                    self.dst.at[index],
                    self.dst.at[index],
                    self.slot + index,
                    {"fsdp": net.at(net.o, net.inner(m))},
                    other,
                )

    def finish(self):
        net = self.net
        for g in range(self.wide):
            for m in range(1, net.ni):
                index = g * net.ni + net.inner(m)
                net.arrived(self.dst.at[index], self.slot + index)
        pl.when(self.mine)(self.own.wait)


class Share:
    def __init__(self, net, dst):
        self.net, self.dst = net, dst
        self.slot = net.take(NS)

    def start(self, src):
        net = self.net
        own = self.dst(net.s)
        net.send(src, own, self.slot + net.s, {"seq": net.across})
        net.send(src, own, self.slot + net.s, {"seq": net.sib})

    def forward(self):
        net = self.net
        far = self.dst(net.across)
        net.arrived(far, self.slot + net.across)
        net.send(far, far, self.slot + net.across, {"seq": net.sib})

    def near(self):
        net = self.net
        net.arrived(self.dst(net.sib), self.slot + net.sib)

    def last(self):
        net = self.net
        net.arrived(self.dst(net.diag), self.slot + net.diag)


class Fold:
    def __init__(self, net, out, into):
        self.net, self.out, self.into = net, out, into
        self.slot = net.take(3)

    def to_diag(self, value):
        net = self.net
        self.out[0] = value.astype(BF16)
        net.send(self.out.at[0], self.into.at[0], self.slot, {"seq": net.sib})

    def to_across(self, value):
        net = self.net
        net.arrived(self.into.at[0], self.slot)
        self.out[1] = (value + self.into[0].astype(F32)).astype(BF16)
        net.send(self.out.at[1], self.into.at[2], self.slot + 2, {"seq": net.across})

    def to_sibling(self, value):
        net = self.net
        self.out[2] = value.astype(BF16)
        net.send(self.out.at[2], self.into.at[1], self.slot + 1, {"seq": net.sib})

    def total(self, value):
        net = self.net
        net.arrived(self.into.at[1], self.slot + 1)
        net.arrived(self.into.at[2], self.slot + 2)
        return value + self.into[1].astype(F32) + self.into[2].astype(F32)


class Reduce:
    def __init__(self, net, src, near, far):
        self.net, self.src, self.near, self.far = net, src, near, far
        self.slot_near = net.take((net.ni - 1) * net.no)
        self.slot_far = net.take(net.no - 1)

    def start(self):
        net = self.net
        for k in [*range(1, net.no), 0]:
            o = net.outer(k)
            for m in range(1, net.ni):
                net.send(
                    self.src.at[net.at(o, net.inner(m))],
                    self.near.at[m - 1, o],
                    self.slot_near + (m - 1) * net.no + o,
                    {"fsdp": net.at(net.o, net.inner(m))},
                )

    def column(self, o):
        net = self.net
        value = self.src[net.at(o, net.i)].astype(F32)
        for m in range(1, net.ni):
            net.arrived(self.near.at[m - 1, o], self.slot_near + (m - 1) * net.no + o)
            value = value + self.near[m - 1, o].astype(F32)
        return value

    def forward(self, k):
        net = self.net
        o = net.outer(k)
        index = net.at(o, net.i)
        self.src[index] = self.column(o).astype(BF16)
        net.send(self.src.at[index], self.far.at[k - 1], self.slot_far + k - 1, {"fsdp": net.at(o, net.i)})

    def finish(self):
        net = self.net
        value = self.column(net.o)
        for k in range(1, net.no):
            net.arrived(self.far.at[k - 1], self.slot_far + k - 1)
            value = value + self.far[k - 1].astype(F32)
        return value


class Collect:
    def __init__(self, net, src, near, far, group, into):
        self.net, self.src, self.near, self.far, self.into = net, src, near, far, into
        self.wide = net.no // NS
        self.first = group * self.wide
        self.mine = jnp.logical_and(net.o >= self.first, net.o < self.first + self.wide)
        self.slot_near = net.take((net.ni - 1) * self.wide)
        self.slot_far = net.take(net.no - 1)
        self.slot_into = net.take(1)
        self.owner = (NS - net.o // self.wide) % NS

    def start(self):
        net = self.net
        for g in range(self.wide):
            for m in range(1, net.ni):
                net.send(
                    self.src.at[g * net.ni + net.inner(m)],
                    self.near.at[m - 1, g],
                    self.slot_near + (m - 1) * self.wide + g,
                    {"fsdp": net.at(net.o, net.inner(m))},
                )

    def forward(self):
        net = self.net
        for g in range(self.wide):
            index = g * net.ni + net.i
            value = self.src[index].astype(F32)
            for m in range(1, net.ni):
                net.arrived(self.near.at[m - 1, g], self.slot_near + (m - 1) * self.wide + g)
                value = value + self.near[m - 1, g].astype(F32)
            self.src[index] = value.astype(BF16)
            o = self.first + g
            step = (o - net.o + net.no) % net.no
            away = step > 0
            place = jnp.where(away, step - 1, 0)
            net.send(self.src.at[index], self.far.at[place], self.slot_far + place, {"fsdp": net.at(o, net.i)}, away)

    def finish(self):
        net = self.net

        @pl.when(self.mine)
        def _():
            value = self.src[jnp.where(self.mine, net.f - self.first * net.ni, 0)].astype(F32)
            for k in range(1, net.no):
                net.arrived(self.far.at[k - 1], self.slot_far + k - 1)
                value = value + self.far[k - 1].astype(F32)
            self.into[...] = value.astype(BF16)

        net.send(self.into, self.into, self.slot_into, {"seq": net.across}, self.mine)
        net.send(self.into, self.into, self.slot_into, {"seq": net.sib}, self.mine)

    def forward_into(self):
        net = self.net
        other = net.s != self.owner
        pl.when(other)(lambda: net.arrived(self.into, self.slot_into))
        net.send(self.into, self.into, self.slot_into, {"seq": net.sib}, net.across == self.owner)


def matrix_of(ref):
    count, rows, cols = ref.shape
    if rows % 8 == 0:
        return ref[...].reshape(count * rows, cols)
    return jnp.concatenate([ref[index].astype(F32) for index in range(count)], axis=0).astype(BF16)


def kernel(n, names, *refs):
    r = dict(zip(names, refs, strict=True))
    net = Net(n, r["send_sems"], r["recv_sems"])
    tok, cot, wo, wg, wu, wd, att = (r[k] for k in ("tok", "cot", "wo", "wg", "wu", "wd", "att"))
    wf, wft, gains, shared, heads = (r[k] for k in ("wf", "wft", "gains", "shared", "heads"))
    qt, kt, vt, kn, vn, lse, att_t = (r[k] for k in ("qt", "kt", "vt", "kn", "vn", "lse", "att_t"))
    cos_ref, sin_ref = r["cosine"], r["sine"]
    tokens, width = tok.shape[1:]
    length = NS * tokens
    rows, cols = wg.shape[1:]
    group = (NS - net.s) % NS
    net.barrier()

    g_wf = Gather(net, r["wf_in"], wf.at[net.core])
    s_tok = Share(net, lambda rank: tok.at[rank])
    slot_sib = net.take(n)

    def to_sibling(index):
        here = wf.at[net.core, index]
        net.send(here, here, slot_sib + index, {"seq": net.sib})

    g_wf.start()
    net.send(r["wf_in"], wf.at[net.core, net.f], slot_sib + net.f, {"seq": net.sib})
    s_tok.start(r["tok_in"])
    own_tok = net.local(r["tok_in"], tok.at[net.s])
    for k in range(1, net.no):
        g_wf.forward(k, to_sibling)
    g_wf.finish(to_sibling)

    g_wo = Gather(net, r["wo_in"], wo.at[net.s])
    g_wd = Spread(net, r["wd_in"], wd, group)
    g_wg = Gather(net, r["wg_in"], wg)
    g_wu = Gather(net, r["wu_in"], wu)
    g_wo.start()
    g_wd.start()
    s_tok.forward()
    s_cot = Share(net, lambda rank: cot.at[rank])
    s_cot.start(r["cot_in"])
    own_cot = net.local(r["cot_in"], cot.at[net.s])
    for index in range(n):
        net.arrived(wf.at[1 - net.core, index], slot_sib + index)

    for half in range(2):
        whole = wf[half].reshape(n * rows, WF).astype(F32).T
        wft[half] = whole.astype(BF16)
        if half == 0:
            gains[...] = whole[NSH + NH : NSH + NH + 8, :]
    own_tok.wait()
    s_tok.near()
    s_tok.last()

    s_att = [Share(net, lambda rank, j=j: att.at[rank, pl.ds(tokens * j, tokens)]) for j in range(NS)]
    s_wo = Share(net, lambda rank: wo.at[rank])

    def rounded(v):
        return v.astype(BF16).astype(F32)

    for j in range(NS):
        here = slice(tokens * j, tokens * (j + 1))
        upto = tokens * j
        values = tok[j].astype(F32)
        inv = lax.rsqrt(jnp.mean(values * values, axis=-1, keepdims=True) + EPS)
        block = (values * inv * gains[0:1, :]).astype(BF16)
        parts = [dot_nt(wft[half], block) for half in range(2)]
        own = dot_nt(wft[net.core, NSH:, :], block)
        cosine, sine = cos_ref[:, here], sin_ref[:, here]

        def turned(piece):
            first, second = piece[: DH // 2], piece[DH // 2 :]
            return jnp.concatenate([first * cosine - second * sine, first * sine + second * cosine], axis=0)

        def piece(half, index):
            return parts[half][DH * index : DH * (index + 1)]

        sq = [rounded(turned(piece(0, p))) for p in range(5)] + [rounded(turned(piece(1, 0)))]
        sk = [rounded(turned(piece(1, 1 + p))) for p in range(RK)]
        sv = [rounded(piece(1, 3 + p)) for p in range(RK)]
        for index, part in enumerate(sq + sk + sv):
            shared[index // 5, DH * (index % 5) : DH * (index % 5 + 1), here] = part.astype(BF16)
        own = rounded(own[:NH])
        heads[:, here] = own
        for h in range(LH):
            q = sum(own[h * RQ + p : h * RQ + p + 1] * sq[p] for p in range(RQ)) * (1.0 / RQ)
            first = LH * RQ
            k = sum(own[first + h * RK + p : first + h * RK + p + 1] * sk[p] for p in range(RK)) * (1.0 / RK)
            first = LH * (RQ + RK)
            v = sum(own[first + h * RK + p : first + h * RK + p + 1] * sv[p] for p in range(RK)) * (1.0 / RK)
            qt[h, :, here] = (q.astype(BF16).astype(F32) * DH**-0.5).astype(BF16)
            kt[h, :, here] = k.astype(BF16)
            vt[h, :, here] = v.astype(BF16)
            kn[h, here, :] = rounded(k).T.astype(BF16)
            vn[h, here, :] = rounded(v).T.astype(BF16)

        def one_head(h, _):
            q = qt[h, :, here]
            keep = lax.broadcasted_iota(jnp.int32, (tokens, tokens), 0) <= lax.broadcasted_iota(
                jnp.int32, (tokens, tokens), 1
            )
            diagonal = jnp.where(keep, dot_nn(kn[h, here, :], q), MASKED)
            top = jnp.max(diagonal, axis=0, keepdims=True)
            if j > 0:
                below = dot_nn(kn[h, 0:upto, :], q)
                top = jnp.maximum(top, jnp.max(below, axis=0, keepdims=True))
            diagonal = jnp.exp(diagonal - top)
            total = jnp.sum(diagonal, axis=0, keepdims=True)
            if j > 0:
                below = jnp.exp(below - top)
                total = total + jnp.sum(below, axis=0, keepdims=True)
            inverse = 1.0 / total
            result = dot_nn(vt[h, :, here], (diagonal * inverse).astype(BF16))
            if j > 0:
                result = result + dot_nn(vt[h, :, 0:upto], (below * inverse).astype(BF16))
            lse[h, :, here] = top + jnp.log(total)
            att_t[h, :, here] = result.astype(BF16)
            return 0

        lax.fori_loop(0, LH, one_head, 0)
        turn = att_t[:, :, here].reshape(LH * DH, tokens).astype(F32).T
        att[net.s, here, :] = turn.astype(BF16)
        s_att[j].start(att.at[net.s, pl.ds(tokens * j, tokens)])
        if j == 1:
            g_wg.start()
            for k in range(1, net.no):
                g_wo.forward(k)
            s_cot.forward()
        if j == 2:
            g_wo.finish()
            s_wo.start(wo.at[net.s])
            g_wd.forward()
            g_wu.start()
    for share in s_att:
        share.forward()
    s_wo.forward()
    for k in range(1, net.no):
        g_wg.forward(k)
    for share in [*s_att, s_wo, s_cot]:
        share.near()
        share.last()
    own_cot.wait()
    g_wd.finish()
    g_wg.finish()
    for k in range(1, net.no):
        g_wu.forward(k)
    g_wu.finish()
    opening = net.taken()

    gain = gains[1:2, :]
    f_dn = Fold(net, r["dn_out"], r["dn_in"])
    f_res = Fold(net, r["res_out"], r["res_in"])
    order = (net.diag, net.across, net.sib, net.s)
    n2_t, mixed_t, gg_all, gu_all = (r[k] for k in ("n2_t", "mixed_t", "gg", "gu"))
    mid_own, inv_own, dn_own, branch = (r[k] for k in ("mid_own", "inv_own", "dn_own", "branch"))
    result = r["result"]
    wd_all = matrix_of(wd)

    for step, b in enumerate(order):
        here = slice(tokens * step, tokens * (step + 1))
        span = pl.ds(pl.multiple_of(b * tokens, tokens), tokens)
        middle = tok[b].astype(F32)
        for rank in range(NS):
            middle = middle + dot_nt(att[rank, span, :], wo[rank].reshape(width, LH * DH))
        inv = lax.rsqrt(jnp.mean(middle * middle, axis=-1, keepdims=True) + EPS)
        normal = middle * inv
        block = (normal * gain).astype(BF16)
        n2_t[:, here] = block.astype(F32).T.astype(BF16)
        if step == 3:
            mid_own[...] = middle
            inv_own[...] = jnp.broadcast_to(inv, inv_own.shape)
        wg_all = matrix_of(wg)
        wu_all = matrix_of(wu)
        gate = dot_nn(block, wg_all)
        up = dot_nn(block, wu_all)
        sg = jax.nn.sigmoid(gate)
        act = gate * sg
        mixed = (act * up).astype(BF16)
        mixed_t[:, here] = mixed.astype(F32).T.astype(BF16)
        grad_mixed = dot_nt(cot[b], wd_all)
        gg = (grad_mixed * up * sg * (1.0 + gate * (1.0 - sg))).astype(BF16)
        gu = (grad_mixed * act).astype(BF16)
        gg_all[here, :] = gg
        gu_all[here, :] = gu
        dn = dot_nt(gg, wg_all) + dot_nt(gu, wu_all)
        if step == 0:
            f_dn.to_diag(dn)
        elif step == 1:
            f_dn.to_across(dn)
        elif step == 2:
            f_dn.to_sibling(dn)
        else:
            dn_own[...] = dn
        part = dot_nn(mixed, wd_all)
        if step == 0:
            f_res.to_diag(part)
        elif step == 1:
            f_res.out[1] = part.astype(BF16)
        elif step == 2:
            f_res.to_sibling(part)
        else:
            result[...] = part.astype(BF16)

    folded = net.taken()
    net.settle(opening)
    wg_grad, wu_grad, wd_grad = wg, wu, wd
    r_down = Collect(net, wd_grad, r["down_near"], r["down_far"], group, r["wd_out"])
    r_gate = Reduce(net, wg_grad, r["gate_near"], r["gate_far"])
    r_up = Reduce(net, wu_grad, r["up_near"], r["up_far"])

    wd_rows = wd_grad.shape[1]
    down = sum(dot_nn(mixed_t[:, tokens * k : tokens * (k + 1)], cot[b]) for k, b in enumerate(order))
    for index in range(wd_grad.shape[0]):
        wd_grad[index] = down[wd_rows * index : wd_rows * (index + 1)].astype(BF16)
    r_down.start()

    total = f_dn.total(dn_own[...])
    inv = inv_own[:, 0:1]
    normal = mid_own[...] * inv
    scaled = total * gain
    mid_grad = cot[net.s].astype(F32) + inv * (scaled - normal * jnp.mean(scaled * normal, axis=-1, keepdims=True))
    grad_mid = r["grad_mid"]
    grad_mid[...] = mid_grad
    ffn_gain = jnp.sum(total * normal, axis=0, keepdims=True)
    branch[net.s] = mid_grad.astype(BF16)
    s_branch = Share(net, lambda rank: branch.at[rank])
    s_branch.start(branch.at[net.s])

    wg_grad[...] = dot_nn(n2_t[...], gg_all[...]).astype(BF16).reshape(wg_grad.shape)
    r_gate.start()
    wu_grad[...] = dot_nn(n2_t[...], gu_all[...]).astype(BF16).reshape(wu_grad.shape)
    r_up.start()

    s_branch.forward()
    f_res.to_across(f_res.out[1].astype(F32))
    r_down.forward()
    wo_t = wo[net.s].reshape(width, LH * DH).astype(F32).T.astype(BF16)
    s_branch.near()
    s_branch.last()

    grad_att, grad_q, grad_k, grad_v = (r[k] for k in ("vt", "grad_q", "grad_k", "grad_v"))
    factors = n2_t
    wo_grad, wf_grad, wf_near = wo.at[net.diag], wf.at[0], mixed_t.at[pl.ds(0, WF)]
    for b in range(NS):
        here = slice(tokens * b, tokens * (b + 1))
        grad_att[:, :, here] = dot_nt(wo_t, branch[b]).astype(BF16).reshape(LH, DH, tokens)
    out_t = sum(
        dot_nn(att_t[:, :, tokens * b : tokens * (b + 1)].reshape(LH * DH, tokens), branch[b]) for b in range(NS)
    )
    wo_grad[...] = out_t.T.astype(BF16).reshape(n, rows, LH * DH)
    r_o = Reduce(net, wo_grad, r["o_near"], r["o_far"])

    grad_k[...] = jnp.zeros_like(grad_k)
    grad_v[...] = jnp.zeros_like(grad_v)
    factors[: 2 * WF, :] = jnp.zeros((2 * WF, length), BF16)
    net.settle(folded)
    f_gn = Fold(net, r["dn_out"], r["dn_in"])

    for j in range(NS - 1, -1, -1):
        here = slice(tokens * j, tokens * (j + 1))
        upto = tokens * j

        def one_head(h, _):
            q = qt[h, :, here]
            da = grad_att[h, :, here]
            stat = lse[h, :, here]
            keep = lax.broadcasted_iota(jnp.int32, (tokens, tokens), 0) <= lax.broadcasted_iota(
                jnp.int32, (tokens, tokens), 1
            )
            probs = jnp.exp(jnp.where(keep, dot_nn(kn[h, here, :], q), MASKED) - stat)
            grad_probs = dot_nn(vn[h, here, :], da)
            delta = jnp.sum(probs * grad_probs, axis=0, keepdims=True)
            if j > 0:
                probs_low = jnp.exp(dot_nn(kn[h, 0:upto, :], q) - stat)
                grad_low = dot_nn(vn[h, 0:upto, :], da)
                delta = delta + jnp.sum(probs_low * grad_low, axis=0, keepdims=True)
            ds = (probs * (grad_probs - delta)).astype(BF16)
            gq = dot_nn(kt[h, :, here], ds)
            grad_k[h, :, here] += dot_nt(q, ds)
            grad_v[h, :, here] += dot_nt(da, probs.astype(BF16))
            if j > 0:
                ds_low = (probs_low * (grad_low - delta)).astype(BF16)
                gq = gq + dot_nn(kt[h, :, 0:upto], ds_low)
                grad_k[h, :, 0:upto] += dot_nt(q, ds_low)
                grad_v[h, :, 0:upto] += dot_nt(da, probs_low.astype(BF16))
            grad_q[h] = gq * DH**-0.5
            return 0

        lax.fori_loop(0, LH, one_head, 0)

        cosine, sine = cos_ref[:, here], sin_ref[:, here]

        def turned_back(piece):
            first, second = piece[: DH // 2], piece[DH // 2 :]
            return jnp.concatenate([first * cosine + second * sine, second * cosine - first * sine], axis=0)

        own = heads[:, here]
        rows_of = []
        pieces = []
        base = 0
        for grads, rank, turn in (
            ([grad_q[h] for h in range(LH)], RQ, True),
            ([grad_k[h, :, here] for h in range(LH)], RK, True),
            ([grad_v[h, :, here] for h in range(LH)], RK, False),
        ):
            for p in range(rank):
                index = len(pieces)
                part = shared[index // 5, DH * (index % 5) : DH * (index % 5 + 1), here].astype(F32)
                rot = sum(own[base + h * rank + p : base + h * rank + p + 1] * grads[h] for h in range(LH)) * (1.0 / rank)
                pieces.append(turned_back(rot) if turn else rot)
                for h in range(LH):
                    rows_of.append(
                        (base + h * rank + p, jnp.sum(part * grads[h], axis=0, keepdims=True) * (1.0 / rank))
                    )
            base += LH * rank
        for index, value in enumerate(pieces):
            first_row = WF * (index // 5) + DH * (index % 5)
            factors[first_row : first_row + DH, here] = value.astype(BF16)
        own_rows = jnp.concatenate([value for _, value in sorted(rows_of, key=lambda pair: pair[0])], axis=0)
        own_rows = jnp.concatenate([own_rows, jnp.zeros((WF - NSH - NH, tokens), F32)], axis=0)
        factors[pl.ds(pl.multiple_of(net.core * WF + NSH, DH), WF - NSH), here] = own_rows.astype(BF16)

        if j == 3:
            for k in range(1, net.no):
                r_gate.forward(k)
        if j == 2:
            result[...] = (mid_own[...] + f_res.total(result[...].astype(F32))).astype(BF16)
        if j == 1:
            for k in range(1, net.no):
                r_up.forward(k)
    r_o.start()

    attn_gain = jnp.zeros((1, width), F32)

    def normed_grad(b):
        columns = pl.ds(pl.multiple_of(b * tokens, tokens), tokens)
        value = sum(dot_nn(factors[WF * half : WF * (half + 1), columns].astype(F32).T.astype(BF16), wft[half]) for half in range(2))
        x = tok[b].astype(F32)
        scale = lax.rsqrt(jnp.mean(x * x, axis=-1, keepdims=True) + EPS)
        normal = x * scale
        cot[b] = (normal * gains[0:1, :]).astype(BF16)
        return value, normal, scale

    value, normal, _ = normed_grad(net.diag)
    attn_gain += jnp.sum(value * normal, axis=0, keepdims=True)
    f_gn.to_diag(value)
    value, normal, _ = normed_grad(net.across)
    attn_gain += jnp.sum(value * normal, axis=0, keepdims=True)
    f_gn.to_across(value)
    value, normal, _ = normed_grad(net.sib)
    attn_gain += jnp.sum(value * normal, axis=0, keepdims=True)
    f_gn.to_sibling(value)
    value, normal, scale = normed_grad(net.s)
    attn_gain += jnp.sum(value * normal, axis=0, keepdims=True)
    dn_own[...] = value

    def map_grad(half):
        return sum(dot_nn(factors[pl.ds(pl.multiple_of(half * WF, WF), WF), tokens * b : tokens * (b + 1)], cot[b]) for b in range(NS))

    slot_map = net.take(1)
    out_map = wft.at[1]
    out_map[...] = map_grad(1 - net.core).astype(BF16)
    net.send(out_map, wf_near, slot_map, {"seq": net.sib})
    mine = map_grad(net.core)
    net.arrived(wf_near, slot_map)
    mine = mine + wf_near[...].astype(F32)
    mine = jnp.concatenate([mine[: NSH + NH], attn_gain, ffn_gain, mine[NSH + NH + 2 :]], axis=0)
    wf_grad[...] = mine.T.astype(BF16).reshape(n, rows, WF)
    r_f = Reduce(net, wf_grad, r["f_near"], r["f_far"])
    r_f.start()

    for k in range(1, net.no):
        r_o.forward(k)
    for k in range(1, net.no):
        r_f.forward(k)
    total = f_gn.total(dn_own[...])
    scaled = total * gains[0:1, :]
    r["input_grad"][...] = (
        grad_mid[...] + scale * (scaled - normal * jnp.mean(scaled * normal, axis=-1, keepdims=True))
    ).astype(BF16)

    shares = []
    r_down.finish()
    for reduce, out in ((r_gate, "wg_out"), (r_up, "wu_out"), (r_o, "wo_out"), (r_f, "wf_out")):
        out = r[out]
        out[net.s] = reduce.finish().astype(BF16)
        share = Share(net, lambda rank, out=out: out.at[rank])
        share.start(out.at[net.s])
        shares.append(share)
    r_down.forward_into()
    for share in shares:
        share.forward()
    for share in shares:
        share.near()
        share.last()
    net.settle(net.taken())


def sems(n):
    return [pltpu.SemaphoreType.DMA((10 * n + 80,))] * 2


def any_space(count):
    return [pl.BlockSpec(memory_space=pl.ANY)] * count


def vmem_space(count):
    return [pl.BlockSpec(memory_space=pltpu.VMEM)] * count


def run(n, given):
    tokens, width = given["tok_in"].shape
    length = tokens * NS
    rows, cols = given["wg_in"].shape
    down = given["wd_in"].shape
    hd = LH * DH
    ni = 2 if n <= 8 else 4
    no = n // ni
    wide = no // NS
    outs = {
        "result": ((tokens, width), BF16),
        "input_grad": ((tokens, width), BF16),
        "wg_out": ((NS, rows, cols), BF16),
        "wu_out": ((NS, rows, cols), BF16),
        "wd_out": (down, BF16),
        "wo_out": ((NS, rows, hd), BF16),
        "wf_out": ((NS, rows, WF), BF16),
    }
    scratch = {
        "tok": ((NS, tokens, width), BF16),
        "cot": ((NS, tokens, width), BF16),
        "wo": ((NS, n, rows, hd), BF16),
        "wg": ((n, rows, cols), BF16),
        "wu": ((n, rows, cols), BF16),
        "wd": ((n // NS,) + down, BF16),
        "att": ((NS, length, hd), BF16),
        "wf": ((2, n, rows, WF), BF16),
        "wft": ((2, WF, width), BF16),
        "gains": ((8, width), F32),
        "shared": ((2, NSH, length), BF16),
        "heads": ((NH, length), F32),
        "qt": ((LH, DH, length), BF16),
        "kt": ((LH, DH, length), BF16),
        "vt": ((LH, DH, length), BF16),
        "kn": ((LH, length, DH), BF16),
        "vn": ((LH, length, DH), BF16),
        "lse": ((LH, 1, length), F32),
        "att_t": ((LH, DH, length), BF16),
        "n2_t": ((width, length), BF16),
        "mixed_t": ((cols, length), BF16),
        "gg": ((length, cols), BF16),
        "gu": ((length, cols), BF16),
        "mid_own": ((tokens, width), F32),
        "inv_own": ((tokens, 128), F32),
        "dn_own": ((tokens, width), F32),
        "grad_mid": ((tokens, width), F32),
        "branch": ((NS, tokens, width), BF16),
        "grad_q": ((LH, DH, tokens), F32),
        "grad_k": ((LH, DH, length), F32),
        "grad_v": ((LH, DH, length), F32),
        "down_near": ((ni - 1, wide) + down, BF16),
        "down_far": ((no - 1,) + down, BF16),
    }
    for key, last in (("gate", cols), ("up", cols), ("o", hd), ("f", WF)):
        scratch[key + "_near"] = ((ni - 1, no, rows, last), BF16)
        scratch[key + "_far"] = ((no - 1, rows, last), BF16)
    for key in ("dn", "res"):
        scratch[key + "_out"] = ((3, tokens, width), BF16)
        scratch[key + "_in"] = ((3, tokens, width), BF16)
    names = [*given, *outs, *scratch, "send_sems", "recv_sems"]
    got = pl.pallas_call(
        functools.partial(kernel, n, names),
        out_shape=[jax.ShapeDtypeStruct(*shape) for shape in outs.values()],
        in_specs=any_space(7) + vmem_space(2),
        out_specs=vmem_space(len(outs)),
        scratch_shapes=[pltpu.VMEM(*shape) for shape in scratch.values()] + sems(n),
        compiler_params=pltpu.CompilerParams(collective_id=1, has_side_effects=True, vmem_limit_bytes=VMEM_LIMIT),
    )(*given.values())
    return dict(zip(outs, got, strict=True))


def tables(length):
    positions = np.arange(length, dtype=np.float32)
    frequency = (BASE ** (-2.0 * np.arange(DH // 2, dtype=np.float32) / DH)).astype(np.float32)
    angles = frequency[:, None] * positions[None, :]
    return np.cos(angles).astype(np.float32), np.sin(angles).astype(np.float32)


def prepare(attn_gain, qh, qs, kh, ks, vh, vs, out_proj, ffn_gain, gate, up):
    s = lax.axis_index("seq")
    rows = qs.shape[0]
    cols = gate.shape[1] // NS
    first = ((NS - s) % NS) * cols
    wg = lax.dynamic_slice(gate, (0, first), (rows, cols))
    wu = lax.dynamic_slice(up, (0, first), (rows, cols))
    wo = lax.dynamic_slice(out_proj, (0, s * LH * DH), (rows, LH * DH))
    half = jnp.where(s % 2 == 0, qs[:, :NSH], jnp.concatenate([qs[:, NSH:], ks, vs], axis=1))
    own = [
        lax.dynamic_slice(w, (0, s * LH * r), (rows, LH * r)) for w, r in ((qh, RQ), (kh, RK), (vh, RK))
    ]
    rest = jnp.zeros((rows, WF - NSH - NH - 2), BF16)
    wf = jnp.concatenate([half, *own, attn_gain[:, None], ffn_gain[:, None], rest], axis=1)
    return wf, wo, wg, wu


def shards(tokens, attn_gain, qh, qs, kh, ks, vh, vs, out_proj, ffn_gain, gate, up, down, cotangent):
    n = lax.axis_size("fsdp")
    wf, wo, wg, wu = prepare(attn_gain, qh, qs, kh, ks, vh, vs, out_proj, ffn_gain, gate, up)
    cosine, sine = tables(tokens.shape[1] * NS)
    given = {
        "tok_in": tokens[0],
        "wf_in": wf,
        "wo_in": wo,
        "wg_in": wg,
        "wu_in": wu,
        "wd_in": down,
        "cot_in": cotangent[0],
        "cosine": cosine,
        "sine": sine,
    }
    got = run(n, given)
    wg_out, wu_out, wo_out, wf_out = (got[k] for k in ("wg_out", "wu_out", "wo_out", "wf_out"))
    rank_of = [(NS - b) % NS for b in range(NS)]
    gate_grad = jnp.concatenate([wg_out[r] for r in rank_of], axis=1).astype(F32)
    up_grad = jnp.concatenate([wu_out[r] for r in rank_of], axis=1).astype(F32)
    out_grad = jnp.concatenate([wo_out[r] for r in range(NS)], axis=1).astype(F32)
    f = wf_out.astype(F32)
    first = f[0, :, :NSH] + f[2, :, :NSH]
    last = f[1, :, :NSH] + f[3, :, :NSH]
    qs_grad = jnp.concatenate([first, last[:, :DH]], axis=1)
    ks_grad = last[:, DH : DH + RK * DH]
    vs_grad = last[:, DH + RK * DH :]
    at = NSH
    heads_grad = []
    for rank in (RQ, RK, RK):
        heads_grad.append(jnp.concatenate([f[r, :, at : at + LH * rank] for r in range(NS)], axis=1))
        at += LH * rank
    attn_gain_grad = jnp.sum(f[:, :, at], axis=0)
    ffn_gain_grad = jnp.sum(f[:, :, at + 1], axis=0)
    return (
        got["result"][None],
        got["input_grad"][None],
        attn_gain_grad,
        heads_grad[0],
        qs_grad,
        heads_grad[1],
        ks_grad,
        heads_grad[2],
        vs_grad,
        out_grad,
        ffn_gain_grad,
        gate_grad,
        up_grad,
        got["wd_out"].astype(F32),
    )


def solution(mesh):
    tokens = P("fsdp", "seq", None)
    matrix = P("fsdp", None)
    vector = P("fsdp")
    kinds = (vector,) + (matrix,) * 7 + (vector,) + (matrix,) * 3
    return jax.shard_map(
        shards,
        mesh=mesh,
        in_specs=(tokens,) + kinds + (tokens,),
        out_specs=(tokens, tokens) + kinds,
        check_vma=False,
    )
```

```python
import functools
import types

import jax
import jax.numpy as jnp
import numpy as np
from jax import lax
from jax.experimental import pallas as pl
from jax.experimental.pallas import tpu as pltpu
from jax.sharding import PartitionSpec as P

SEQ = "seq"
FSDP = "fsdp"
H = 16
DH = 64
RQ = 6
RK = 2
NS = 4
LH = H // NS
EPS = 1e-06
BASE = 10000.0
MASKED = -1e30
NSH = 320
NH = 40
WF = 384
F32 = jnp.float32
BF16 = jnp.bfloat16
VMEM_LIMIT = 62 << 20


def dot_nn(a, b):
    return lax.dot_general(a, b, (((1,), (0,)), ((), ())), preferred_element_type=F32)


def dot_nt(a, b):
    return lax.dot_general(a, b, (((1,), (1,)), ((), ())), preferred_element_type=F32)


def dot_tn(a, b):
    return lax.dot_general(a, b, (((0,), (0,)), ((), ())), preferred_element_type=F32)


class Net:
    def __init__(self, n, send_sems, recv_sems):
        self.n = n
        self.ni = 2 if n <= 8 else 4
        self.no = n // self.ni
        self.s = lax.axis_index(SEQ)
        self.f = lax.axis_index(FSDP)
        self.o = self.f // self.ni
        self.i = self.f % self.ni
        self.core = self.s % 2
        self.sib = self.s + 1 - 2 * self.core
        self.across = (self.s + 2) % 4
        self.diag = (self.sib + 2) % 4
        self.send_sems = send_sems
        self.recv_sems = recv_sems
        self.sends = 0
        self.recvs = 0
        self.open = []

    def at(self, o, i):
        return o * self.ni + i

    def outer(self, k):
        return (self.o + k) % self.no

    def inner(self, m):
        return (self.i + m) % self.ni

    def inside(self, step):
        return jnp.logical_and(self.o + step >= 0, self.o + step < self.no)

    def next_outer(self, way):
        return {FSDP: self.at((self.o + way + self.no) % self.no, self.i)}

    def take(self, count):
        first = self.recvs
        self.recvs += count
        return first

    def barrier(self):
        sem = pltpu.get_barrier_semaphore()
        peers = [{SEQ: self.sib}, {SEQ: self.across}]
        peers += [{FSDP: self.at(self.outer(k), self.i)} for k in range(1, self.no)]
        peers += [{FSDP: self.at(self.o, self.inner(m))} for m in range(1, self.ni)]
        for peer in peers:
            pl.semaphore_signal(sem, inc=1, device_id=peer, device_id_type=pl.DeviceIdType.MESH)
        pl.semaphore_wait(sem, len(peers))

    def send(self, src, dst, slot, device, when=None):
        copy = pltpu.make_async_remote_copy(
            src_ref=src,
            dst_ref=dst,
            send_sem=self.send_sems.at[self.sends],
            recv_sem=self.recv_sems.at[slot],
            device_id=device,
            device_id_type=pl.DeviceIdType.MESH,
        )
        self.sends += 1
        if when is None:
            copy.start()
        else:
            pl.when(when)(copy.start)
        self.open.append((copy, when))

    def local(self, src, dst):
        copy = pltpu.make_async_copy(src, dst, self.send_sems.at[self.sends])
        self.sends += 1
        copy.start()
        return copy

    def arrived(self, dst, slot):
        pltpu.make_async_remote_copy(
            src_ref=dst,
            dst_ref=dst,
            send_sem=self.send_sems.at[0],
            recv_sem=self.recv_sems.at[slot],
            device_id={SEQ: self.sib},
            device_id_type=pl.DeviceIdType.MESH,
        ).wait_recv()

    def taken(self):
        copies, self.open = self.open, []
        return copies

    def settle(self, copies):
        for copy, when in copies:
            if when is None:
                copy.wait_send()
            else:
                pl.when(when)(copy.wait_send)


class Gather:
    def __init__(self, net, src, dst):
        self.net, self.src, self.dst = net, src, dst
        self.slot = net.take(net.n)

    def start(self):
        net = self.net
        own = self.dst.at[net.f]
        for m in range(1, net.ni):
            net.send(self.src, own, self.slot + net.f, {FSDP: net.at(net.o, net.inner(m))})
        for k in range(1, net.no):
            net.send(self.src, own, self.slot + net.f, {FSDP: net.at(net.outer(k), net.i)})
        self.own = net.local(self.src, own)

    def block(self, index):
        self.net.arrived(self.dst.at[index], self.slot + index)

    def forward(self, k, then=None):
        net = self.net
        index = net.at((net.o - k + net.no) % net.no, net.i)
        self.block(index)
        for m in range(1, net.ni):
            net.send(self.dst.at[index], self.dst.at[index], self.slot + index, {FSDP: net.at(net.o, net.inner(m))})
        if then is not None:
            then(index)

    def finish(self, then=None):
        net = self.net
        for k in range(net.no):
            for m in range(1, net.ni):
                index = net.at((net.o - k + net.no) % net.no, net.inner(m))
                self.block(index)
                if then is not None:
                    then(index)
        self.own.wait()


class Line:
    def __init__(self, net, src, dst):
        self.net, self.src, self.dst = net, src, dst
        self.slot = net.take(net.n)

    def start(self):
        net = self.net
        own = self.dst.at[net.f]
        for way in (1, -1):
            net.send(self.src, own, self.slot + net.f, net.next_outer(way), net.inside(way))
        self.own = net.local(self.src, own)

    def start_inner(self):
        net = self.net
        own = self.dst.at[net.f]
        for m in range(1, net.ni):
            net.send(self.src, own, self.slot + net.f, {FSDP: net.at(net.o, net.inner(m))})

    def hop(self, h):
        net = self.net
        for way in (1, -1):
            here = net.inside(-way * h)
            index = net.at((net.o - way * h + net.no) % net.no, net.i)
            block = self.dst.at[index]
            slot = self.slot + index
            pl.when(here)(lambda block=block, slot=slot: net.arrived(block, slot))
            if h < net.no - 1:
                net.send(block, block, slot, net.next_outer(way), jnp.logical_and(here, net.inside(way)))
            for m in range(1, net.ni):
                net.send(block, block, slot, {FSDP: net.at(net.o, net.inner(m))}, here)

    def finish(self):
        net = self.net
        for o in range(net.no):
            for m in range(1, net.ni):
                index = net.at(o, net.inner(m))
                net.arrived(self.dst.at[index], self.slot + index)
        self.own.wait()


class Spread:
    def __init__(self, net, src, dst, group):
        self.net, self.src, self.dst = net, src, dst
        self.wide = net.no // NS
        self.first = group * self.wide
        self.slot = net.take(net.n // NS)
        self.mine = jnp.logical_and(net.o >= self.first, net.o < self.first + self.wide)

    def along(self, index, when, way):
        net = self.net
        block = self.dst.at[index]
        net.send(block, block, self.slot + index, net.next_outer(way), jnp.logical_and(when, net.inside(way)))

    def start(self):
        net = self.net
        group = jnp.where(self.mine, net.o - self.first, 0)
        index = group * net.ni + net.i
        own = self.dst.at[index]
        for m in range(1, net.ni):
            net.send(self.src, own, self.slot + index, {FSDP: net.at(net.o, net.inner(m))}, self.mine)
        for way in (1, -1):
            when = jnp.logical_and(self.mine, net.inside(way))
            net.send(self.src, own, self.slot + index, net.next_outer(way), when)
        self.own = pltpu.make_async_copy(self.src, own, net.send_sems.at[net.sends])
        net.sends += 1
        pl.when(self.mine)(self.own.start)

    def second(self):
        net = self.net
        group = jnp.where(self.mine, net.o - self.first, 0)
        for m in range(1, net.ni):
            index = group * net.ni + net.inner(m)
            pl.when(self.mine)(lambda index=index: net.arrived(self.dst.at[index], self.slot + index))
            for way in (1, -1):
                self.along(index, self.mine, way)

    def hop(self, h):
        net = self.net
        for g in range(self.wide):
            for way in (1, -1):
                here = net.o - (self.first + g) == way * h
                for m in range(net.ni):
                    index = g * net.ni + net.inner(m)
                    pl.when(here)(lambda index=index: net.arrived(self.dst.at[index], self.slot + index))
                    if h < net.no - 1:
                        self.along(index, here, way)

    def finish(self):
        pl.when(self.mine)(self.own.wait)


class Share:
    def __init__(self, net, dst):
        self.net, self.dst = net, dst
        self.slot = net.take(NS)

    def start(self, src):
        net = self.net
        own = self.dst(net.s)
        net.send(src, own, self.slot + net.s, {SEQ: net.across})
        net.send(src, own, self.slot + net.s, {SEQ: net.sib})

    def forward(self):
        net = self.net
        far = self.dst(net.across)
        net.arrived(far, self.slot + net.across)
        net.send(far, far, self.slot + net.across, {SEQ: net.sib})

    def near(self):
        net = self.net
        net.arrived(self.dst(net.sib), self.slot + net.sib)

    def last(self):
        net = self.net
        net.arrived(self.dst(net.diag), self.slot + net.diag)


class Fold:
    def __init__(self, net, out, into):
        self.net, self.out, self.into = net, out, into
        self.slot = net.take(3)

    def to_diag(self, value):
        net = self.net
        self.out[0] = value.astype(BF16)
        net.send(self.out.at[0], self.into.at[0], self.slot, {SEQ: net.sib})

    def to_across(self, value):
        net = self.net
        net.arrived(self.into.at[0], self.slot)
        self.out[1] = (value + self.into[0].astype(F32)).astype(BF16)
        net.send(self.out.at[1], self.into.at[2], self.slot + 2, {SEQ: net.across})

    def to_sibling(self, value):
        net = self.net
        self.out[2] = value.astype(BF16)
        net.send(self.out.at[2], self.into.at[1], self.slot + 1, {SEQ: net.sib})

    def total(self, value):
        net = self.net
        net.arrived(self.into.at[1], self.slot + 1)
        net.arrived(self.into.at[2], self.slot + 2)
        return value + self.into[1].astype(F32) + self.into[2].astype(F32)


class Reduce:
    def __init__(self, net, src, near, far):
        self.net, self.src, self.near, self.far = net, src, near, far
        self.slot_near = net.take((net.ni - 1) * net.no)
        self.slot_far = net.take(net.no - 1)

    def start(self):
        net = self.net
        for k in [*range(1, net.no), 0]:
            o = net.outer(k)
            for m in range(1, net.ni):
                net.send(
                    self.src.at[net.at(o, net.inner(m))],
                    self.near.at[m - 1, o],
                    self.slot_near + (m - 1) * net.no + o,
                    {FSDP: net.at(net.o, net.inner(m))},
                )

    def column(self, o):
        net = self.net
        value = self.src[net.at(o, net.i)].astype(F32)
        for m in range(1, net.ni):
            net.arrived(self.near.at[m - 1, o], self.slot_near + (m - 1) * net.no + o)
            value = value + self.near[m - 1, o].astype(F32)
        return value

    def forward(self, k):
        net = self.net
        o = net.outer(k)
        index = net.at(o, net.i)
        self.src[index] = self.column(o).astype(BF16)
        net.send(self.src.at[index], self.far.at[k - 1], self.slot_far + k - 1, {FSDP: net.at(o, net.i)})

    def finish(self):
        net = self.net
        value = self.column(net.o)
        for k in range(1, net.no):
            net.arrived(self.far.at[k - 1], self.slot_far + k - 1)
            value = value + self.far[k - 1].astype(F32)
        return value


class Collect:
    def __init__(self, net, src, near, far, group, into):
        self.net, self.src, self.near, self.far, self.into = net, src, near, far, into
        self.wide = net.no // NS
        self.first = group * self.wide
        self.mine = jnp.logical_and(net.o >= self.first, net.o < self.first + self.wide)
        self.slot_near = net.take((net.ni - 1) * self.wide)
        self.slot_far = net.take(net.no - 1)
        self.slot_into = net.take(1)
        self.owner = (NS - net.o // self.wide) % NS

    def start(self):
        net = self.net
        for g in range(self.wide):
            for m in range(1, net.ni):
                net.send(
                    self.src.at[g * net.ni + net.inner(m)],
                    self.near.at[m - 1, g],
                    self.slot_near + (m - 1) * self.wide + g,
                    {FSDP: net.at(net.o, net.inner(m))},
                )

    def forward(self):
        net = self.net
        for g in range(self.wide):
            index = g * net.ni + net.i
            value = self.src[index].astype(F32)
            for m in range(1, net.ni):
                net.arrived(self.near.at[m - 1, g], self.slot_near + (m - 1) * self.wide + g)
                value = value + self.near[m - 1, g].astype(F32)
            self.src[index] = value.astype(BF16)
            o = self.first + g
            step = (o - net.o + net.no) % net.no
            away = step > 0
            place = jnp.where(away, step - 1, 0)
            net.send(self.src.at[index], self.far.at[place], self.slot_far + place, {FSDP: net.at(o, net.i)}, away)

    def finish(self):
        net = self.net

        @pl.when(self.mine)
        def _():
            value = self.src[jnp.where(self.mine, net.f - self.first * net.ni, 0)].astype(F32)
            for k in range(1, net.no):
                net.arrived(self.far.at[k - 1], self.slot_far + k - 1)
                value = value + self.far[k - 1].astype(F32)
            self.into[...] = value.astype(BF16)

        net.send(self.into, self.into, self.slot_into, {SEQ: net.across}, self.mine)
        net.send(self.into, self.into, self.slot_into, {SEQ: net.sib}, self.mine)

    def forward_into(self):
        net = self.net
        other = net.s != self.owner
        pl.when(other)(lambda: net.arrived(self.into, self.slot_into))
        net.send(self.into, self.into, self.slot_into, {SEQ: net.sib}, net.across == self.owner)


def matrix_of(ref):
    count, rows, cols = ref.shape
    if rows % 8 == 0:
        return ref[...].reshape(count * rows, cols)
    return jnp.concatenate([ref[index].astype(F32) for index in range(count)], axis=0).astype(BF16)


def kernel(n, names, *refs):
    r = types.SimpleNamespace(**dict(zip(names, refs, strict=True)))
    net = Net(n, r.send_sems, r.recv_sems)
    tok, cot, wo, wg, wu, wd, att = r.tok, r.cot, r.wo, r.wg, r.wu, r.wd, r.att
    wf, wft, gains, shared, heads = r.wf, r.wft, r.gains, r.shared, r.heads
    qt, kt, vt, kn, vn, lse, att_t = r.qt, r.kt, r.vt, r.kn, r.vn, r.lse, r.att_t
    cos_ref, sin_ref = r.cosine, r.sine
    tokens, width = tok.shape[1:]
    length = NS * tokens
    rows, cols = wg.shape[1:]
    group = (NS - net.s) % NS
    net.barrier()

    g_wf = Gather(net, r.wf_in, wf.at[net.core])
    s_tok = Share(net, lambda rank: tok.at[rank])
    slot_sib = net.take(n)

    def to_sibling(index):
        here = wf.at[net.core, index]
        net.send(here, here, slot_sib + index, {SEQ: net.sib})

    g_wf.start()
    net.send(r.wf_in, wf.at[net.core, net.f], slot_sib + net.f, {SEQ: net.sib})
    s_tok.start(r.tok_in)
    own_tok = net.local(r.tok_in, tok.at[net.s])
    g_wo = Gather(net, r.wo_in.at[:, pl.ds(pl.multiple_of(net.s * LH * DH, LH * DH), LH * DH)], wo.at[net.s])
    g_wd = Spread(net, r.wd_in, wd, group)
    g_wg = Line(net, r.wg_in, wg)
    g_wu = Line(net, r.wu_in, wu)
    s_cot = Share(net, lambda rank: cot.at[rank])
    s_cot.start(r.cot_in)
    own_cot = net.local(r.cot_in, cot.at[net.s])
    g_wd.start()
    for k in range(1, net.no):
        g_wf.forward(k, to_sibling)
    g_wo.start()
    g_wg.start()
    g_wu.start_inner()
    g_wf.finish(to_sibling)
    s_tok.forward()
    for index in range(n):
        net.arrived(wf.at[1 - net.core, index], slot_sib + index)

    for half in range(2):
        whole = wf[half].reshape(n * rows, WF).astype(F32).T
        wft[half] = whole.astype(BF16)
        if half == 0:
            gains[...] = whole[NSH + NH : NSH + NH + 8, :]
    own_tok.wait()
    s_tok.near()
    s_tok.last()
    g_wu.start()
    g_wg.start_inner()

    s_att = [Share(net, lambda rank, j=j: att.at[rank, pl.ds(tokens * j, tokens)]) for j in range(NS)]
    s_wo = Share(net, lambda rank: wo.at[rank])

    def rounded(v):
        return v.astype(BF16).astype(F32)

    for j in range(NS):
        here = slice(tokens * j, tokens * (j + 1))
        upto = tokens * j
        values = tok[j].astype(F32)
        inv = lax.rsqrt(jnp.mean(values * values, axis=-1, keepdims=True) + EPS)
        block = (values * inv * gains[0:1, :]).astype(BF16)
        parts = [dot_nt(wft[half], block) for half in range(2)]
        own = dot_nt(wft[net.core, NSH:, :], block)
        cosine, sine = cos_ref[:, here], sin_ref[:, here]

        def turned(piece):
            first, second = piece[: DH // 2], piece[DH // 2 :]
            return jnp.concatenate([first * cosine - second * sine, first * sine + second * cosine], axis=0)

        def piece(half, index):
            return parts[half][DH * index : DH * (index + 1)]

        sq = [rounded(turned(piece(0, p))) for p in range(5)] + [rounded(turned(piece(1, 0)))]
        sk = [rounded(turned(piece(1, 1 + p))) for p in range(RK)]
        sv = [rounded(piece(1, 3 + p)) for p in range(RK)]
        for index, part in enumerate(sq + sk + sv):
            shared[index // 5, DH * (index % 5) : DH * (index % 5 + 1), here] = part.astype(BF16)
        own = rounded(own[:NH])
        heads[:, here] = own
        for h in range(LH):
            q = sum(own[h * RQ + p : h * RQ + p + 1] * sq[p] for p in range(RQ)) * (1.0 / RQ)
            first = LH * RQ
            k = sum(own[first + h * RK + p : first + h * RK + p + 1] * sk[p] for p in range(RK)) * (1.0 / RK)
            first = LH * (RQ + RK)
            v = sum(own[first + h * RK + p : first + h * RK + p + 1] * sv[p] for p in range(RK)) * (1.0 / RK)
            qt[h, :, here] = (q.astype(BF16).astype(F32) * DH**-0.5).astype(BF16)
            kt[h, :, here] = k.astype(BF16)
            vt[h, :, here] = v.astype(BF16)
            kn[h, here, :] = rounded(k).T.astype(BF16)
            vn[h, here, :] = rounded(v).T.astype(BF16)

        def one_head(h, _):
            q = qt[h, :, here]
            keep = lax.broadcasted_iota(jnp.int32, (tokens, tokens), 0) <= lax.broadcasted_iota(
                jnp.int32, (tokens, tokens), 1
            )
            diagonal = jnp.where(keep, dot_nn(kn[h, here, :], q), MASKED)
            top = jnp.max(diagonal, axis=0, keepdims=True)
            if j > 0:
                below = dot_nn(kn[h, 0:upto, :], q)
                top = jnp.maximum(top, jnp.max(below, axis=0, keepdims=True))
            diagonal = jnp.exp(diagonal - top)
            total = jnp.sum(diagonal, axis=0, keepdims=True)
            if j > 0:
                below = jnp.exp(below - top)
                total = total + jnp.sum(below, axis=0, keepdims=True)
            inverse = 1.0 / total
            result = dot_nn(vt[h, :, here], (diagonal * inverse).astype(BF16))
            if j > 0:
                result = result + dot_nn(vt[h, :, 0:upto], (below * inverse).astype(BF16))
            lse[h, :, here] = top + jnp.log(total)
            att_t[h, :, here] = result
            return 0

        lax.fori_loop(0, LH, one_head, 0)
        turn = att_t[:, :, here].reshape(LH * DH, tokens).T
        att[net.s, here, :] = turn.astype(BF16)
        s_att[j].start(att.at[net.s, pl.ds(tokens * j, tokens)])
        if j == 0:
            for k in range(1, net.no):
                g_wo.forward(k)
            g_wd.second()
        if j == 1:
            g_wg.hop(1)
            s_cot.forward()
        if j == 2:
            g_wd.hop(1)
            g_wo.finish()
            s_wo.start(wo.at[net.s])
            g_wg.hop(2)
            g_wu.hop(1)
    g_wd.hop(2)
    for h in range(3, net.no):
        g_wg.hop(h)
    for share in s_att[:-1]:
        share.forward()
    g_wu.hop(2)
    s_wo.forward()
    s_att[-1].forward()
    for h in range(3, net.no):
        g_wu.hop(h)
    for share in [*s_att, s_wo]:
        share.near()
        share.last()

    gain = gains[1:2, :]
    f_dn = Fold(net, r.dn_out, r.dn_in)
    f_res = Fold(net, r.res_out, r.res_in)
    order = (net.diag, net.across, net.sib, net.s)
    n2_t, mixed_t, gg_all, gu_all = r.n2_t, r.mixed_t, r.gg, r.gu
    mid_own, inv_own, dn_own, branch = r.mid_own, r.inv_own, r.grad_mid, r.branch
    result = r.result

    for step, b in enumerate(order):
        here = slice(tokens * step, tokens * (step + 1))
        span = pl.ds(pl.multiple_of(b * tokens, tokens), tokens)
        middle = tok[b].astype(F32)
        for rank in range(NS):
            middle = middle + dot_nt(att[rank, span, :], wo[rank].reshape(width, LH * DH))
        inv = lax.rsqrt(jnp.mean(middle * middle, axis=-1, keepdims=True) + EPS)
        normal = middle * inv
        block = (normal * gain).astype(BF16)
        n2_t[:, here] = block.astype(F32).T.astype(BF16)
        if step == 3:
            mid_own[...] = middle
            inv_own[...] = jnp.broadcast_to(inv, inv_own.shape)
        if step == 0:
            g_wg.finish()
        wg_all = matrix_of(wg)
        gate = dot_nn(block, wg_all)
        if step == 0:
            for h in range(3, net.no):
                g_wd.hop(h)
            g_wu.finish()
        wu_all = matrix_of(wu)
        up = dot_nn(block, wu_all)
        sg = jax.nn.sigmoid(gate)
        act = gate * sg
        mixed = (act * up).astype(BF16)
        mixed_t[:, here] = mixed.astype(F32).T.astype(BF16)
        if step == 0:
            g_wd.finish()
            s_cot.near()
            s_cot.last()
            own_cot.wait()
            opening = net.taken()
        wd_all = matrix_of(wd)
        grad_mixed = dot_nt(cot[b], wd_all)
        gg = (grad_mixed * up * sg * (1.0 + gate * (1.0 - sg))).astype(BF16)
        gu = (grad_mixed * act).astype(BF16)
        gg_all[here, :] = gg
        gu_all[here, :] = gu
        dn = dot_nt(gg, wg_all) + dot_nt(gu, wu_all)
        if step == 0:
            f_dn.to_diag(dn)
        elif step == 1:
            f_dn.to_across(dn)
        elif step == 2:
            f_dn.to_sibling(dn)
        else:
            dn_own[...] = dn
        part = dot_nn(mixed, wd_all)
        if step == 0:
            f_res.to_diag(part)
        elif step == 1:
            f_res.out[1] = part.astype(BF16)
        elif step == 2:
            f_res.to_sibling(part)
        else:
            result[...] = part.astype(BF16)

    folded = net.taken()
    net.settle(opening)
    wg_grad, wu_grad, wd_grad = wg, wu, wd
    r_down = Collect(net, wd_grad, r.down_near, r.down_far, group, r.wd_out)
    r_gate = Reduce(net, wg_grad, r.gate_near, r.gate_far)
    r_up = Reduce(net, wu_grad, r.up_near, r.up_far)

    grad_mid = r.grad_mid
    s_branch = Share(net, lambda rank: branch.at[rank])
    kept = types.SimpleNamespace()
    wo_t = wo[net.s].reshape(width, LH * DH).astype(F32).T.astype(BF16)

    grad_att, grad_q, grad_k, grad_v = r.vt, r.grad_q, r.grad_k, r.grad_v
    factors = n2_t
    wo_grad, wf_grad = wo.at[net.diag], wf.at[0]
    r_o = Reduce(net, wo_grad, r.o_near, r.o_far)
    below = lax.broadcasted_iota(jnp.int32, (tokens, tokens), 0) <= lax.broadcasted_iota(
        jnp.int32, (tokens, tokens), 1
    )

    def span_of(block):
        return pl.ds(pl.multiple_of(block * tokens, tokens), tokens)

    def back_factors(grads, rank, base, first_piece, turn, span):
        cosine, sine = cos_ref[:, span], sin_ref[:, span]
        own = heads[:, span]
        found = {}
        for p in range(rank):
            index = first_piece + p
            part = shared[index // 5, DH * (index % 5) : DH * (index % 5 + 1), span].astype(F32)
            rot = sum(own[base + h * rank + p : base + h * rank + p + 1] * grads[h] for h in range(LH)) * (1.0 / rank)
            if turn:
                first, second = rot[: DH // 2], rot[DH // 2 :]
                rot = jnp.concatenate([first * cosine + second * sine, second * cosine - first * sine], axis=0)
            first_row = WF * (index // 5) + DH * (index % 5)
            factors[first_row : first_row + DH, span] = rot.astype(BF16)
            for h in range(LH):
                found[h * rank + p] = jnp.sum(part * grads[h], axis=0, keepdims=True) * (1.0 / rank)
        head_grads[base : base + LH * rank, span] = jnp.concatenate([found[k] for k in range(LH * rank)], axis=0)

    head_grads = r.head_grads

    def attend_back(b):
        span = span_of(b)
        grad_att[:, :, span] = dot_nt(wo_t, branch[b]).astype(BF16).reshape(LH, DH, tokens)
        for h in range(LH):
            delta_all[h, :, :] = jnp.sum(
                grad_att[h, :, span].astype(F32) * att_t[h, :, span], axis=0, keepdims=True
            )

        def tile(k, diagonal):
            keys = span_of(k)
            for h in range(LH):
                q = qt[h, :, span]
                da = grad_att[h, :, span]
                scores = dot_nn(kn[h, keys, :], q)
                if diagonal:
                    scores = jnp.where(below, scores, MASKED)
                probs = jnp.exp(scores - lse[h, :, span])
                ds = (probs * (dot_nn(vn[h, keys, :], da) - delta_all[h])).astype(BF16)
                gq = dot_nn(kt[h, :, keys], ds)
                if diagonal:
                    grad_q[h] = gq
                else:
                    grad_q[h] += gq
                grad_k[h, :, keys] += dot_nt(q, ds)
                grad_v[h, :, keys] += dot_nt(da, probs.astype(BF16))

        tile(b, True)
        lax.fori_loop(0, b, lambda k, _: (tile(k, False), 0)[1], 0)
        back_factors([grad_q[h] * DH**-0.5 for h in range(LH)], RQ, 0, 0, True, span)

    delta_all = r.delta
    r_f = Reduce(net, wf_grad, r.f_near, r.f_far)
    f_gn = Fold(net, r.dn_out, r.dn_in)
    def map_grad(half):
        return sum(
            dot_nn(factors[pl.ds(pl.multiple_of(half * WF, WF), WF), tokens * b : tokens * (b + 1)], cot[b])
            for b in range(NS)
        )

    def gain_part(half, value):
        return jnp.sum(wft[half].astype(F32) * value, axis=0, keepdims=True)

    def normed_grad(b):
        columns = pl.ds(pl.multiple_of(b * tokens, tokens), tokens)
        return sum(
            dot_nn(factors[WF * half : WF * (half + 1), columns].astype(F32).T.astype(BF16), wft[half])
            for half in range(2)
        )

    def down_grad():
        wd_rows = wd_grad.shape[1]
        down = sum(dot_nn(mixed_t[:, tokens * k : tokens * (k + 1)], cot[b]) for k, b in enumerate(order))
        for index in range(wd_grad.shape[0]):
            wd_grad[index] = down[wd_rows * index : wd_rows * (index + 1)].astype(BF16)
        r_down.start()

    def gate_grad():
        wg_grad[...] = dot_nn(n2_t[...], gg_all[...]).astype(BF16).reshape(wg_grad.shape)
        r_gate.start()

    def up_grad():
        wu_grad[...] = dot_nn(n2_t[...], gu_all[...]).astype(BF16).reshape(wu_grad.shape)
        r_up.start()

    def mid_grads():
        total = f_dn.total(dn_own[...])
        inv = inv_own[:, 0:1]
        normal = mid_own[...] * inv
        scaled = total * gain
        mid_grad = cot[net.s].astype(F32) + inv * (scaled - normal * jnp.mean(scaled * normal, axis=-1, keepdims=True))
        grad_mid[...] = mid_grad
        kept.ffn_gain = jnp.sum(total * normal, axis=0, keepdims=True)
        branch[net.s] = mid_grad.astype(BF16)
        s_branch.start(branch.at[net.s])

    def norm_again():
        for b in range(NS):
            x = tok[b].astype(F32)
            scale = lax.rsqrt(jnp.mean(x * x, axis=-1, keepdims=True) + EPS)
            cot[b] = (x * scale * gains[0:1, :]).astype(BF16)
        grad_k[...] = jnp.zeros_like(grad_k)
        grad_v[...] = jnp.zeros_like(grad_v)
        factors[: 2 * WF, :] = jnp.zeros((2 * WF, length), BF16)

    def attend(b):
        return lambda: attend_back(b)

    def res_across():
        f_res.to_across(f_res.out[1].astype(F32))

    def res_total():
        result[...] = (mid_own[...] + f_res.total(result[...].astype(F32))).astype(BF16)

    def key_value_factors():
        for b in range(NS):
            here = slice(tokens * b, tokens * (b + 1))
            back_factors([grad_k[h, :, here] for h in range(LH)], RK, LH * RQ, RQ, True, here)
            back_factors([grad_v[h, :, here] for h in range(LH)], RK, LH * (RQ + RK), RQ + RK, False, here)
        rest = jnp.zeros((WF - NSH - NH, length), F32)
        factors[pl.ds(pl.multiple_of(net.core * WF + NSH, DH), WF - NSH), :] = jnp.concatenate(
            [head_grads[...], rest], axis=0
        ).astype(BF16)

    def out_grad():
        out_t = sum(
            dot_nn(att_t[:, :, tokens * b : tokens * (b + 1)].reshape(LH * DH, tokens).astype(BF16), branch[b]) for b in range(NS)
        )
        wo_grad[...] = out_t.T.astype(BF16).reshape(n, rows, LH * DH)
        r_o.start()

    def map_grads():
        slot_map = net.take(1)
        other = map_grad(1 - net.core)
        away = (n2_t.at[pl.ds(2 * WF, tokens)], mixed_t.at[pl.ds(WF, WF - tokens)])
        near = (mixed_t.at[pl.ds(0, tokens)], mixed_t.at[pl.ds(tokens, WF - tokens)])
        away[0][...] = other[:tokens].astype(BF16)
        away[1][...] = other[tokens:].astype(BF16)
        slot_more = net.take(1)
        net.send(away[0], near[0], slot_map, {SEQ: net.sib})
        net.send(away[1], near[1], slot_more, {SEQ: net.sib})
        mine = map_grad(net.core)
        attn_gain = (gain_part(net.core, mine) + gain_part(1 - net.core, other)) / gains[0:1, :]
        net.arrived(near[0], slot_map)
        net.arrived(near[1], slot_more)
        mine = mine + mixed_t[:WF].astype(F32)
        mine = jnp.concatenate([mine[: NSH + NH], attn_gain, kept.ffn_gain, mine[NSH + NH + 2 :]], axis=0)
        wf_grad[...] = mine.T.astype(BF16).reshape(n, rows, WF)
        r_f.start()

    def fold_grad(step):
        def act():
            if step == 0:
                net.settle(folded)
                f_gn.to_diag(normed_grad(net.diag))
            elif step == 1:
                f_gn.to_across(normed_grad(net.across))
            elif step == 2:
                f_gn.to_sibling(normed_grad(net.sib))
            else:
                kept.own_grad = normed_grad(net.s)

        return act

    def fold_total():
        total = f_gn.total(kept.own_grad)
        x = tok[net.s].astype(F32)
        scale = lax.rsqrt(jnp.mean(x * x, axis=-1, keepdims=True) + EPS)
        normal = x * scale
        scaled = total * gains[0:1, :]
        r.input_grad[...] = (
            grad_mid[...] + scale * (scaled - normal * jnp.mean(scaled * normal, axis=-1, keepdims=True))
        ).astype(BF16)

    def on(reduce, *places):
        def act():
            for k in range(1, net.no):
                if min(k, 3) in places:
                    reduce.forward(k)

        return act

    shares = {}

    def share_out(reduce, out):
        def act():
            out[net.s] = reduce.finish().astype(BF16)
            shares[reduce] = Share(net, lambda rank: out.at[rank])
            shares[reduce].start(out.at[net.s])

        return act

    def pass_on(reduce):
        return lambda: shares[reduce].forward()

    steps = [
        gate_grad,
        mid_grads,
        up_grad,
        on(r_gate, 1),
        down_grad,
        norm_again,
        res_across,
        attend(net.s),
        s_branch.near,
        on(r_gate, 2),
        attend(net.sib),
        s_branch.forward,
        attend(net.across),
        s_branch.last,
        on(r_gate, 3),
        attend(net.diag),
        on(r_up, 1),
        res_total,
        key_value_factors,
        out_grad,
        map_grads,
        on(r_up, 2),
        on(r_up, 3),
        fold_grad(0),
        fold_grad(1),
        r_down.forward,
        share_out(r_gate, r.wg_out),
        fold_grad(2),
        fold_grad(3),
        on(r_o, 1),
        share_out(r_up, r.wu_out),
        on(r_o, 2),
        on(r_o, 3),
        fold_total,
        r_down.finish,
        on(r_f, 1),
        on(r_f, 2),
        share_out(r_o, r.wo_out),
        on(r_f, 3),
        share_out(r_f, r.wf_out),
        pass_on(r_gate),
        pass_on(r_up),
        pass_on(r_o),
        pass_on(r_f),
        r_down.forward_into,
    ]
    for step in steps:
        step()
    for share in shares.values():
        share.near()
        share.last()
    net.settle(net.taken())


def sems(n):
    return [pltpu.SemaphoreType.DMA((10 * n + 80,))] * 2


def any_space(count):
    return [pl.BlockSpec(memory_space=pl.ANY)] * count


def vmem_space(count):
    return [pl.BlockSpec(memory_space=pltpu.VMEM)] * count


def run(n, given):
    r = types.SimpleNamespace(**given)
    tokens, width = r.tok_in.shape
    length = tokens * NS
    rows, cols = r.wg_in.shape
    down = r.wd_in.shape
    hd = LH * DH
    ni = 2 if n <= 8 else 4
    no = n // ni
    wide = no // NS
    outs = dict(
        result=((tokens, width), BF16),
        input_grad=((tokens, width), BF16),
        wg_out=((NS, rows, cols), BF16),
        wu_out=((NS, rows, cols), BF16),
        wd_out=(down, BF16),
        wo_out=((NS, rows, hd), BF16),
        wf_out=((NS, rows, WF), BF16),
    )
    scratch = dict(
        tok=((NS, tokens, width), BF16),
        cot=((NS, tokens, width), BF16),
        wo=((NS, n, rows, hd), BF16),
        wg=((n, rows, cols), BF16),
        wu=((n, rows, cols), BF16),
        wd=((n // NS,) + down, BF16),
        att=((NS, length, hd), BF16),
        wf=((2, n, rows, WF), BF16),
        wft=((2, WF, width), BF16),
        gains=((8, width), F32),
        shared=((2, NSH, length), BF16),
        heads=((NH, length), F32),
        qt=((LH, DH, length), BF16),
        kt=((LH, DH, length), BF16),
        vt=((LH, DH, length), BF16),
        kn=((LH, length, DH), BF16),
        vn=((LH, length, DH), BF16),
        lse=((LH, 1, length), F32),
        att_t=((LH, DH, length), F32),
        n2_t=((width, length), BF16),
        mixed_t=((cols, length), BF16),
        gg=((length, cols), BF16),
        gu=((length, cols), BF16),
        mid_own=((tokens, width), F32),
        inv_own=((tokens, 128), F32),
        grad_mid=((tokens, width), F32),
        branch=((NS, tokens, width), BF16),
        grad_q=((LH, DH, tokens), F32),
        delta=((LH, 1, tokens), F32),
        head_grads=((NH, length), F32),
        grad_k=((LH, DH, length), F32),
        grad_v=((LH, DH, length), F32),
        down_near=((ni - 1, wide) + down, BF16),
        down_far=((no - 1,) + down, BF16),
    )
    near, far = [
        [(lead + (rows, last), BF16) for last in (cols, hd, WF)] for lead in ((ni - 1, no), (no - 1,))
    ]
    three = ((3, tokens, width), BF16)
    scratch.update(
        gate_near=near[0],
        gate_far=far[0],
        up_near=near[0],
        up_far=far[0],
        o_near=near[1],
        o_far=far[1],
        f_near=near[2],
        f_far=far[2],
        dn_out=three,
        dn_in=three,
        res_out=three,
        res_in=three,
    )
    names = [*given, *outs, *scratch, *dict(send_sems=0, recv_sems=0)]
    got = pl.pallas_call(
        functools.partial(kernel, n, names),
        out_shape=[jax.ShapeDtypeStruct(*shape) for shape in outs.values()],
        in_specs=any_space(7) + vmem_space(2),
        out_specs=vmem_space(len(outs)),
        scratch_shapes=[pltpu.VMEM(*shape) for shape in scratch.values()] + sems(n),
        compiler_params=pltpu.CompilerParams(collective_id=1, has_side_effects=True, vmem_limit_bytes=VMEM_LIMIT),
    )(*given.values())
    return dict(zip(outs, got, strict=True))


def tables(length):
    positions = np.arange(length, dtype=np.float32)
    frequency = (BASE ** (-2.0 * np.arange(DH // 2, dtype=np.float32) / DH)).astype(np.float32)
    angles = frequency[:, None] * positions[None, :]
    return np.cos(angles).astype(np.float32), np.sin(angles).astype(np.float32)


def slice_kernel(attn_gain, qh, qs, kh, ks, vh, vs, ffn_gain, gate, up, wf, wg, wu, windows, sem):
    s = lax.axis_index(SEQ)
    rows, cols = wg.shape
    group = (NS - s) % NS
    first = group * cols
    start = pl.multiple_of(first // 128 * 128, 128)
    wide = windows.shape[2]
    copies = []
    for index, ref in enumerate((gate, up)):
        copies.append(pltpu.make_async_copy(ref.at[:, pl.ds(start, wide)], windows.at[index], sem.at[index]))
        copies[-1].start()

    all_qs = qs[...].astype(F32)
    both = jnp.concatenate([all_qs[:, 256:], ks[...].astype(F32), vs[...].astype(F32)], axis=1)
    both = pltpu.roll(both, WF - (NSH - 256), 1)
    value = jnp.where(s % 2 == 0, all_qs, both)
    lane = lax.broadcasted_iota(jnp.int32, (rows, WF), 1)
    value = jnp.where(lane < NSH, value, 0.0)
    at = NSH
    for ref, rank in ((qh, RQ), (kh, RK), (vh, RK)):
        count = LH * rank
        place = lax.broadcasted_iota(jnp.int32, (ref.shape[0], WF), 1) - at
        source = lax.broadcasted_iota(jnp.int32, (ref.shape[0], WF), 0) - s * count
        pick = jnp.logical_and(place == source, jnp.logical_and(place >= 0, place < count))
        value = value + dot_tn(ref[...], jnp.where(pick, 1.0, 0.0).astype(BF16))
        at += count
    eye = lax.broadcasted_iota(jnp.int32, (rows, rows), 0) == lax.broadcasted_iota(jnp.int32, (rows, rows), 1)
    for index, ref in enumerate((attn_gain, ffn_gain)):
        column = jnp.sum(jnp.where(eye, ref[...].astype(F32).reshape(1, rows), 0.0), axis=1, keepdims=True)
        value = jnp.where(lane == at + index, column, value)
    wf[...] = value.astype(BF16)

    for index, out in enumerate((wg, wu)):
        copies[index].wait()

        @pl.when(first == start)
        def _():
            out[...] = windows[index, :, :cols]

        @pl.when(first != start)
        def _():
            moved = pltpu.roll(windows[index].astype(F32), wide - 64, 1)
            out[...] = moved[:, :cols].astype(BF16)


def run_slices(attn_gain, qh, qs, kh, ks, vh, vs, ffn_gain, gate, up):
    rows = qs.shape[0]
    cols = gate.shape[1] // NS
    wide = -(-cols // 128) * 128
    shapes = [(rows, WF), (rows, cols), (rows, cols)]
    return pl.pallas_call(
        slice_kernel,
        out_shape=[jax.ShapeDtypeStruct(shape, BF16) for shape in shapes],
        in_specs=vmem_space(8) + any_space(2),
        out_specs=vmem_space(3),
        scratch_shapes=[pltpu.VMEM((2, rows, wide), BF16), pltpu.SemaphoreType.DMA((2,))],
    )(attn_gain, qh.T, qs, kh.T, ks, vh.T, vs, ffn_gain, gate, up)


def finish_kernel(names, *refs):
    r = types.SimpleNamespace(**dict(zip(names, refs, strict=True)))
    r.result_out[...] = r.result[...]
    r.input_out[...] = r.input_grad[...]
    cols = r.wg_out.shape[2]
    for blocks, out in ((r.wg_out, r.wg_grad), (r.wu_out, r.wu_grad)):
        out[...] = jnp.concatenate([blocks[(NS - b) % NS].astype(F32) for b in range(NS)], axis=1)
    hd = LH * DH
    for rank in range(NS):
        r.wo_grad[:, hd * rank : hd * (rank + 1)] = r.wo_out[rank].astype(F32)
    r.wd_grad[...] = r.wd_out[...].astype(F32)
    f = [r.wf_out[rank].astype(F32) for rank in range(NS)]
    low = f[0] + f[2]
    high = f[1] + f[3]
    lane = lax.broadcasted_iota(jnp.int32, low.shape, 1)
    r.qs_grad[:, :256] = low[:, :256]
    moved = pltpu.roll(high, NSH, 1)
    r.qs_grad[:, 256:] = jnp.where(lane[:, 256:] < NSH, low[:, 256:], moved[:, 256:])
    shifted = pltpu.roll(high, WF - DH, 1)
    r.ks_grad[...] = shifted[:, :128]
    r.vs_grad[...] = shifted[:, 128:256]
    at = NSH
    for out, rank in ((r.qh_grad, RQ), (r.kh_grad, RK), (r.vh_grad, RK)):
        count = LH * rank
        place = lax.broadcasted_iota(jnp.int32, (NS * count, WF), 1) - at
        target = lax.broadcasted_iota(jnp.int32, (NS * count, WF), 0)
        total = 0.0
        for s in range(NS):
            pick = jnp.logical_and(target - s * count == place, jnp.logical_and(place >= 0, place < count))
            total = total + dot_nt(jnp.where(pick, 1.0, 0.0).astype(BF16), r.wf_out[s])
        out[...] = total
        at += count
    whole = low + high
    rows = whole.shape[0]
    eye = lax.broadcasted_iota(jnp.int32, (rows, rows), 0) == lax.broadcasted_iota(jnp.int32, (rows, rows), 1)
    for index in range(2):
        column = jnp.sum(jnp.where(lane == at + index, whole, 0.0), axis=1, keepdims=True)
        (r.attn_gain_grad, r.ffn_gain_grad)[index][...] = jnp.sum(jnp.where(eye, column, 0.0), axis=0)


def run_finish(got):
    one = types.SimpleNamespace(**got)
    rows, cols = one.wg_out.shape[1:]
    outs = dict(
        result_out=(one.result.shape, BF16),
        input_out=(one.result.shape, BF16),
        wg_grad=((rows, NS * cols), F32),
        wu_grad=((rows, NS * cols), F32),
        wd_grad=(one.wd_out.shape, F32),
        wo_grad=((rows, H * DH), F32),
        qh_grad=((H * RQ, rows), F32),
        qs_grad=((rows, RQ * DH), F32),
        kh_grad=((H * RK, rows), F32),
        ks_grad=((rows, RK * DH), F32),
        vh_grad=((H * RK, rows), F32),
        vs_grad=((rows, RK * DH), F32),
        attn_gain_grad=((rows,), F32),
        ffn_gain_grad=((rows,), F32),
    )
    names = [*got, *outs]
    done = pl.pallas_call(
        functools.partial(finish_kernel, names),
        out_shape=[jax.ShapeDtypeStruct(*shape) for shape in outs.values()],
        in_specs=vmem_space(len(got)),
        out_specs=vmem_space(len(outs)),
    )(*got.values())
    return types.SimpleNamespace(**dict(zip(outs, done, strict=True)))


def shards(tokens, attn_gain, qh, qs, kh, ks, vh, vs, out_proj, ffn_gain, gate, up, down, cotangent):
    n = lax.axis_size(FSDP)
    wf, wg, wu = run_slices(attn_gain, qh, qs, kh, ks, vh, vs, ffn_gain, gate, up)
    cosine, sine = tables(tokens.shape[1] * NS)
    given = dict(
        tok_in=tokens[0],
        wf_in=wf,
        wo_in=out_proj,
        wg_in=wg,
        wu_in=wu,
        wd_in=down,
        cot_in=cotangent[0],
        cosine=cosine,
        sine=sine,
    )
    done = run_finish(run(n, given))
    return (
        done.result_out[None],
        done.input_out[None],
        done.attn_gain_grad,
        done.qh_grad.T,
        done.qs_grad,
        done.kh_grad.T,
        done.ks_grad,
        done.vh_grad.T,
        done.vs_grad,
        done.wo_grad,
        done.ffn_gain_grad,
        done.wg_grad,
        done.wu_grad,
        done.wd_grad,
    )


def solution(mesh):
    tokens = P(FSDP, SEQ, None)
    matrix = P(FSDP, None)
    vector = P(FSDP)
    kinds = (vector,) + (matrix,) * 7 + (vector,) + (matrix,) * 3
    return jax.shard_map(
        shards,
        mesh=mesh,
        in_specs=(tokens,) + kinds + (tokens,),
        out_specs=(tokens, tokens) + kinds,
        check_vma=False,
    )
```

```python
import functools
import types

import jax
import jax.numpy as jnp
import numpy as np
from jax import lax
from jax.experimental import pallas as pl
from jax.experimental.pallas import tpu as pltpu
from jax.sharding import PartitionSpec as P

SEQ = "seq"
FSDP = "fsdp"
H = 16
DH = 64
RQ = 6
RK = 2
NS = 4
LH = H // NS
EPS = 1e-06
BASE = 10000.0
MASKED = -1e30
NSH = 320
NH = 40
WF = 384
F32 = jnp.float32
BF16 = jnp.bfloat16
VMEM_LIMIT = 62 << 20


def dot_nn(a, b):
    return lax.dot_general(a, b, (((1,), (0,)), ((), ())), preferred_element_type=F32)


def dot_nt(a, b):
    return lax.dot_general(a, b, (((1,), (1,)), ((), ())), preferred_element_type=F32)


def dot_tn(a, b):
    return lax.dot_general(a, b, (((0,), (0,)), ((), ())), preferred_element_type=F32)


class Net:
    def __init__(self, n, send_sems, recv_sems):
        self.n = n
        self.ni = 2 if n <= 8 else 4
        self.no = n // self.ni
        self.s = lax.axis_index(SEQ)
        self.f = lax.axis_index(FSDP)
        self.o = self.f // self.ni
        self.i = self.f % self.ni
        self.core = self.s % 2
        self.sib = self.s + 1 - 2 * self.core
        self.across = (self.s + 2) % 4
        self.diag = (self.sib + 2) % 4
        self.send_sems = send_sems
        self.recv_sems = recv_sems
        self.sends = 0
        self.recvs = 0
        self.open = []

    def at(self, o, i):
        return o * self.ni + i

    def outer(self, k):
        return (self.o + k) % self.no

    def inner(self, m):
        return (self.i + m) % self.ni

    def inside(self, step):
        return jnp.logical_and(self.o + step >= 0, self.o + step < self.no)

    def next_outer(self, way):
        return {FSDP: self.at((self.o + way + self.no) % self.no, self.i)}

    def take(self, count):
        first = self.recvs
        self.recvs += count
        return first

    def greet(self):
        sem = pltpu.get_barrier_semaphore()
        peers = [{SEQ: self.sib}, {SEQ: self.across}]
        peers += [{FSDP: self.at(self.outer(k), self.i)} for k in range(1, self.no)]
        peers += [{FSDP: self.at(self.o, self.inner(m))} for m in range(1, self.ni)]
        for peer in peers:
            pl.semaphore_signal(sem, inc=1, device_id=peer, device_id_type=pl.DeviceIdType.MESH)
        return lambda: pl.semaphore_wait(sem, len(peers))

    def send(self, src, dst, slot, device, when=None):
        copy = pltpu.make_async_remote_copy(
            src_ref=src,
            dst_ref=dst,
            send_sem=self.send_sems.at[self.sends],
            recv_sem=self.recv_sems.at[slot],
            device_id=device,
            device_id_type=pl.DeviceIdType.MESH,
        )
        self.sends += 1
        if when is None:
            copy.start()
        else:
            pl.when(when)(copy.start)
        self.open.append((copy, when))

    def local(self, src, dst):
        copy = pltpu.make_async_copy(src, dst, self.send_sems.at[self.sends])
        self.sends += 1
        copy.start()
        return copy

    def arrived(self, dst, slot):
        pltpu.make_async_remote_copy(
            src_ref=dst,
            dst_ref=dst,
            send_sem=self.send_sems.at[0],
            recv_sem=self.recv_sems.at[slot],
            device_id={SEQ: self.sib},
            device_id_type=pl.DeviceIdType.MESH,
        ).wait_recv()

    def taken(self):
        copies, self.open = self.open, []
        return copies

    def settle(self, copies):
        for copy, when in copies:
            if when is None:
                copy.wait_send()
            else:
                pl.when(when)(copy.wait_send)


class Gather:
    def __init__(self, net, src, dst):
        self.net, self.src, self.dst = net, src, dst
        self.slot = net.take(net.n)

    def start(self):
        net = self.net
        own = self.dst.at[net.f]
        src = own if self.src is None else self.src
        for m in range(1, net.ni):
            net.send(src, own, self.slot + net.f, {FSDP: net.at(net.o, net.inner(m))})
        for k in range(1, net.no):
            net.send(src, own, self.slot + net.f, {FSDP: net.at(net.outer(k), net.i)})
        self.own = None if self.src is None else net.local(self.src, own)

    def block(self, index):
        self.net.arrived(self.dst.at[index], self.slot + index)

    def forward(self, k, then=None):
        net = self.net
        index = net.at((net.o - k + net.no) % net.no, net.i)
        self.block(index)
        for m in range(1, net.ni):
            net.send(self.dst.at[index], self.dst.at[index], self.slot + index, {FSDP: net.at(net.o, net.inner(m))})
        if then is not None:
            then(index)

    def finish(self, then=None):
        net = self.net
        for k in range(net.no):
            for m in range(1, net.ni):
                index = net.at((net.o - k + net.no) % net.no, net.inner(m))
                self.block(index)
                if then is not None:
                    then(index)
        if self.own is not None:
            self.own.wait()


class Line:
    def __init__(self, net, dst):
        self.net, self.dst = net, dst
        self.slot = net.take(net.n)

    def start(self):
        net = self.net
        own = self.dst.at[net.f]
        for way in (1, -1):
            net.send(own, own, self.slot + net.f, net.next_outer(way), net.inside(way))

    def start_inner(self):
        net = self.net
        own = self.dst.at[net.f]
        for m in range(1, net.ni):
            net.send(own, own, self.slot + net.f, {FSDP: net.at(net.o, net.inner(m))})

    def hop(self, h):
        net = self.net
        for way in (1, -1):
            here = net.inside(-way * h)
            index = net.at((net.o - way * h + net.no) % net.no, net.i)
            block = self.dst.at[index]
            slot = self.slot + index
            pl.when(here)(lambda block=block, slot=slot: net.arrived(block, slot))
            if h < net.no - 1:
                net.send(block, block, slot, net.next_outer(way), jnp.logical_and(here, net.inside(way)))
            for m in range(1, net.ni):
                net.send(block, block, slot, {FSDP: net.at(net.o, net.inner(m))}, here)

    def finish(self):
        net = self.net
        for o in range(net.no):
            for m in range(1, net.ni):
                index = net.at(o, net.inner(m))
                net.arrived(self.dst.at[index], self.slot + index)


class Spread:
    def __init__(self, net, src, dst, group):
        self.net, self.src, self.dst = net, src, dst
        self.wide = net.no // NS
        self.first = group * self.wide
        self.slot = net.take(net.n // NS)
        self.mine = jnp.logical_and(net.o >= self.first, net.o < self.first + self.wide)

    def along(self, index, when, way):
        net = self.net
        block = self.dst.at[index]
        net.send(block, block, self.slot + index, net.next_outer(way), jnp.logical_and(when, net.inside(way)))

    def start(self):
        net = self.net
        group = jnp.where(self.mine, net.o - self.first, 0)
        index = group * net.ni + net.i
        own = self.dst.at[index]
        for m in range(1, net.ni):
            net.send(self.src, own, self.slot + index, {FSDP: net.at(net.o, net.inner(m))}, self.mine)
        for way in (1, -1):
            when = jnp.logical_and(self.mine, net.inside(way))
            net.send(self.src, own, self.slot + index, net.next_outer(way), when)
        self.own = pltpu.make_async_copy(self.src, own, net.send_sems.at[net.sends])
        net.sends += 1
        pl.when(self.mine)(self.own.start)

    def second(self):
        net = self.net
        group = jnp.where(self.mine, net.o - self.first, 0)
        for m in range(1, net.ni):
            index = group * net.ni + net.inner(m)
            pl.when(self.mine)(lambda index=index: net.arrived(self.dst.at[index], self.slot + index))
            for way in (1, -1):
                self.along(index, self.mine, way)

    def hop(self, h):
        net = self.net
        for g in range(self.wide):
            for way in (1, -1):
                here = net.o - (self.first + g) == way * h
                for m in range(net.ni):
                    index = g * net.ni + net.inner(m)
                    pl.when(here)(lambda index=index: net.arrived(self.dst.at[index], self.slot + index))
                    if h < net.no - 1:
                        self.along(index, here, way)

    def finish(self):
        pl.when(self.mine)(self.own.wait)


class Share:
    def __init__(self, net, dst):
        self.net, self.dst = net, dst
        self.slot = net.take(NS)

    def start(self, src):
        net = self.net
        own = self.dst(net.s)
        net.send(src, own, self.slot + net.s, {SEQ: net.across})
        net.send(src, own, self.slot + net.s, {SEQ: net.sib})

    def forward(self):
        net = self.net
        far = self.dst(net.across)
        net.arrived(far, self.slot + net.across)
        net.send(far, far, self.slot + net.across, {SEQ: net.sib})

    def near(self):
        net = self.net
        net.arrived(self.dst(net.sib), self.slot + net.sib)

    def last(self):
        net = self.net
        net.arrived(self.dst(net.diag), self.slot + net.diag)


class Fold:
    def __init__(self, net, out, into):
        self.net, self.out, self.into = net, out, into
        self.slot = net.take(3)

    def to_diag(self, value):
        net = self.net
        self.out[0] = value.astype(BF16)
        net.send(self.out.at[0], self.into.at[0], self.slot, {SEQ: net.sib})

    def to_across(self, value):
        net = self.net
        net.arrived(self.into.at[0], self.slot)
        self.out[1] = (value + self.into[0].astype(F32)).astype(BF16)
        net.send(self.out.at[1], self.into.at[2], self.slot + 2, {SEQ: net.across})

    def to_sibling(self, value):
        net = self.net
        self.out[2] = value.astype(BF16)
        net.send(self.out.at[2], self.into.at[1], self.slot + 1, {SEQ: net.sib})

    def total(self, value):
        net = self.net
        net.arrived(self.into.at[1], self.slot + 1)
        net.arrived(self.into.at[2], self.slot + 2)
        return value + self.into[1].astype(F32) + self.into[2].astype(F32)


class Reduce:
    def __init__(self, net, src, near, far):
        self.net, self.src, self.near, self.far = net, src, near, far
        self.slot_near = net.take((net.ni - 1) * net.no)
        self.slot_far = net.take(net.no - 1)

    def start(self):
        net = self.net
        for k in [*range(1, net.no), 0]:
            o = net.outer(k)
            for m in range(1, net.ni):
                net.send(
                    self.src.at[net.at(o, net.inner(m))],
                    self.near.at[m - 1, o],
                    self.slot_near + (m - 1) * net.no + o,
                    {FSDP: net.at(net.o, net.inner(m))},
                )

    def column(self, o):
        net = self.net
        value = self.src[net.at(o, net.i)].astype(F32)
        for m in range(1, net.ni):
            net.arrived(self.near.at[m - 1, o], self.slot_near + (m - 1) * net.no + o)
            value = value + self.near[m - 1, o].astype(F32)
        return value

    def forward(self, k):
        net = self.net
        o = net.outer(k)
        index = net.at(o, net.i)
        self.src[index] = self.column(o).astype(BF16)
        net.send(self.src.at[index], self.far.at[k - 1], self.slot_far + k - 1, {FSDP: net.at(o, net.i)})

    def finish(self):
        net = self.net
        value = self.column(net.o)
        for k in range(1, net.no):
            net.arrived(self.far.at[k - 1], self.slot_far + k - 1)
            value = value + self.far[k - 1].astype(F32)
        return value


class Collect:
    def __init__(self, net, src, near, far, group, into):
        self.net, self.src, self.near, self.far, self.into = net, src, near, far, into
        self.wide = net.no // NS
        self.first = group * self.wide
        self.mine = jnp.logical_and(net.o >= self.first, net.o < self.first + self.wide)
        self.slot_near = net.take((net.ni - 1) * self.wide)
        self.slot_far = net.take(net.no - 1)
        self.slot_into = net.take(1)
        self.owner = (NS - net.o // self.wide) % NS

    def start(self):
        net = self.net
        for g in range(self.wide):
            for m in range(1, net.ni):
                net.send(
                    self.src.at[g * net.ni + net.inner(m)],
                    self.near.at[m - 1, g],
                    self.slot_near + (m - 1) * self.wide + g,
                    {FSDP: net.at(net.o, net.inner(m))},
                )

    def forward(self):
        net = self.net
        for g in range(self.wide):
            index = g * net.ni + net.i
            value = self.src[index].astype(F32)
            for m in range(1, net.ni):
                net.arrived(self.near.at[m - 1, g], self.slot_near + (m - 1) * self.wide + g)
                value = value + self.near[m - 1, g].astype(F32)
            self.src[index] = value.astype(BF16)
            o = self.first + g
            step = (o - net.o + net.no) % net.no
            away = step > 0
            place = jnp.where(away, step - 1, 0)
            net.send(self.src.at[index], self.far.at[place], self.slot_far + place, {FSDP: net.at(o, net.i)}, away)

    def finish(self):
        net = self.net

        @pl.when(self.mine)
        def _():
            value = self.src[jnp.where(self.mine, net.f - self.first * net.ni, 0)].astype(F32)
            for k in range(1, net.no):
                net.arrived(self.far.at[k - 1], self.slot_far + k - 1)
                value = value + self.far[k - 1].astype(F32)
            self.into[...] = value.astype(BF16)

        net.send(self.into, self.into, self.slot_into, {SEQ: net.across}, self.mine)
        net.send(self.into, self.into, self.slot_into, {SEQ: net.sib}, self.mine)

    def forward_into(self):
        net = self.net
        other = net.s != self.owner
        pl.when(other)(lambda: net.arrived(self.into, self.slot_into))
        net.send(self.into, self.into, self.slot_into, {SEQ: net.sib}, net.across == self.owner)


def matrix_of(ref):
    count, rows, cols = ref.shape
    if rows % 8 == 0:
        return ref[...].reshape(count * rows, cols)
    return jnp.concatenate([ref[index].astype(F32) for index in range(count)], axis=0).astype(BF16)


def own_maps(net, r, rows):
    all_qs = r.qs[...].astype(F32)
    both = jnp.concatenate([all_qs[:, 256:], r.ks[...].astype(F32), r.vs[...].astype(F32)], axis=1)
    both = pltpu.roll(both, WF - (NSH - 256), 1)
    value = jnp.where(net.core == 0, all_qs, both)
    lane = lax.broadcasted_iota(jnp.int32, (rows, WF), 1)
    value = jnp.where(lane < NSH, value, 0.0)
    at = NSH
    for ref, rank in ((r.qh, RQ), (r.kh, RK), (r.vh, RK)):
        count = LH * rank
        place = lax.broadcasted_iota(jnp.int32, (ref.shape[0], WF), 1) - at
        source = lax.broadcasted_iota(jnp.int32, (ref.shape[0], WF), 0) - net.s * count
        pick = jnp.logical_and(place == source, jnp.logical_and(place >= 0, place < count))
        value = value + dot_tn(ref[...], jnp.where(pick, 1.0, 0.0).astype(BF16))
        at += count
    eye = lax.broadcasted_iota(jnp.int32, (rows, rows), 0) == lax.broadcasted_iota(jnp.int32, (rows, rows), 1)
    for index, ref in enumerate((r.attn_gain, r.ffn_gain)):
        column = jnp.sum(jnp.where(eye, ref[...].astype(F32).reshape(1, rows), 0.0), axis=1, keepdims=True)
        value = jnp.where(lane == at + index, column, value)
    return value.astype(BF16)


def kernel(n, names, *refs):
    r = types.SimpleNamespace(**dict(zip(names, refs, strict=True)))
    net = Net(n, r.send_sems, r.recv_sems)
    tok, cot, wo, wg, wu, wd, att = r.tok, r.cot, r.wo, r.wg, r.wu, r.wd, r.att
    wf, wft, gains, shared, heads = r.wf, r.wft, r.gains, r.shared, r.heads
    qt, kt, vt, kn, vn, lse, att_t = r.qt, r.kt, r.vt, r.kn, r.vn, r.lse, r.att_t
    cos_ref, sin_ref = r.cosine, r.sine
    tokens, width = tok.shape[1:]
    length = NS * tokens
    rows, cols = wg.shape[1:]
    group = (NS - net.s) % NS
    meet = net.greet()
    first = group * cols
    begin = pl.multiple_of(first // 128 * 128, 128)
    wide = -(-cols // 128) * 128
    windows = [r.branch.at[index, pl.ds(0, rows), pl.ds(0, wide)] for index in range(2)]
    moves = [net.local(ref.at[:, pl.ds(begin, wide)], windows[index]) for index, ref in enumerate((r.gate, r.up))]
    wf[net.core, net.f] = own_maps(net, r, rows)
    meet()

    g_wf = Gather(net, None, wf.at[net.core])
    s_tok = Share(net, lambda rank: tok.at[rank])
    slot_sib = net.take(n)

    def to_sibling(index):
        here = wf.at[net.core, index]
        net.send(here, here, slot_sib + index, {SEQ: net.sib})

    g_wf.start()
    to_sibling(net.f)
    s_tok.start(r.tok_in)
    own_tok = net.local(r.tok_in, tok.at[net.s])
    g_wo = Gather(net, r.wo_in.at[:, pl.ds(pl.multiple_of(net.s * LH * DH, LH * DH), LH * DH)], wo.at[net.s])
    g_wd = Spread(net, r.wd_in, wd, group)
    g_wg = Line(net, wg)
    g_wu = Line(net, wu)
    s_cot = Share(net, lambda rank: cot.at[rank])
    s_cot.start(r.cot_in)
    own_cot = net.local(r.cot_in, cot.at[net.s])
    g_wd.start()

    def own_columns(index, out):
        moves[index].wait()

        @pl.when(first == begin)
        def _():
            out[net.f] = r.branch[index, :rows, :cols]

        @pl.when(first != begin)
        def _():
            moved = pltpu.roll(r.branch[index, :rows, :wide].astype(F32), wide - 64, 1)
            out[net.f] = moved[:, :cols].astype(BF16)

    own_columns(0, wg)
    own_columns(1, wu)
    for k in range(1, net.no):
        g_wf.forward(k, to_sibling)
    g_wo.start()
    g_wg.start()
    g_wu.start_inner()
    g_wf.finish(to_sibling)
    s_tok.forward()
    for index in range(n):
        net.arrived(wf.at[1 - net.core, index], slot_sib + index)

    for half in range(2):
        whole = wf[half].reshape(n * rows, WF).astype(F32).T
        wft[half] = whole.astype(BF16)
        if half == 0:
            gains[...] = whole[NSH + NH : NSH + NH + 8, :]
    own_tok.wait()
    s_tok.near()
    s_tok.last()
    g_wu.start()
    g_wg.start_inner()

    s_att = [Share(net, lambda rank, j=j: att.at[rank, pl.ds(tokens * j, tokens)]) for j in range(NS)]
    s_wo = Share(net, lambda rank: wo.at[rank])

    def rounded(v):
        return v.astype(BF16).astype(F32)

    for j in range(NS):
        here = slice(tokens * j, tokens * (j + 1))
        upto = tokens * j
        values = tok[j].astype(F32)
        inv = lax.rsqrt(jnp.mean(values * values, axis=-1, keepdims=True) + EPS)
        block = (values * inv * gains[0:1, :]).astype(BF16)
        parts = [dot_nt(wft[half], block) for half in range(2)]
        own = dot_nt(wft[net.core, NSH:, :], block)
        cosine, sine = cos_ref[:, here], sin_ref[:, here]

        def turned(piece):
            first, second = piece[: DH // 2], piece[DH // 2 :]
            return jnp.concatenate([first * cosine - second * sine, first * sine + second * cosine], axis=0)

        def piece(half, index):
            return parts[half][DH * index : DH * (index + 1)]

        sq = [rounded(turned(piece(0, p))) for p in range(5)] + [rounded(turned(piece(1, 0)))]
        sk = [rounded(turned(piece(1, 1 + p))) for p in range(RK)]
        sv = [rounded(piece(1, 3 + p)) for p in range(RK)]
        for index, part in enumerate(sq + sk + sv):
            shared[index // 5, DH * (index % 5) : DH * (index % 5 + 1), here] = part.astype(BF16)
        own = rounded(own[:NH])
        heads[:, here] = own
        for h in range(LH):
            q = sum(own[h * RQ + p : h * RQ + p + 1] * sq[p] for p in range(RQ)) * (1.0 / RQ)
            first = LH * RQ
            k = sum(own[first + h * RK + p : first + h * RK + p + 1] * sk[p] for p in range(RK)) * (1.0 / RK)
            first = LH * (RQ + RK)
            v = sum(own[first + h * RK + p : first + h * RK + p + 1] * sv[p] for p in range(RK)) * (1.0 / RK)
            qt[h, :, here] = (q.astype(BF16).astype(F32) * DH**-0.5).astype(BF16)
            kt[h, :, here] = k.astype(BF16)
            vt[h, :, here] = v.astype(BF16)
            kn[h, here, :] = rounded(k).T.astype(BF16)
            vn[h, here, :] = rounded(v).T.astype(BF16)

        def one_head(h, _):
            q = qt[h, :, here]
            keep = lax.broadcasted_iota(jnp.int32, (tokens, tokens), 0) <= lax.broadcasted_iota(
                jnp.int32, (tokens, tokens), 1
            )
            diagonal = jnp.where(keep, dot_nn(kn[h, here, :], q), MASKED)
            top = jnp.max(diagonal, axis=0, keepdims=True)
            if j > 0:
                below = dot_nn(kn[h, 0:upto, :], q)
                top = jnp.maximum(top, jnp.max(below, axis=0, keepdims=True))
            diagonal = jnp.exp(diagonal - top)
            total = jnp.sum(diagonal, axis=0, keepdims=True)
            if j > 0:
                below = jnp.exp(below - top)
                total = total + jnp.sum(below, axis=0, keepdims=True)
            inverse = 1.0 / total
            result = dot_nn(vt[h, :, here], (diagonal * inverse).astype(BF16))
            if j > 0:
                result = result + dot_nn(vt[h, :, 0:upto], (below * inverse).astype(BF16))
            lse[h, :, here] = top + jnp.log(total)
            att_t[h, :, here] = result
            return 0

        lax.fori_loop(0, LH, one_head, 0)
        turn = att_t[:, :, here].reshape(LH * DH, tokens).T
        att[net.s, here, :] = turn.astype(BF16)
        s_att[j].start(att.at[net.s, pl.ds(tokens * j, tokens)])
        if j == 0:
            for k in range(1, net.no):
                g_wo.forward(k)
            g_wd.second()
        if j == 1:
            g_wg.hop(1)
            s_cot.forward()
        if j == 2:
            g_wd.hop(1)
            g_wo.finish()
            s_wo.start(wo.at[net.s])
            g_wg.hop(2)
            g_wu.hop(1)
    g_wd.hop(2)
    for h in range(3, net.no):
        g_wg.hop(h)
    for share in s_att[:-1]:
        share.forward()
    g_wu.hop(2)
    s_wo.forward()
    s_att[-1].forward()
    for h in range(3, net.no):
        g_wu.hop(h)
    for share in [*s_att, s_wo]:
        share.near()
        share.last()

    gain = gains[1:2, :]
    f_dn = Fold(net, r.dn_out, r.dn_in)
    f_res = Fold(net, r.res_out, r.res_in)
    order = (net.diag, net.across, net.sib, net.s)
    n2_t, mixed_t, gg_all, gu_all = r.n2_t, r.mixed_t, r.gg, r.gu
    mid_own, inv_own, dn_own, branch = r.mid_own, r.inv_own, r.grad_mid, r.branch
    result = r.result

    for step, b in enumerate(order):
        here = slice(tokens * step, tokens * (step + 1))
        span = pl.ds(pl.multiple_of(b * tokens, tokens), tokens)
        middle = tok[b].astype(F32)
        for rank in range(NS):
            middle = middle + dot_nt(att[rank, span, :], wo[rank].reshape(width, LH * DH))
        inv = lax.rsqrt(jnp.mean(middle * middle, axis=-1, keepdims=True) + EPS)
        normal = middle * inv
        block = (normal * gain).astype(BF16)
        n2_t[:, here] = block.astype(F32).T.astype(BF16)
        if step == 3:
            mid_own[...] = middle
            inv_own[...] = jnp.broadcast_to(inv, inv_own.shape)
        if step == 0:
            g_wg.finish()
        wg_all = matrix_of(wg)
        gate = dot_nn(block, wg_all)
        if step == 0:
            for h in range(3, net.no):
                g_wd.hop(h)
            g_wu.finish()
        wu_all = matrix_of(wu)
        up = dot_nn(block, wu_all)
        sg = jax.nn.sigmoid(gate)
        act = gate * sg
        mixed = (act * up).astype(BF16)
        mixed_t[:, here] = mixed.astype(F32).T.astype(BF16)
        if step == 0:
            g_wd.finish()
            s_cot.near()
            s_cot.last()
            own_cot.wait()
            opening = net.taken()
        wd_all = matrix_of(wd)
        grad_mixed = dot_nt(cot[b], wd_all)
        gg = (grad_mixed * up * sg * (1.0 + gate * (1.0 - sg))).astype(BF16)
        gu = (grad_mixed * act).astype(BF16)
        gg_all[here, :] = gg
        gu_all[here, :] = gu
        dn = dot_nt(gg, wg_all) + dot_nt(gu, wu_all)
        if step == 0:
            f_dn.to_diag(dn)
        elif step == 1:
            f_dn.to_across(dn)
        elif step == 2:
            f_dn.to_sibling(dn)
        else:
            dn_own[...] = dn
        part = dot_nn(mixed, wd_all)
        if step == 0:
            f_res.to_diag(part)
        elif step == 1:
            f_res.out[1] = part.astype(BF16)
        elif step == 2:
            f_res.to_sibling(part)
        else:
            result[...] = part.astype(BF16)

    folded = net.taken()
    net.settle(opening)
    wg_grad, wu_grad, wd_grad = wg, wu, wd
    r_down = Collect(net, wd_grad, r.down_near, r.down_far, group, r.wd_out)
    r_gate = Reduce(net, wg_grad, r.gate_near, r.gate_far)
    r_up = Reduce(net, wu_grad, r.up_near, r.up_far)

    grad_mid = r.grad_mid
    s_branch = Share(net, lambda rank: branch.at[rank])
    kept = types.SimpleNamespace(saved=[])
    wo_t = wo[net.s].reshape(width, LH * DH).astype(F32).T.astype(BF16)

    grad_att, grad_q, grad_k, grad_v = r.vt, r.grad_q, r.grad_k, r.grad_v
    factors = n2_t
    wo_grad, wf_grad = wo.at[net.diag], wf.at[0]
    r_o = Reduce(net, wo_grad, r.o_near, r.o_far)
    below = lax.broadcasted_iota(jnp.int32, (tokens, tokens), 0) <= lax.broadcasted_iota(
        jnp.int32, (tokens, tokens), 1
    )

    def span_of(block):
        return pl.ds(pl.multiple_of(block * tokens, tokens), tokens)

    def back_factors(grads, rank, base, first_piece, turn, span):
        cosine, sine = cos_ref[:, span], sin_ref[:, span]
        own = heads[:, span]
        found = {}
        for p in range(rank):
            index = first_piece + p
            part = shared[index // 5, DH * (index % 5) : DH * (index % 5 + 1), span].astype(F32)
            rot = sum(own[base + h * rank + p : base + h * rank + p + 1] * grads[h] for h in range(LH)) * (1.0 / rank)
            if turn:
                first, second = rot[: DH // 2], rot[DH // 2 :]
                rot = jnp.concatenate([first * cosine + second * sine, second * cosine - first * sine], axis=0)
            first_row = WF * (index // 5) + DH * (index % 5)
            factors[first_row : first_row + DH, span] = rot.astype(BF16)
            for h in range(LH):
                found[h * rank + p] = jnp.sum(part * grads[h], axis=0, keepdims=True) * (1.0 / rank)
        head_grads[base : base + LH * rank, span] = jnp.concatenate([found[k] for k in range(LH * rank)], axis=0)

    head_grads = r.head_grads

    def attend_back(b):
        span = span_of(b)
        grad_att[:, :, span] = dot_nt(wo_t, branch[b]).astype(BF16).reshape(LH, DH, tokens)
        for h in range(LH):
            delta_all[h, :, :] = jnp.sum(
                grad_att[h, :, span].astype(F32) * att_t[h, :, span], axis=0, keepdims=True
            )

        def tile(k, diagonal):
            keys = span_of(k)
            for h in range(LH):
                q = qt[h, :, span]
                da = grad_att[h, :, span]
                scores = dot_nn(kn[h, keys, :], q)
                if diagonal:
                    scores = jnp.where(below, scores, MASKED)
                probs = jnp.exp(scores - lse[h, :, span])
                ds = (probs * (dot_nn(vn[h, keys, :], da) - delta_all[h])).astype(BF16)
                gq = dot_nn(kt[h, :, keys], ds)
                if diagonal:
                    grad_q[h] = gq
                else:
                    grad_q[h] += gq
                grad_k[h, :, keys] += dot_nt(q, ds)
                grad_v[h, :, keys] += dot_nt(da, probs.astype(BF16))

        tile(b, True)
        lax.fori_loop(0, b, lambda k, _: (tile(k, False), 0)[1], 0)
        back_factors([grad_q[h] * DH**-0.5 for h in range(LH)], RQ, 0, 0, True, span)

    delta_all = r.delta
    r_f = Reduce(net, wf_grad, r.f_near, r.f_far)
    f_gn = Fold(net, r.dn_out, r.dn_in)
    def map_grad(half):
        return sum(
            dot_nn(factors[pl.ds(pl.multiple_of(half * WF, WF), WF), tokens * b : tokens * (b + 1)], cot[b])
            for b in range(NS)
        )

    def gain_part(half, value):
        return jnp.sum(wft[half].astype(F32) * value, axis=0, keepdims=True)

    def normed_grad(b):
        columns = pl.ds(pl.multiple_of(b * tokens, tokens), tokens)
        return sum(
            dot_nn(factors[WF * half : WF * (half + 1), columns].astype(F32).T.astype(BF16), wft[half])
            for half in range(2)
        )

    def down_grad():
        wd_rows = wd_grad.shape[1]
        down = sum(dot_nn(mixed_t[:, tokens * k : tokens * (k + 1)], cot[b]) for k, b in enumerate(order))
        for index in range(wd_grad.shape[0]):
            wd_grad[index] = down[wd_rows * index : wd_rows * (index + 1)].astype(BF16)
        r_down.start()

    def gate_grad():
        wg_grad[...] = dot_nn(n2_t[...], gg_all[...]).astype(BF16).reshape(wg_grad.shape)
        r_gate.start()

    def up_grad():
        wu_grad[...] = dot_nn(n2_t[...], gu_all[...]).astype(BF16).reshape(wu_grad.shape)
        r_up.start()

    def mid_grads():
        total = f_dn.total(dn_own[...])
        inv = inv_own[:, 0:1]
        normal = mid_own[...] * inv
        scaled = total * gain
        mid_grad = cot[net.s].astype(F32) + inv * (scaled - normal * jnp.mean(scaled * normal, axis=-1, keepdims=True))
        grad_mid[...] = mid_grad
        kept.ffn_gain = jnp.sum(total * normal, axis=0, keepdims=True)
        branch[net.s] = mid_grad.astype(BF16)
        s_branch.start(branch.at[net.s])

    def norm_again():
        for b in range(NS):
            x = tok[b].astype(F32)
            scale = lax.rsqrt(jnp.mean(x * x, axis=-1, keepdims=True) + EPS)
            cot[b] = (x * scale * gains[0:1, :]).astype(BF16)
        grad_k[...] = jnp.zeros_like(grad_k)
        grad_v[...] = jnp.zeros_like(grad_v)
        factors[: 2 * WF, :] = jnp.zeros((2 * WF, length), BF16)

    def attend(b):
        return lambda: attend_back(b)

    def res_across():
        f_res.to_across(f_res.out[1].astype(F32))

    def res_total():
        result[...] = (mid_own[...] + f_res.total(result[...].astype(F32))).astype(BF16)
        kept.saved.append(net.local(result, r.result_end))

    def key_value_factors():
        for b in range(NS):
            here = slice(tokens * b, tokens * (b + 1))
            back_factors([grad_k[h, :, here] for h in range(LH)], RK, LH * RQ, RQ, True, here)
            back_factors([grad_v[h, :, here] for h in range(LH)], RK, LH * (RQ + RK), RQ + RK, False, here)
        rest = jnp.zeros((WF - NSH - NH, length), F32)
        factors[pl.ds(pl.multiple_of(net.core * WF + NSH, DH), WF - NSH), :] = jnp.concatenate(
            [head_grads[...], rest], axis=0
        ).astype(BF16)

    def out_grad():
        out_t = sum(
            dot_nn(att_t[:, :, tokens * b : tokens * (b + 1)].reshape(LH * DH, tokens).astype(BF16), branch[b]) for b in range(NS)
        )
        wo_grad[...] = out_t.T.astype(BF16).reshape(n, rows, LH * DH)
        r_o.start()

    def map_grads():
        slot_map = net.take(1)
        other = map_grad(1 - net.core)
        away = (n2_t.at[pl.ds(2 * WF, tokens)], mixed_t.at[pl.ds(WF, WF - tokens)])
        near = (mixed_t.at[pl.ds(0, tokens)], mixed_t.at[pl.ds(tokens, WF - tokens)])
        away[0][...] = other[:tokens].astype(BF16)
        away[1][...] = other[tokens:].astype(BF16)
        slot_more = net.take(1)
        net.send(away[0], near[0], slot_map, {SEQ: net.sib})
        net.send(away[1], near[1], slot_more, {SEQ: net.sib})
        mine = map_grad(net.core)
        attn_gain = (gain_part(net.core, mine) + gain_part(1 - net.core, other)) / gains[0:1, :]
        net.arrived(near[0], slot_map)
        net.arrived(near[1], slot_more)
        mine = mine + mixed_t[:WF].astype(F32)
        mine = jnp.concatenate([mine[: NSH + NH], attn_gain, kept.ffn_gain, mine[NSH + NH + 2 :]], axis=0)
        wf_grad[...] = mine.T.astype(BF16).reshape(n, rows, WF)
        r_f.start()

    def fold_grad(step):
        def act():
            if step == 0:
                net.settle(folded)
                f_gn.to_diag(normed_grad(net.diag))
            elif step == 1:
                f_gn.to_across(normed_grad(net.across))
            elif step == 2:
                f_gn.to_sibling(normed_grad(net.sib))
            else:
                kept.own_grad = normed_grad(net.s)

        return act

    def fold_total():
        total = f_gn.total(kept.own_grad)
        x = tok[net.s].astype(F32)
        scale = lax.rsqrt(jnp.mean(x * x, axis=-1, keepdims=True) + EPS)
        normal = x * scale
        scaled = total * gains[0:1, :]
        r.input_grad[...] = (
            grad_mid[...] + scale * (scaled - normal * jnp.mean(scaled * normal, axis=-1, keepdims=True))
        ).astype(BF16)
        kept.saved.append(net.local(r.input_grad, r.input_end))

    def on(reduce, *places):
        def act():
            for k in range(1, net.no):
                if min(k, 3) in places:
                    reduce.forward(k)

        return act

    shares = {}

    def share_out(reduce, out):
        def act():
            out[net.s] = reduce.finish().astype(BF16)
            shares[reduce] = Share(net, lambda rank: out.at[rank])
            shares[reduce].start(out.at[net.s])

        return act

    def pass_on(reduce):
        return lambda: shares[reduce].forward()

    steps = [
        gate_grad,
        mid_grads,
        up_grad,
        on(r_gate, 1),
        down_grad,
        res_across,
        norm_again,
        attend(net.s),
        s_branch.near,
        on(r_gate, 2),
        attend(net.sib),
        on(r_gate, 3),
        s_branch.forward,
        attend(net.across),
        s_branch.last,
        on(r_up, 1),
        attend(net.diag),
        on(r_up, 3),
        res_total,
        key_value_factors,
        out_grad,
        on(r_up, 2),
        fold_grad(0),
        fold_grad(1),
        map_grads,
        r_down.forward,
        fold_grad(2),
        share_out(r_gate, r.wg_out),
        share_out(r_up, r.wu_out),
        on(r_o, 1),
        fold_grad(3),
        on(r_o, 2),
        on(r_o, 3),
        on(r_f, 1),
        on(r_f, 2),
        on(r_f, 3),
        r_down.finish,
        fold_total,
        pass_on(r_up),
        share_out(r_o, r.wo_out),
        pass_on(r_gate),
        share_out(r_f, r.wf_out),
        r_down.forward_into,
        pass_on(r_o),
        pass_on(r_f),
    ]
    for step in steps:
        step()
    kept.saved.append(net.local(r.wd_out, r.wd_end))
    ends = ((r_gate, r.wg_out, r.wg_end), (r_up, r.wu_out, r.wu_end), (r_o, r.wo_out, r.wo_end), (r_f, r.wf_out, r.wf_end))
    for reduce, out, end in ends:
        shares[reduce].near()
        shares[reduce].last()
        kept.saved.append(net.local(out, end))
    for copy in kept.saved:
        copy.wait()
    net.settle(net.taken())


def sems(n):
    return [pltpu.SemaphoreType.DMA((10 * n + 80,))] * 2


def any_space(count):
    return [pl.BlockSpec(memory_space=pl.ANY)] * count


def vmem_space(count):
    return [pl.BlockSpec(memory_space=pltpu.VMEM)] * count


def run(n, given, small):
    r = types.SimpleNamespace(**given, **small)
    tokens, width = r.tok_in.shape
    length = tokens * NS
    rows = r.qs.shape[0]
    cols = r.gate.shape[1] // NS
    down = r.wd_in.shape
    hd = LH * DH
    ni = 2 if n <= 8 else 4
    no = n // ni
    wide = no // NS
    outs = dict(
        result=((tokens, width), BF16),
        input_grad=((tokens, width), BF16),
        wg_out=((NS, rows, cols), BF16),
        wu_out=((NS, rows, cols), BF16),
        wd_out=(down, BF16),
        wo_out=((NS, rows, hd), BF16),
        wf_out=((NS, rows, WF), BF16),
    )
    ends = dict(zip(dict(result_end=0, input_end=0, wg_end=0, wu_end=0, wd_end=0, wo_end=0, wf_end=0), outs.values()))
    scratch = dict(
        tok=((NS, tokens, width), BF16),
        cot=((NS, tokens, width), BF16),
        wo=((NS, n, rows, hd), BF16),
        wg=((n, rows, cols), BF16),
        wu=((n, rows, cols), BF16),
        wd=((n // NS,) + down, BF16),
        att=((NS, length, hd), BF16),
        wf=((2, n, rows, WF), BF16),
        wft=((2, WF, width), BF16),
        gains=((8, width), F32),
        shared=((2, NSH, length), BF16),
        heads=((NH, length), F32),
        qt=((LH, DH, length), BF16),
        kt=((LH, DH, length), BF16),
        vt=((LH, DH, length), BF16),
        kn=((LH, length, DH), BF16),
        vn=((LH, length, DH), BF16),
        lse=((LH, 1, length), F32),
        att_t=((LH, DH, length), F32),
        n2_t=((width, length), BF16),
        mixed_t=((cols, length), BF16),
        gg=((length, cols), BF16),
        gu=((length, cols), BF16),
        mid_own=((tokens, width), F32),
        inv_own=((tokens, 128), F32),
        grad_mid=((tokens, width), F32),
        branch=((NS, tokens, width), BF16),
        grad_q=((LH, DH, tokens), F32),
        delta=((LH, 1, tokens), F32),
        head_grads=((NH, length), F32),
        grad_k=((LH, DH, length), F32),
        grad_v=((LH, DH, length), F32),
        down_near=((ni - 1, wide) + down, BF16),
        down_far=((no - 1,) + down, BF16),
    )
    near, far = [
        [(lead + (rows, last), BF16) for last in (cols, hd, WF)] for lead in ((ni - 1, no), (no - 1,))
    ]
    three = ((3, tokens, width), BF16)
    scratch.update(
        gate_near=near[0],
        gate_far=far[0],
        up_near=near[0],
        up_far=far[0],
        o_near=near[1],
        o_far=far[1],
        f_near=near[2],
        f_far=far[2],
        dn_out=three,
        dn_in=three,
        res_out=three,
        res_in=three,
    )
    names = [*given, *small, *ends, *outs, *scratch, *dict(send_sems=0, recv_sems=0)]
    got = pl.pallas_call(
        functools.partial(kernel, n, names),
        out_shape=[jax.ShapeDtypeStruct(*shape) for shape in outs.values()],
        in_specs=any_space(len(given)) + vmem_space(len(small)),
        out_specs=any_space(len(outs)),
        scratch_shapes=[pltpu.VMEM(*shape) for shape in [*outs.values(), *scratch.values()]] + sems(n),
        compiler_params=pltpu.CompilerParams(collective_id=1, has_side_effects=True, vmem_limit_bytes=VMEM_LIMIT),
    )(*given.values(), *small.values())
    return dict(zip(outs, got, strict=True))


def tables(length):
    positions = np.arange(length, dtype=np.float32)
    frequency = (BASE ** (-2.0 * np.arange(DH // 2, dtype=np.float32) / DH)).astype(np.float32)
    angles = frequency[:, None] * positions[None, :]
    return np.cos(angles).astype(np.float32), np.sin(angles).astype(np.float32)


def finish_kernel(names, *refs):
    r = types.SimpleNamespace(**dict(zip(names, refs, strict=True)))
    r.result_out[...] = r.result[...]
    r.input_out[...] = r.input_grad[...]
    cols = r.wg_out.shape[2]
    for blocks, out in ((r.wg_out, r.wg_grad), (r.wu_out, r.wu_grad)):
        out[...] = jnp.concatenate([blocks[(NS - b) % NS].astype(F32) for b in range(NS)], axis=1)
    hd = LH * DH
    for rank in range(NS):
        r.wo_grad[:, hd * rank : hd * (rank + 1)] = r.wo_out[rank].astype(F32)
    r.wd_grad[...] = r.wd_out[...].astype(F32)
    f = [r.wf_out[rank].astype(F32) for rank in range(NS)]
    low = f[0] + f[2]
    high = f[1] + f[3]
    lane = lax.broadcasted_iota(jnp.int32, low.shape, 1)
    r.qs_grad[:, :256] = low[:, :256]
    moved = pltpu.roll(high, NSH, 1)
    r.qs_grad[:, 256:] = jnp.where(lane[:, 256:] < NSH, low[:, 256:], moved[:, 256:])
    shifted = pltpu.roll(high, WF - DH, 1)
    r.ks_grad[...] = shifted[:, :128]
    r.vs_grad[...] = shifted[:, 128:256]
    at = NSH
    for out, rank in ((r.qh_grad, RQ), (r.kh_grad, RK), (r.vh_grad, RK)):
        count = LH * rank
        place = lax.broadcasted_iota(jnp.int32, (NS * count, WF), 1) - at
        target = lax.broadcasted_iota(jnp.int32, (NS * count, WF), 0)
        total = 0.0
        for s in range(NS):
            pick = jnp.logical_and(target - s * count == place, jnp.logical_and(place >= 0, place < count))
            total = total + dot_nt(jnp.where(pick, 1.0, 0.0).astype(BF16), r.wf_out[s])
        out[...] = total
        at += count
    whole = low + high
    rows = whole.shape[0]
    eye = lax.broadcasted_iota(jnp.int32, (rows, rows), 0) == lax.broadcasted_iota(jnp.int32, (rows, rows), 1)
    for index in range(2):
        column = jnp.sum(jnp.where(lane == at + index, whole, 0.0), axis=1, keepdims=True)
        (r.attn_gain_grad, r.ffn_gain_grad)[index][...] = jnp.sum(jnp.where(eye, column, 0.0), axis=0)


def run_finish(got):
    one = types.SimpleNamespace(**got)
    rows, cols = one.wg_out.shape[1:]
    outs = dict(
        result_out=(one.result.shape, BF16),
        input_out=(one.result.shape, BF16),
        wg_grad=((rows, NS * cols), F32),
        wu_grad=((rows, NS * cols), F32),
        wd_grad=(one.wd_out.shape, F32),
        wo_grad=((rows, H * DH), F32),
        qh_grad=((H * RQ, rows), F32),
        qs_grad=((rows, RQ * DH), F32),
        kh_grad=((H * RK, rows), F32),
        ks_grad=((rows, RK * DH), F32),
        vh_grad=((H * RK, rows), F32),
        vs_grad=((rows, RK * DH), F32),
        attn_gain_grad=((rows,), F32),
        ffn_gain_grad=((rows,), F32),
    )
    names = [*got, *outs]
    done = pl.pallas_call(
        functools.partial(finish_kernel, names),
        out_shape=[jax.ShapeDtypeStruct(*shape) for shape in outs.values()],
        in_specs=vmem_space(len(got)),
        out_specs=vmem_space(len(outs)),
    )(*got.values())
    return types.SimpleNamespace(**dict(zip(outs, done, strict=True)))


def shards(tokens, attn_gain, qh, qs, kh, ks, vh, vs, out_proj, ffn_gain, gate, up, down, cotangent):
    n = lax.axis_size(FSDP)
    cosine, sine = tables(tokens.shape[1] * NS)
    given = dict(
        tok_in=tokens[0],
        wo_in=out_proj,
        gate=gate,
        up=up,
        wd_in=down,
        cot_in=cotangent[0],
    )
    small = dict(
        cosine=cosine,
        sine=sine,
        attn_gain=attn_gain,
        qh=qh.T,
        qs=qs,
        kh=kh.T,
        ks=ks,
        vh=vh.T,
        vs=vs,
        ffn_gain=ffn_gain,
    )
    done = run_finish(run(n, given, small))
    return (
        done.result_out[None],
        done.input_out[None],
        done.attn_gain_grad,
        done.qh_grad.T,
        done.qs_grad,
        done.kh_grad.T,
        done.ks_grad,
        done.vh_grad.T,
        done.vs_grad,
        done.wo_grad,
        done.ffn_gain_grad,
        done.wg_grad,
        done.wu_grad,
        done.wd_grad,
    )


def solution(mesh):
    tokens = P(FSDP, SEQ, None)
    matrix = P(FSDP, None)
    vector = P(FSDP)
    kinds = (vector,) + (matrix,) * 7 + (vector,) + (matrix,) * 3
    return jax.shard_map(
        shards,
        mesh=mesh,
        in_specs=(tokens,) + kinds + (tokens,),
        out_specs=(tokens, tokens) + kinds,
        check_vma=False,
    )
```

```python
import functools
import types

import jax
import jax.numpy as jnp
import numpy as np
from jax import lax
from jax.experimental import pallas as pl
from jax.experimental.pallas import tpu as pltpu
from jax.sharding import PartitionSpec as P

SEQ = "seq"
FSDP = "fsdp"
H = 16
DH = 64
RQ = 6
RK = 2
NS = 4
LH = H // NS
EPS = 1e-06
BASE = 10000.0
MASKED = -1e30
NSH = 320
NH = 40
WF = 384
F32 = jnp.float32
BF16 = jnp.bfloat16
VMEM_LIMIT = 62 << 20


def dot_nn(a, b):
    return lax.dot_general(a, b, (((1,), (0,)), ((), ())), preferred_element_type=F32)


def dot_nt(a, b):
    return lax.dot_general(a, b, (((1,), (1,)), ((), ())), preferred_element_type=F32)


def dot_tn(a, b):
    return lax.dot_general(a, b, (((0,), (0,)), ((), ())), preferred_element_type=F32)


class Net:
    def __init__(self, n, send_sems, recv_sems):
        self.n = n
        self.ni = 2 if n <= 8 else 4
        self.no = n // self.ni
        self.s = lax.axis_index(SEQ)
        self.f = lax.axis_index(FSDP)
        self.o = self.f // self.ni
        self.i = self.f % self.ni
        self.core = self.s % 2
        self.sib = self.s + 1 - 2 * self.core
        self.across = (self.s + 2) % 4
        self.diag = (self.sib + 2) % 4
        self.send_sems = send_sems
        self.recv_sems = recv_sems
        self.sends = 0
        self.recvs = 0
        self.open = []

    def at(self, o, i):
        return o * self.ni + i

    def outer(self, k):
        return (self.o + k) % self.no

    def inner(self, m):
        return (self.i + m) % self.ni

    def inside(self, step):
        return jnp.logical_and(self.o + step >= 0, self.o + step < self.no)

    def next_outer(self, way):
        return {FSDP: self.at((self.o + way + self.no) % self.no, self.i)}

    def take(self, count):
        first = self.recvs
        self.recvs += count
        return first

    def greet(self):
        sem = pltpu.get_barrier_semaphore()
        peers = [{SEQ: self.sib}, {SEQ: self.across}]
        peers += [{FSDP: self.at(self.outer(k), self.i)} for k in range(1, self.no)]
        peers += [{FSDP: self.at(self.o, self.inner(m))} for m in range(1, self.ni)]
        for peer in peers:
            pl.semaphore_signal(sem, inc=1, device_id=peer, device_id_type=pl.DeviceIdType.MESH)
        return lambda: pl.semaphore_wait(sem, len(peers))

    def send(self, src, dst, slot, device, when=None):
        copy = pltpu.make_async_remote_copy(
            src_ref=src,
            dst_ref=dst,
            send_sem=self.send_sems.at[self.sends],
            recv_sem=self.recv_sems.at[slot],
            device_id=device,
            device_id_type=pl.DeviceIdType.MESH,
        )
        self.sends += 1
        if when is None:
            copy.start()
        else:
            pl.when(when)(copy.start)
        self.open.append((copy, when))

    def local(self, src, dst):
        copy = pltpu.make_async_copy(src, dst, self.send_sems.at[self.sends])
        self.sends += 1
        copy.start()
        return copy

    def arrived(self, dst, slot):
        pltpu.make_async_remote_copy(
            src_ref=dst,
            dst_ref=dst,
            send_sem=self.send_sems.at[0],
            recv_sem=self.recv_sems.at[slot],
            device_id={SEQ: self.sib},
            device_id_type=pl.DeviceIdType.MESH,
        ).wait_recv()

    def taken(self):
        copies, self.open = self.open, []
        return copies

    def settle(self, copies):
        for copy, when in copies:
            if when is None:
                copy.wait_send()
            else:
                pl.when(when)(copy.wait_send)


class Gather:
    def __init__(self, net, src, dst):
        self.net, self.src, self.dst = net, src, dst
        self.slot = net.take(net.n)

    def start(self):
        net = self.net
        own = self.dst.at[net.f]
        src = own if self.src is None else self.src
        for m in range(1, net.ni):
            net.send(src, own, self.slot + net.f, {FSDP: net.at(net.o, net.inner(m))})
        for k in range(1, net.no):
            net.send(src, own, self.slot + net.f, {FSDP: net.at(net.outer(k), net.i)})
        self.own = None if self.src is None else net.local(self.src, own)

    def block(self, index):
        self.net.arrived(self.dst.at[index], self.slot + index)

    def forward(self, k, then=None):
        net = self.net
        index = net.at((net.o - k + net.no) % net.no, net.i)
        self.block(index)
        for m in range(1, net.ni):
            net.send(self.dst.at[index], self.dst.at[index], self.slot + index, {FSDP: net.at(net.o, net.inner(m))})
        if then is not None:
            then(index)

    def finish(self, then=None):
        net = self.net
        for k in range(net.no):
            for m in range(1, net.ni):
                index = net.at((net.o - k + net.no) % net.no, net.inner(m))
                self.block(index)
                if then is not None:
                    then(index)
        if self.own is not None:
            self.own.wait()


class Line:
    def __init__(self, net, dst):
        self.net, self.dst = net, dst
        self.slot = net.take(net.n)

    def start(self):
        net = self.net
        own = self.dst.at[net.f]
        for way in (1, -1):
            net.send(own, own, self.slot + net.f, net.next_outer(way), net.inside(way))

    def start_inner(self):
        net = self.net
        own = self.dst.at[net.f]
        for m in range(1, net.ni):
            net.send(own, own, self.slot + net.f, {FSDP: net.at(net.o, net.inner(m))})

    def hop(self, h):
        net = self.net
        for way in (1, -1):
            here = net.inside(-way * h)
            index = net.at((net.o - way * h + net.no) % net.no, net.i)
            block = self.dst.at[index]
            slot = self.slot + index
            pl.when(here)(lambda block=block, slot=slot: net.arrived(block, slot))
            if h < net.no - 1:
                net.send(block, block, slot, net.next_outer(way), jnp.logical_and(here, net.inside(way)))
            for m in range(1, net.ni):
                net.send(block, block, slot, {FSDP: net.at(net.o, net.inner(m))}, here)

    def finish(self):
        net = self.net
        for o in range(net.no):
            for m in range(1, net.ni):
                index = net.at(o, net.inner(m))
                net.arrived(self.dst.at[index], self.slot + index)


class Spread:
    def __init__(self, net, src, dst, group):
        self.net, self.src, self.dst = net, src, dst
        self.wide = net.no // NS
        self.first = group * self.wide
        self.slot = net.take(net.n // NS)
        self.mine = jnp.logical_and(net.o >= self.first, net.o < self.first + self.wide)

    def along(self, index, when, way):
        net = self.net
        block = self.dst.at[index]
        net.send(block, block, self.slot + index, net.next_outer(way), jnp.logical_and(when, net.inside(way)))

    def start(self):
        net = self.net
        group = jnp.where(self.mine, net.o - self.first, 0)
        index = group * net.ni + net.i
        own = self.dst.at[index]
        for m in range(1, net.ni):
            net.send(self.src, own, self.slot + index, {FSDP: net.at(net.o, net.inner(m))}, self.mine)
        for way in (1, -1):
            when = jnp.logical_and(self.mine, net.inside(way))
            net.send(self.src, own, self.slot + index, net.next_outer(way), when)
        self.own = pltpu.make_async_copy(self.src, own, net.send_sems.at[net.sends])
        net.sends += 1
        pl.when(self.mine)(self.own.start)

    def second(self):
        net = self.net
        group = jnp.where(self.mine, net.o - self.first, 0)
        for m in range(1, net.ni):
            index = group * net.ni + net.inner(m)
            pl.when(self.mine)(lambda index=index: net.arrived(self.dst.at[index], self.slot + index))
            for way in (1, -1):
                self.along(index, self.mine, way)

    def hop(self, h):
        net = self.net
        for g in range(self.wide):
            for way in (1, -1):
                here = net.o - (self.first + g) == way * h
                for m in range(net.ni):
                    index = g * net.ni + net.inner(m)
                    pl.when(here)(lambda index=index: net.arrived(self.dst.at[index], self.slot + index))
                    if h < net.no - 1:
                        self.along(index, here, way)

    def finish(self):
        pl.when(self.mine)(self.own.wait)


class Share:
    def __init__(self, net, dst):
        self.net, self.dst = net, dst
        self.slot = net.take(NS)

    def start(self, src):
        net = self.net
        own = self.dst(net.s)
        net.send(src, own, self.slot + net.s, {SEQ: net.across})
        net.send(src, own, self.slot + net.s, {SEQ: net.sib})

    def forward(self):
        net = self.net
        far = self.dst(net.across)
        net.arrived(far, self.slot + net.across)
        net.send(far, far, self.slot + net.across, {SEQ: net.sib})

    def near(self):
        net = self.net
        net.arrived(self.dst(net.sib), self.slot + net.sib)

    def last(self):
        net = self.net
        net.arrived(self.dst(net.diag), self.slot + net.diag)


class Fold:
    def __init__(self, net, out, into):
        self.net, self.out, self.into = net, out, into
        self.slot = net.take(3)

    def to_diag(self, value):
        net = self.net
        self.out[0] = value.astype(BF16)
        net.send(self.out.at[0], self.into.at[0], self.slot, {SEQ: net.sib})

    def to_across(self, value):
        net = self.net
        net.arrived(self.into.at[0], self.slot)
        self.out[1] = (value + self.into[0].astype(F32)).astype(BF16)
        net.send(self.out.at[1], self.into.at[2], self.slot + 2, {SEQ: net.across})

    def to_sibling(self, value):
        net = self.net
        self.out[2] = value.astype(BF16)
        net.send(self.out.at[2], self.into.at[1], self.slot + 1, {SEQ: net.sib})

    def total(self, value):
        net = self.net
        net.arrived(self.into.at[1], self.slot + 1)
        net.arrived(self.into.at[2], self.slot + 2)
        return value + self.into[1].astype(F32) + self.into[2].astype(F32)


class Reduce:
    def __init__(self, net, src, near, far):
        self.net, self.src, self.near, self.far = net, src, near, far
        self.slot_near = net.take((net.ni - 1) * net.no)
        self.slot_far = net.take(net.no - 1)

    def start(self):
        net = self.net
        for k in [*range(1, net.no), 0]:
            o = net.outer(k)
            for m in range(1, net.ni):
                net.send(
                    self.src.at[net.at(o, net.inner(m))],
                    self.near.at[m - 1, o],
                    self.slot_near + (m - 1) * net.no + o,
                    {FSDP: net.at(net.o, net.inner(m))},
                )

    def column(self, o):
        net = self.net
        value = self.src[net.at(o, net.i)].astype(F32)
        for m in range(1, net.ni):
            net.arrived(self.near.at[m - 1, o], self.slot_near + (m - 1) * net.no + o)
            value = value + self.near[m - 1, o].astype(F32)
        return value

    def forward(self, k):
        net = self.net
        o = net.outer(k)
        index = net.at(o, net.i)
        self.src[index] = self.column(o).astype(BF16)
        net.send(self.src.at[index], self.far.at[k - 1], self.slot_far + k - 1, {FSDP: net.at(o, net.i)})

    def finish(self):
        net = self.net
        value = self.column(net.o)
        for k in range(1, net.no):
            net.arrived(self.far.at[k - 1], self.slot_far + k - 1)
            value = value + self.far[k - 1].astype(F32)
        return value


class Collect:
    def __init__(self, net, src, near, far, group, into):
        self.net, self.src, self.near, self.far, self.into = net, src, near, far, into
        self.wide = net.no // NS
        self.first = group * self.wide
        self.mine = jnp.logical_and(net.o >= self.first, net.o < self.first + self.wide)
        self.slot_near = net.take((net.ni - 1) * self.wide)
        self.slot_far = net.take(net.no - 1)
        self.slot_into = net.take(1)
        self.owner = (NS - net.o // self.wide) % NS

    def start(self):
        net = self.net
        for g in range(self.wide):
            for m in range(1, net.ni):
                net.send(
                    self.src.at[g * net.ni + net.inner(m)],
                    self.near.at[m - 1, g],
                    self.slot_near + (m - 1) * self.wide + g,
                    {FSDP: net.at(net.o, net.inner(m))},
                )

    def forward(self):
        net = self.net
        for g in range(self.wide):
            index = g * net.ni + net.i
            value = self.src[index].astype(F32)
            for m in range(1, net.ni):
                net.arrived(self.near.at[m - 1, g], self.slot_near + (m - 1) * self.wide + g)
                value = value + self.near[m - 1, g].astype(F32)
            self.src[index] = value.astype(BF16)
            o = self.first + g
            step = (o - net.o + net.no) % net.no
            away = step > 0
            place = jnp.where(away, step - 1, 0)
            net.send(self.src.at[index], self.far.at[place], self.slot_far + place, {FSDP: net.at(o, net.i)}, away)

    def finish(self):
        net = self.net

        @pl.when(self.mine)
        def _():
            value = self.src[jnp.where(self.mine, net.f - self.first * net.ni, 0)].astype(F32)
            for k in range(1, net.no):
                net.arrived(self.far.at[k - 1], self.slot_far + k - 1)
                value = value + self.far[k - 1].astype(F32)
            self.into[...] = value.astype(BF16)

        net.send(self.into, self.into, self.slot_into, {SEQ: net.across}, self.mine)
        net.send(self.into, self.into, self.slot_into, {SEQ: net.sib}, self.mine)

    def forward_into(self):
        net = self.net
        other = net.s != self.owner
        pl.when(other)(lambda: net.arrived(self.into, self.slot_into))
        net.send(self.into, self.into, self.slot_into, {SEQ: net.sib}, net.across == self.owner)


def matrix_of(ref):
    count, rows, cols = ref.shape
    if rows % 8 == 0:
        return ref[...].reshape(count * rows, cols)
    return jnp.concatenate([ref[index].astype(F32) for index in range(count)], axis=0).astype(BF16)


def own_maps(net, r, rows):
    all_qs = r.qs[...].astype(F32)
    both = jnp.concatenate([all_qs[:, 256:], r.ks[...].astype(F32), r.vs[...].astype(F32)], axis=1)
    both = pltpu.roll(both, WF - (NSH - 256), 1)
    value = jnp.where(net.core == 0, all_qs, both)
    lane = lax.broadcasted_iota(jnp.int32, (rows, WF), 1)
    value = jnp.where(lane < NSH, value, 0.0)
    at = NSH
    for ref, rank in ((r.qh, RQ), (r.kh, RK), (r.vh, RK)):
        count = LH * rank
        place = lax.broadcasted_iota(jnp.int32, (ref.shape[0], WF), 1) - at
        source = lax.broadcasted_iota(jnp.int32, (ref.shape[0], WF), 0) - net.s * count
        pick = jnp.logical_and(place == source, jnp.logical_and(place >= 0, place < count))
        value = value + dot_tn(ref[...], jnp.where(pick, 1.0, 0.0).astype(BF16))
        at += count
    eye = lax.broadcasted_iota(jnp.int32, (rows, rows), 0) == lax.broadcasted_iota(jnp.int32, (rows, rows), 1)
    for index, ref in enumerate((r.attn_gain, r.ffn_gain)):
        column = jnp.sum(jnp.where(eye, ref[...].astype(F32).reshape(1, rows), 0.0), axis=1, keepdims=True)
        value = jnp.where(lane == at + index, column, value)
    return value.astype(BF16)


def kernel(n, names, *refs):
    r = types.SimpleNamespace(**dict(zip(names, refs, strict=True)))
    net = Net(n, r.send_sems, r.recv_sems)
    tok, cot, wo, wg, wu, wd, att = r.tok, r.cot, r.wo, r.wg, r.wu, r.wd, r.att
    wf, wft, gains, shared, heads = r.wf, r.wft, r.gains, r.shared, r.heads
    qt, kt, vt, kn, vn, lse, att_t = r.qt, r.kt, r.vt, r.kn, r.vn, r.lse, r.att_t
    cos_ref, sin_ref = r.cosine, r.sine
    tokens, width = tok.shape[1:]
    length = NS * tokens
    rows, cols = wg.shape[1:]
    group = (NS - net.s) % NS
    meet = net.greet()
    first = group * cols
    begin = pl.multiple_of(first // 128 * 128, 128)
    wide = -(-cols // 128) * 128
    windows = [r.branch.at[index, pl.ds(0, rows), pl.ds(0, wide)] for index in range(2)]
    moves = [net.local(ref.at[:, pl.ds(begin, wide)], windows[index]) for index, ref in enumerate((r.gate, r.up))]
    wf[net.core, net.f] = own_maps(net, r, rows)
    meet()

    g_wf = Gather(net, None, wf.at[net.core])
    s_tok = Share(net, lambda rank: tok.at[rank])
    slot_sib = net.take(n)

    def to_sibling(index):
        here = wf.at[net.core, index]
        net.send(here, here, slot_sib + index, {SEQ: net.sib})

    g_wf.start()
    to_sibling(net.f)
    s_tok.start(r.tok_in)
    own_tok = net.local(r.tok_in, tok.at[net.s])
    g_wo = Gather(net, r.wo_in.at[:, pl.ds(pl.multiple_of(net.s * LH * DH, LH * DH), LH * DH)], wo.at[net.s])
    g_wd = Spread(net, r.wd_in, wd, group)
    g_wg = Line(net, wg)
    g_wu = Line(net, wu)
    s_cot = Share(net, lambda rank: cot.at[rank])
    s_cot.start(r.cot_in)
    own_cot = net.local(r.cot_in, cot.at[net.s])
    g_wd.start()

    def own_columns(index, out):
        moves[index].wait()

        @pl.when(first == begin)
        def _():
            out[net.f] = r.branch[index, :rows, :cols]

        @pl.when(first != begin)
        def _():
            moved = pltpu.roll(r.branch[index, :rows, :wide].astype(F32), wide - 64, 1)
            out[net.f] = moved[:, :cols].astype(BF16)

    own_columns(0, wg)
    own_columns(1, wu)
    for k in range(1, net.no):
        g_wf.forward(k, to_sibling)
    g_wo.start()
    g_wg.start()
    g_wu.start_inner()
    g_wf.finish(to_sibling)
    s_tok.forward()
    for index in range(n):
        net.arrived(wf.at[1 - net.core, index], slot_sib + index)

    for half in range(2):
        whole = wf[half].reshape(n * rows, WF).astype(F32).T
        wft[half] = whole.astype(BF16)
        if half == 0:
            gains[...] = whole[NSH + NH : NSH + NH + 8, :]
    own_tok.wait()
    s_tok.near()
    s_tok.last()
    g_wu.start()
    g_wg.start_inner()

    s_att = [Share(net, lambda rank, j=j: att.at[rank, pl.ds(tokens * j, tokens)]) for j in range(NS)]
    s_wo = Share(net, lambda rank: wo.at[rank])

    def rounded(v):
        return v.astype(BF16).astype(F32)

    for j in range(NS):
        here = slice(tokens * j, tokens * (j + 1))
        upto = tokens * j
        values = tok[j].astype(F32)
        inv = lax.rsqrt(jnp.mean(values * values, axis=-1, keepdims=True) + EPS)
        block = (values * inv * gains[0:1, :]).astype(BF16)
        parts = [dot_nt(wft[half], block) for half in range(2)]
        own = dot_nt(wft[net.core, NSH:, :], block)
        cosine, sine = cos_ref[:, here], sin_ref[:, here]

        def turned(piece):
            first, second = piece[: DH // 2], piece[DH // 2 :]
            return jnp.concatenate([first * cosine - second * sine, first * sine + second * cosine], axis=0)

        def piece(half, index):
            return parts[half][DH * index : DH * (index + 1)]

        sq = [rounded(turned(piece(0, p))) for p in range(5)] + [rounded(turned(piece(1, 0)))]
        sk = [rounded(turned(piece(1, 1 + p))) for p in range(RK)]
        sv = [rounded(piece(1, 3 + p)) for p in range(RK)]
        for index, part in enumerate(sq + sk + sv):
            shared[index // 5, DH * (index % 5) : DH * (index % 5 + 1), here] = part.astype(BF16)
        own = rounded(own[:NH])
        heads[:, here] = own
        for h in range(LH):
            q = sum(own[h * RQ + p : h * RQ + p + 1] * sq[p] for p in range(RQ)) * (1.0 / RQ)
            first = LH * RQ
            k = sum(own[first + h * RK + p : first + h * RK + p + 1] * sk[p] for p in range(RK)) * (1.0 / RK)
            first = LH * (RQ + RK)
            v = sum(own[first + h * RK + p : first + h * RK + p + 1] * sv[p] for p in range(RK)) * (1.0 / RK)
            qt[h, :, here] = (q.astype(BF16).astype(F32) * DH**-0.5).astype(BF16)
            kt[h, :, here] = k.astype(BF16)
            vt[h, :, here] = v.astype(BF16)
            kn[h, here, :] = rounded(k).T.astype(BF16)
            vn[h, here, :] = rounded(v).T.astype(BF16)

        def one_head(h, _):
            q = qt[h, :, here]
            keep = lax.broadcasted_iota(jnp.int32, (tokens, tokens), 0) <= lax.broadcasted_iota(
                jnp.int32, (tokens, tokens), 1
            )
            diagonal = jnp.where(keep, dot_nn(kn[h, here, :], q), MASKED)
            top = jnp.max(diagonal, axis=0, keepdims=True)
            if j > 0:
                below = dot_nn(kn[h, 0:upto, :], q)
                top = jnp.maximum(top, jnp.max(below, axis=0, keepdims=True))
            diagonal = jnp.exp(diagonal - top)
            total = jnp.sum(diagonal, axis=0, keepdims=True)
            if j > 0:
                below = jnp.exp(below - top)
                total = total + jnp.sum(below, axis=0, keepdims=True)
            inverse = 1.0 / total
            result = dot_nn(vt[h, :, here], (diagonal * inverse).astype(BF16))
            if j > 0:
                result = result + dot_nn(vt[h, :, 0:upto], (below * inverse).astype(BF16))
            lse[h, :, here] = top + jnp.log(total)
            att_t[h, :, here] = result
            return 0

        def two_heads(pair, _):
            one_head(2 * pair, 0)
            return one_head(2 * pair + 1, 0)

        lax.fori_loop(0, LH // 2, two_heads, 0)
        turn = att_t[:, :, here].reshape(LH * DH, tokens).T
        att[net.s, here, :] = turn.astype(BF16)
        s_att[j].start(att.at[net.s, pl.ds(tokens * j, tokens)])
        if j == 0:
            for k in range(1, net.no):
                g_wo.forward(k)
            g_wd.second()
        if j == 1:
            g_wg.hop(1)
            s_cot.forward()
        if j == 2:
            g_wd.hop(1)
            g_wo.finish()
            s_wo.start(wo.at[net.s])
            g_wg.hop(2)
            g_wu.hop(1)
    g_wd.hop(2)
    for h in range(3, net.no):
        g_wg.hop(h)
    for share in s_att[:-1]:
        share.forward()
    g_wu.hop(2)
    s_wo.forward()
    s_att[-1].forward()
    for h in range(3, net.no):
        g_wu.hop(h)
    for share in [*s_att, s_wo]:
        share.near()
        share.last()

    gain = gains[1:2, :]
    f_dn = Fold(net, r.dn_out, r.dn_in)
    f_res = Fold(net, r.res_out, r.res_in)
    order = (net.diag, net.across, net.sib, net.s)
    n2_t, mixed_t, gg_all, gu_all = r.n2_t, r.mixed_t, r.gg, r.gu
    mid_own, inv_own, dn_own, branch = r.mid_own, r.inv_own, r.grad_mid, r.branch
    result = r.result

    for step, b in enumerate(order):
        here = slice(tokens * step, tokens * (step + 1))
        span = pl.ds(pl.multiple_of(b * tokens, tokens), tokens)
        middle = tok[b].astype(F32)
        for rank in range(NS):
            middle = middle + dot_nt(att[rank, span, :], wo[rank].reshape(width, LH * DH))
        inv = lax.rsqrt(jnp.mean(middle * middle, axis=-1, keepdims=True) + EPS)
        normal = middle * inv
        block = (normal * gain).astype(BF16)
        n2_t[:, here] = block.astype(F32).T.astype(BF16)
        if step == 3:
            mid_own[...] = middle
            inv_own[...] = jnp.broadcast_to(inv, inv_own.shape)
        if step == 0:
            g_wg.finish()
        wg_all = matrix_of(wg)
        gate = dot_nn(block, wg_all)
        if step == 0:
            for h in range(3, net.no):
                g_wd.hop(h)
            g_wu.finish()
        wu_all = matrix_of(wu)
        up = dot_nn(block, wu_all)
        sg = jax.nn.sigmoid(gate)
        act = gate * sg
        mixed = (act * up).astype(BF16)
        mixed_t[:, here] = mixed.astype(F32).T.astype(BF16)
        if step == 0:
            g_wd.finish()
            s_cot.near()
            s_cot.last()
            own_cot.wait()
            opening = net.taken()
        wd_all = matrix_of(wd)
        grad_mixed = dot_nt(cot[b], wd_all)
        gg = (grad_mixed * up * sg * (1.0 + gate * (1.0 - sg))).astype(BF16)
        gu = (grad_mixed * act).astype(BF16)
        gg_all[here, :] = gg
        gu_all[here, :] = gu
        dn = dot_nt(gg, wg_all) + dot_nt(gu, wu_all)
        if step == 0:
            f_dn.to_diag(dn)
        elif step == 1:
            f_dn.to_across(dn)
        elif step == 2:
            f_dn.to_sibling(dn)
        else:
            dn_own[...] = dn
        part = dot_nn(mixed, wd_all)
        if step == 0:
            f_res.to_diag(part)
        elif step == 1:
            f_res.out[1] = part.astype(BF16)
        elif step == 2:
            f_res.to_sibling(part)
        else:
            result[...] = part.astype(BF16)

    folded = net.taken()
    net.settle(opening)
    wg_grad, wu_grad, wd_grad = wg, wu, wd
    r_down = Collect(net, wd_grad, r.down_near, r.down_far, group, r.wd_out)
    r_gate = Reduce(net, wg_grad, r.gate_near, r.gate_far)
    r_up = Reduce(net, wu_grad, r.up_near, r.up_far)

    grad_mid = r.grad_mid
    s_branch = Share(net, lambda rank: branch.at[rank])
    kept = types.SimpleNamespace(saved=[])
    wo_t = wo[net.s].reshape(width, LH * DH).astype(F32).T.astype(BF16)

    grad_att, grad_q, grad_k, grad_v = r.vt, r.grad_q, r.grad_k, r.grad_v
    factors = n2_t
    wo_grad, wf_grad = wo.at[net.diag], wf.at[0]
    r_o = Reduce(net, wo_grad, r.o_near, r.o_far)
    below = lax.broadcasted_iota(jnp.int32, (tokens, tokens), 0) <= lax.broadcasted_iota(
        jnp.int32, (tokens, tokens), 1
    )

    def span_of(block):
        return pl.ds(pl.multiple_of(block * tokens, tokens), tokens)

    def back_factors(grads, rank, base, first_piece, turn, span):
        cosine, sine = cos_ref[:, span], sin_ref[:, span]
        own = heads[:, span]
        found = {}
        for p in range(rank):
            index = first_piece + p
            part = shared[index // 5, DH * (index % 5) : DH * (index % 5 + 1), span].astype(F32)
            rot = sum(own[base + h * rank + p : base + h * rank + p + 1] * grads[h] for h in range(LH)) * (1.0 / rank)
            if turn:
                first, second = rot[: DH // 2], rot[DH // 2 :]
                rot = jnp.concatenate([first * cosine + second * sine, second * cosine - first * sine], axis=0)
            first_row = WF * (index // 5) + DH * (index % 5)
            factors[first_row : first_row + DH, span] = rot.astype(BF16)
            for h in range(LH):
                found[h * rank + p] = jnp.sum(part * grads[h], axis=0, keepdims=True) * (1.0 / rank)
        head_grads[base : base + LH * rank, span] = jnp.concatenate([found[k] for k in range(LH * rank)], axis=0)

    head_grads = r.head_grads

    def attend_back(b):
        span = span_of(b)
        grad_att[:, :, span] = dot_nt(wo_t, branch[b]).astype(BF16).reshape(LH, DH, tokens)
        for h in range(LH):
            delta_all[h, :, :] = jnp.sum(
                grad_att[h, :, span].astype(F32) * att_t[h, :, span], axis=0, keepdims=True
            )

        def tile(k, diagonal):
            keys = span_of(k)
            for h in range(LH):
                q = qt[h, :, span]
                da = grad_att[h, :, span]
                scores = dot_nn(kn[h, keys, :], q)
                if diagonal:
                    scores = jnp.where(below, scores, MASKED)
                probs = jnp.exp(scores - lse[h, :, span])
                ds = (probs * (dot_nn(vn[h, keys, :], da) - delta_all[h])).astype(BF16)
                gq = dot_nn(kt[h, :, keys], ds)
                if diagonal:
                    grad_q[h] = gq
                else:
                    grad_q[h] += gq
                grad_k[h, :, keys] += dot_nt(q, ds)
                grad_v[h, :, keys] += dot_nt(da, probs.astype(BF16))

        tile(b, True)
        lax.fori_loop(0, b, lambda k, _: (tile(k, False), 0)[1], 0)
        back_factors([grad_q[h] * DH**-0.5 for h in range(LH)], RQ, 0, 0, True, span)

    delta_all = r.delta
    r_f = Reduce(net, wf_grad, r.f_near, r.f_far)
    f_gn = Fold(net, r.dn_out, r.dn_in)
    def map_grad(half):
        return sum(
            dot_nn(factors[pl.ds(pl.multiple_of(half * WF, WF), WF), tokens * b : tokens * (b + 1)], cot[b])
            for b in range(NS)
        )

    def gain_part(half, value):
        return jnp.sum(wft[half].astype(F32) * value, axis=0, keepdims=True)

    def normed_grad(b):
        columns = pl.ds(pl.multiple_of(b * tokens, tokens), tokens)
        return sum(
            dot_nn(factors[WF * half : WF * (half + 1), columns].astype(F32).T.astype(BF16), wft[half])
            for half in range(2)
        )

    def down_grad():
        wd_rows = wd_grad.shape[1]
        down = sum(dot_nn(mixed_t[:, tokens * k : tokens * (k + 1)], cot[b]) for k, b in enumerate(order))
        for index in range(wd_grad.shape[0]):
            wd_grad[index] = down[wd_rows * index : wd_rows * (index + 1)].astype(BF16)
        r_down.start()

    def gate_grad():
        wg_grad[...] = dot_nn(n2_t[...], gg_all[...]).astype(BF16).reshape(wg_grad.shape)
        r_gate.start()

    def up_grad():
        wu_grad[...] = dot_nn(n2_t[...], gu_all[...]).astype(BF16).reshape(wu_grad.shape)
        r_up.start()

    def mid_grads():
        total = f_dn.total(dn_own[...])
        inv = inv_own[:, 0:1]
        normal = mid_own[...] * inv
        scaled = total * gain
        mid_grad = cot[net.s].astype(F32) + inv * (scaled - normal * jnp.mean(scaled * normal, axis=-1, keepdims=True))
        grad_mid[...] = mid_grad
        kept.ffn_gain = jnp.sum(total * normal, axis=0, keepdims=True)
        branch[net.s] = mid_grad.astype(BF16)
        s_branch.start(branch.at[net.s])

    def norm_again():
        for b in range(NS):
            x = tok[b].astype(F32)
            scale = lax.rsqrt(jnp.mean(x * x, axis=-1, keepdims=True) + EPS)
            cot[b] = (x * scale * gains[0:1, :]).astype(BF16)
        grad_k[...] = jnp.zeros_like(grad_k)
        grad_v[...] = jnp.zeros_like(grad_v)
        factors[: 2 * WF, :] = jnp.zeros((2 * WF, length), BF16)

    def attend(b):
        return lambda: attend_back(b)

    def res_across():
        f_res.to_across(f_res.out[1].astype(F32))

    def res_total():
        result[...] = (mid_own[...] + f_res.total(result[...].astype(F32))).astype(BF16)
        kept.saved.append(net.local(result, r.result_end))

    def key_value_factors():
        for b in range(NS):
            here = slice(tokens * b, tokens * (b + 1))
            back_factors([grad_k[h, :, here] for h in range(LH)], RK, LH * RQ, RQ, True, here)
            back_factors([grad_v[h, :, here] for h in range(LH)], RK, LH * (RQ + RK), RQ + RK, False, here)
        rest = jnp.zeros((WF - NSH - NH, length), F32)
        factors[pl.ds(pl.multiple_of(net.core * WF + NSH, DH), WF - NSH), :] = jnp.concatenate(
            [head_grads[...], rest], axis=0
        ).astype(BF16)

    def out_grad():
        out_t = sum(
            dot_nn(att_t[:, :, tokens * b : tokens * (b + 1)].reshape(LH * DH, tokens).astype(BF16), branch[b]) for b in range(NS)
        )
        wo_grad[...] = out_t.T.astype(BF16).reshape(n, rows, LH * DH)
        r_o.start()

    def map_grads():
        slot_map = net.take(1)
        other = map_grad(1 - net.core)
        away = (n2_t.at[pl.ds(2 * WF, tokens)], mixed_t.at[pl.ds(WF, WF - tokens)])
        near = (mixed_t.at[pl.ds(0, tokens)], mixed_t.at[pl.ds(tokens, WF - tokens)])
        away[0][...] = other[:tokens].astype(BF16)
        away[1][...] = other[tokens:].astype(BF16)
        slot_more = net.take(1)
        net.send(away[0], near[0], slot_map, {SEQ: net.sib})
        net.send(away[1], near[1], slot_more, {SEQ: net.sib})
        mine = map_grad(net.core)
        attn_gain = (gain_part(net.core, mine) + gain_part(1 - net.core, other)) / gains[0:1, :]
        net.arrived(near[0], slot_map)
        net.arrived(near[1], slot_more)
        mine = mine + mixed_t[:WF].astype(F32)
        mine = jnp.concatenate([mine[: NSH + NH], attn_gain, kept.ffn_gain, mine[NSH + NH + 2 :]], axis=0)
        wf_grad[...] = mine.T.astype(BF16).reshape(n, rows, WF)
        r_f.start()

    def fold_grad(step):
        def act():
            if step == 0:
                net.settle(folded)
                f_gn.to_diag(normed_grad(net.diag))
            elif step == 1:
                f_gn.to_across(normed_grad(net.across))
            elif step == 2:
                f_gn.to_sibling(normed_grad(net.sib))
            else:
                kept.own_grad = normed_grad(net.s)

        return act

    def fold_total():
        total = f_gn.total(kept.own_grad)
        x = tok[net.s].astype(F32)
        scale = lax.rsqrt(jnp.mean(x * x, axis=-1, keepdims=True) + EPS)
        normal = x * scale
        scaled = total * gains[0:1, :]
        r.input_grad[...] = (
            grad_mid[...] + scale * (scaled - normal * jnp.mean(scaled * normal, axis=-1, keepdims=True))
        ).astype(BF16)
        kept.saved.append(net.local(r.input_grad, r.input_end))

    def on(reduce, *places):
        def act():
            for k in range(1, net.no):
                if min(k, 3) in places:
                    reduce.forward(k)

        return act

    shares = {}

    def share_out(reduce, out):
        def act():
            out[net.s] = reduce.finish().astype(BF16)
            shares[reduce] = Share(net, lambda rank: out.at[rank])
            shares[reduce].start(out.at[net.s])

        return act

    def pass_on(reduce):
        return lambda: shares[reduce].forward()

    steps = [
        gate_grad,
        mid_grads,
        up_grad,
        on(r_gate, 1),
        down_grad,
        res_across,
        norm_again,
        attend(net.s),
        s_branch.near,
        on(r_gate, 2),
        attend(net.sib),
        on(r_gate, 3),
        s_branch.forward,
        attend(net.across),
        s_branch.last,
        on(r_up, 1),
        attend(net.diag),
        on(r_up, 3),
        res_total,
        key_value_factors,
        out_grad,
        on(r_up, 2),
        fold_grad(0),
        fold_grad(1),
        map_grads,
        r_down.forward,
        fold_grad(2),
        share_out(r_gate, r.wg_out),
        share_out(r_up, r.wu_out),
        on(r_o, 1),
        fold_grad(3),
        on(r_o, 2),
        on(r_o, 3),
        on(r_f, 1),
        on(r_f, 2),
        on(r_f, 3),
        r_down.finish,
        fold_total,
        pass_on(r_up),
        share_out(r_o, r.wo_out),
        pass_on(r_gate),
        share_out(r_f, r.wf_out),
        r_down.forward_into,
        pass_on(r_o),
        pass_on(r_f),
    ]
    for step in steps:
        step()
    kept.saved.append(net.local(r.wd_out, r.wd_end))
    ends = ((r_gate, r.wg_out, r.wg_end), (r_up, r.wu_out, r.wu_end), (r_o, r.wo_out, r.wo_end), (r_f, r.wf_out, r.wf_end))
    for reduce, out, end in ends:
        shares[reduce].near()
        shares[reduce].last()
        kept.saved.append(net.local(out, end))
    for copy in kept.saved:
        copy.wait()
    net.settle(net.taken())


def sems(n):
    return [pltpu.SemaphoreType.DMA((10 * n + 80,))] * 2


def any_space(count):
    return [pl.BlockSpec(memory_space=pl.ANY)] * count


def vmem_space(count):
    return [pl.BlockSpec(memory_space=pltpu.VMEM)] * count


def run(n, given, small):
    r = types.SimpleNamespace(**given, **small)
    tokens, width = r.tok_in.shape
    length = tokens * NS
    rows = r.qs.shape[0]
    cols = r.gate.shape[1] // NS
    down = r.wd_in.shape
    hd = LH * DH
    ni = 2 if n <= 8 else 4
    no = n // ni
    wide = no // NS
    outs = dict(
        result=((tokens, width), BF16),
        input_grad=((tokens, width), BF16),
        wg_out=((NS, rows, cols), BF16),
        wu_out=((NS, rows, cols), BF16),
        wd_out=(down, BF16),
        wo_out=((NS, rows, hd), BF16),
        wf_out=((NS, rows, WF), BF16),
    )
    ends = dict(zip(dict(result_end=0, input_end=0, wg_end=0, wu_end=0, wd_end=0, wo_end=0, wf_end=0), outs.values()))
    scratch = dict(
        tok=((NS, tokens, width), BF16),
        cot=((NS, tokens, width), BF16),
        wo=((NS, n, rows, hd), BF16),
        wg=((n, rows, cols), BF16),
        wu=((n, rows, cols), BF16),
        wd=((n // NS,) + down, BF16),
        att=((NS, length, hd), BF16),
        wf=((2, n, rows, WF), BF16),
        wft=((2, WF, width), BF16),
        gains=((8, width), F32),
        shared=((2, NSH, length), BF16),
        heads=((NH, length), F32),
        qt=((LH, DH, length), BF16),
        kt=((LH, DH, length), BF16),
        vt=((LH, DH, length), BF16),
        kn=((LH, length, DH), BF16),
        vn=((LH, length, DH), BF16),
        lse=((LH, 1, length), F32),
        att_t=((LH, DH, length), F32),
        n2_t=((width, length), BF16),
        mixed_t=((cols, length), BF16),
        gg=((length, cols), BF16),
        gu=((length, cols), BF16),
        mid_own=((tokens, width), F32),
        inv_own=((tokens, 128), F32),
        grad_mid=((tokens, width), F32),
        branch=((NS, tokens, width), BF16),
        grad_q=((LH, DH, tokens), F32),
        delta=((LH, 1, tokens), F32),
        head_grads=((NH, length), F32),
        grad_k=((LH, DH, length), F32),
        grad_v=((LH, DH, length), F32),
        down_near=((ni - 1, wide) + down, BF16),
        down_far=((no - 1,) + down, BF16),
    )
    near, far = [
        [(lead + (rows, last), BF16) for last in (cols, hd, WF)] for lead in ((ni - 1, no), (no - 1,))
    ]
    three = ((3, tokens, width), BF16)
    scratch.update(
        gate_near=near[0],
        gate_far=far[0],
        up_near=near[0],
        up_far=far[0],
        o_near=near[1],
        o_far=far[1],
        f_near=near[2],
        f_far=far[2],
        dn_out=three,
        dn_in=three,
        res_out=three,
        res_in=three,
    )
    names = [*given, *small, *ends, *outs, *scratch, *dict(send_sems=0, recv_sems=0)]
    got = pl.pallas_call(
        functools.partial(kernel, n, names),
        out_shape=[jax.ShapeDtypeStruct(*shape) for shape in outs.values()],
        in_specs=any_space(len(given)) + vmem_space(len(small)),
        out_specs=any_space(len(outs)),
        scratch_shapes=[pltpu.VMEM(*shape) for shape in [*outs.values(), *scratch.values()]] + sems(n),
        compiler_params=pltpu.CompilerParams(collective_id=1, has_side_effects=True, vmem_limit_bytes=VMEM_LIMIT),
    )(*given.values(), *small.values())
    return dict(zip(outs, got, strict=True))


def tables(length):
    positions = np.arange(length, dtype=np.float32)
    frequency = (BASE ** (-2.0 * np.arange(DH // 2, dtype=np.float32) / DH)).astype(np.float32)
    angles = frequency[:, None] * positions[None, :]
    return np.cos(angles).astype(np.float32), np.sin(angles).astype(np.float32)


def finish_kernel(names, *refs):
    r = types.SimpleNamespace(**dict(zip(names, refs, strict=True)))
    r.result_out[...] = r.result[...]
    r.input_out[...] = r.input_grad[...]
    cols = r.wg_out.shape[2]
    for blocks, out in ((r.wg_out, r.wg_grad), (r.wu_out, r.wu_grad)):
        out[...] = jnp.concatenate([blocks[(NS - b) % NS].astype(F32) for b in range(NS)], axis=1)
    hd = LH * DH
    for rank in range(NS):
        r.wo_grad[:, hd * rank : hd * (rank + 1)] = r.wo_out[rank].astype(F32)
    r.wd_grad[...] = r.wd_out[...].astype(F32)
    f = [r.wf_out[rank].astype(F32) for rank in range(NS)]
    low = f[0] + f[2]
    high = f[1] + f[3]
    lane = lax.broadcasted_iota(jnp.int32, low.shape, 1)
    r.qs_grad[:, :256] = low[:, :256]
    moved = pltpu.roll(high, NSH, 1)
    r.qs_grad[:, 256:] = jnp.where(lane[:, 256:] < NSH, low[:, 256:], moved[:, 256:])
    shifted = pltpu.roll(high, WF - DH, 1)
    r.ks_grad[...] = shifted[:, :128]
    r.vs_grad[...] = shifted[:, 128:256]
    at = NSH
    for out, rank in ((r.qh_grad, RQ), (r.kh_grad, RK), (r.vh_grad, RK)):
        count = LH * rank
        place = lax.broadcasted_iota(jnp.int32, (NS * count, WF), 1) - at
        target = lax.broadcasted_iota(jnp.int32, (NS * count, WF), 0)
        total = 0.0
        for s in range(NS):
            pick = jnp.logical_and(target - s * count == place, jnp.logical_and(place >= 0, place < count))
            total = total + dot_nt(jnp.where(pick, 1.0, 0.0).astype(BF16), r.wf_out[s])
        out[...] = total
        at += count
    whole = low + high
    rows = whole.shape[0]
    eye = lax.broadcasted_iota(jnp.int32, (rows, rows), 0) == lax.broadcasted_iota(jnp.int32, (rows, rows), 1)
    for index in range(2):
        column = jnp.sum(jnp.where(lane == at + index, whole, 0.0), axis=1, keepdims=True)
        (r.attn_gain_grad, r.ffn_gain_grad)[index][...] = jnp.sum(jnp.where(eye, column, 0.0), axis=0)


def run_finish(got):
    one = types.SimpleNamespace(**got)
    rows, cols = one.wg_out.shape[1:]
    outs = dict(
        result_out=(one.result.shape, BF16),
        input_out=(one.result.shape, BF16),
        wg_grad=((rows, NS * cols), F32),
        wu_grad=((rows, NS * cols), F32),
        wd_grad=(one.wd_out.shape, F32),
        wo_grad=((rows, H * DH), F32),
        qh_grad=((H * RQ, rows), F32),
        qs_grad=((rows, RQ * DH), F32),
        kh_grad=((H * RK, rows), F32),
        ks_grad=((rows, RK * DH), F32),
        vh_grad=((H * RK, rows), F32),
        vs_grad=((rows, RK * DH), F32),
        attn_gain_grad=((rows,), F32),
        ffn_gain_grad=((rows,), F32),
    )
    names = [*got, *outs]
    done = pl.pallas_call(
        functools.partial(finish_kernel, names),
        out_shape=[jax.ShapeDtypeStruct(*shape) for shape in outs.values()],
        in_specs=vmem_space(len(got)),
        out_specs=vmem_space(len(outs)),
    )(*got.values())
    return types.SimpleNamespace(**dict(zip(outs, done, strict=True)))


def shards(tokens, attn_gain, qh, qs, kh, ks, vh, vs, out_proj, ffn_gain, gate, up, down, cotangent):
    n = lax.axis_size(FSDP)
    cosine, sine = tables(tokens.shape[1] * NS)
    given = dict(
        tok_in=tokens[0],
        wo_in=out_proj,
        gate=gate,
        up=up,
        wd_in=down,
        cot_in=cotangent[0],
    )
    small = dict(
        cosine=cosine,
        sine=sine,
        attn_gain=attn_gain,
        qh=qh.T,
        qs=qs,
        kh=kh.T,
        ks=ks,
        vh=vh.T,
        vs=vs,
        ffn_gain=ffn_gain,
    )
    done = run_finish(run(n, given, small))
    return (
        done.result_out[None],
        done.input_out[None],
        done.attn_gain_grad,
        done.qh_grad.T,
        done.qs_grad,
        done.kh_grad.T,
        done.ks_grad,
        done.vh_grad.T,
        done.vs_grad,
        done.wo_grad,
        done.ffn_gain_grad,
        done.wg_grad,
        done.wu_grad,
        done.wd_grad,
    )


def solution(mesh):
    tokens = P(FSDP, SEQ, None)
    matrix = P(FSDP, None)
    vector = P(FSDP)
    kinds = (vector,) + (matrix,) * 7 + (vector,) + (matrix,) * 3
    return jax.shard_map(
        shards,
        mesh=mesh,
        in_specs=(tokens,) + kinds + (tokens,),
        out_specs=(tokens, tokens) + kinds,
        check_vma=False,
    )
```
